32 devices in a mesh: tok: 4 (over y, x), ffn: 8 (over z, core).
Axes of the slice: x: 2, y: 2, z: 4, core: 2. Of those that a mesh axis runs over, the one named last changes fastest.
Arguments:
- targets: bfloat16 [8192, 1024], P(('tok', 'ffn')), may hold values from -6 to 6
- memory: bfloat16 [64, 2048, 1024], P('tok', 'ffn'), may hold values from -6 to 6
- out_grad: bfloat16 [8192, 1024], P(('tok', 'ffn')), may hold values from -6 to 6
- target_lengths: int32 [64], P(('tok', 'ffn')), may hold values from 32 to 128
- memory_lengths: int32 [64], P(('tok', 'ffn')), may hold values from 512 to 2048, as said below
- buckets: int32 [128, 128], replicated, may hold values from 0 to 31
- rel_table: bfloat16 [512], P(('tok', 'ffn')), may hold values from -5 to 5
- gain_self: bfloat16 [1024], P(('tok', 'ffn')), may hold values from 0.25 to 1.75
- gain_cross: bfloat16 [1024], P(('tok', 'ffn')), may hold values from 0.25 to 1.75
- gain_ffn: bfloat16 [1024], P(('tok', 'ffn')), may hold values from 0.25 to 1.75
- self_query: bfloat16 [1024, 1024], P(('tok', 'ffn')), may hold values from -0.1875 to 0.1875
- self_key: bfloat16 [1024, 512], P(('tok', 'ffn')), may hold values from -0.1875 to 0.1875
- self_value: bfloat16 [1024, 512], P(('tok', 'ffn')), may hold values from -0.1875 to 0.1875
- self_output: bfloat16 [1024, 1024], P(('tok', 'ffn')), may hold values from -0.75 to 0.75
- cross_query: bfloat16 [1024, 1024], P(('tok', 'ffn')), may hold values from -0.1875 to 0.1875
- cross_key: bfloat16 [1024, 512], P(('tok', 'ffn')), may hold values from -0.1875 to 0.1875
- cross_value: bfloat16 [1024, 512], P(('tok', 'ffn')), may hold values from -0.1875 to 0.1875
- cross_output: bfloat16 [1024, 1024], P(('tok', 'ffn')), may hold values from -2 to 2
- ffn_gate: bfloat16 [1024, 2816], P(None, 'ffn'), may hold values from -0.1875 to 0.1875
- ffn_up: bfloat16 [1024, 2816], P(None, 'ffn'), may hold values from -0.1875 to 0.1875
- ffn_down: bfloat16 [2816, 1024], P('ffn'), may hold values from -0.109375 to 0.109375
Outputs:
- layer_out: bfloat16 [8192, 1024], P(('tok', 'ffn'))
- targets_grad: bfloat16 [8192, 1024], P(('tok', 'ffn'))
- memory_grad: bfloat16 [64, 2048, 1024], P('tok', 'ffn')
- rms_values: float32 [64, 4], P(('tok', 'ffn'))
- rel_table_grad: float32 [512], P(('tok', 'ffn'))
- gain_self_grad: float32 [1024], P(('tok', 'ffn'))
- gain_cross_grad: float32 [1024], P(('tok', 'ffn'))
- gain_ffn_grad: float32 [1024], P(('tok', 'ffn'))
- self_query_grad: float32 [1024, 1024], P(('tok', 'ffn'))
- self_key_grad: float32 [1024, 512], P(('tok', 'ffn'))
- self_value_grad: float32 [1024, 512], P(('tok', 'ffn'))
- self_output_grad: float32 [1024, 1024], P(('tok', 'ffn'))
- cross_query_grad: float32 [1024, 1024], P(('tok', 'ffn'))
- cross_key_grad: float32 [1024, 512], P(('tok', 'ffn'))
- cross_value_grad: float32 [1024, 512], P(('tok', 'ffn'))
- cross_output_grad: float32 [1024, 1024], P(('tok', 'ffn'))
- ffn_gate_grad: float32 [1024, 2816], P(None, 'ffn')
- ffn_up_grad: float32 [1024, 2816], P(None, 'ffn')
- ffn_down_grad: float32 [2816, 1024], P('ffn')
The draws below stay inside these ranges and needn't reach their ends.
Inputs may be any that keep to these rules, and one draw needn't show every extreme that they name: `memory_lengths`: in every aligned run of 8 pairs one pair has all 2048 memory positions valid and another a quarter of them.
All inputs are finite; a program needn't handle non-finite values.
Results may differ from the reference program's by a relative error of at most 0.024.
Values may be sent and summed in bfloat16 or wider, within the bound.
No kernel may reach another device: no remote copies, remote signals or barrier semaphores. Data moves between devices by JAX's collectives and lax.ppermute only.
A program may use at most 320 MiB of HBM per device.

```python
import jax
import jax.numpy as jnp
from jax import lax

D = 1024
HEADS = 16
HEAD = 64
GROUPS = 8
FF = 2816
BUCKETS = 32
TGT = 128
MEM = 2048
PAIRS = 64
TOKENS = 8192


def draw_memory_lengths(key, part):
    key = jax.random.fold_in(key, 11)
    base_key, pick_key = jax.random.split(key, 2)
    lengths = jax.random.randint(base_key, (PAIRS,), MEM // 4, MEM + 1)
    chosen = jax.random.randint(pick_key, (), 0, 8)
    slot = jnp.arange(PAIRS) % 8
    lengths = jnp.where(slot == chosen, MEM, lengths)
    lengths = jnp.where(slot == (chosen + 4) % 8, MEM // 4, lengths)
    return lengths.astype(jnp.int32)


def with_ends(entries, stream_key, low, largest):
    spot = [jax.random.randint(jax.random.fold_in(stream_key, axis), (), 0, length) for axis, length in enumerate(entries.shape)]
    main_axis = entries.shape.index(max(entries.shape))
    neighbour = spot[:main_axis] + [(spot[main_axis] + 1) % entries.shape[main_axis]] + spot[main_axis + 1:]
    return entries.at[tuple(spot)].set(low).at[tuple(neighbour)].set(largest)


def block_levels(rng, dims, cuts, smallest, top_value):
    def one(axis_at, shards_of):
        steps = jax.random.uniform(jax.random.fold_in(jax.random.fold_in(rng, 6), axis_at), (shards_of,), jnp.float32, smallest / len(cuts), top_value / len(cuts))
        return jnp.repeat(jnp.exp(steps), dims[axis_at] // shards_of).reshape((-1,) + (1,) * (len(dims) - axis_at - 1))

    factor_of = one(*cuts[0])
    for cut in cuts[1:]:
        factor_of = factor_of * one(*cut)
    return factor_of


def gaussian(stream_key, dims, deviation, reach, cuts=(), held_as=jnp.bfloat16):
    loudness = block_levels(stream_key, dims, cuts, -0.22, 0.18) if cuts else 1.0
    array = jax.random.normal(stream_key, dims, jnp.float32) * deviation * loudness
    return jnp.minimum(jnp.maximum(array, -reach), reach).astype(held_as)


def setup_inputs(seed: int = 0) -> dict:
    seeds = jax.random.split(jax.random.key(seed), 22)
    return {
        "targets": gaussian(seeds[0], (TOKENS, D), 1.0, 6.0, ((0, 32),)),
        "memory": gaussian(seeds[1], (PAIRS, MEM, D), 1.0, 6.0, ((0, 4), (1, 8))),
        "out_grad": gaussian(seeds[2], (TOKENS, D), 1.0, 6.0, ((0, 32),)),
        "target_lengths": with_ends(jax.random.randint(seeds[3], (PAIRS,), TGT // 4, TGT + 1), jax.random.fold_in(seeds[3], 1), TGT // 4, TGT).astype(jnp.int32),
        "memory_lengths": draw_memory_lengths(jax.random.fold_in(seeds[21], 71), 0),
        "buckets": with_ends(jax.random.randint(seeds[5], (TGT, TGT), 0, BUCKETS), jax.random.fold_in(seeds[5], 1), 0, BUCKETS - 1).astype(jnp.int32),
        "rel_table": gaussian(seeds[6], (HEADS * BUCKETS,), 1.0, 5.0, ((0, 32),)),
        "gain_self": jnp.clip(1.0 + 0.15 * jax.random.normal(seeds[7], (D,), jnp.float32), 0.25, 1.75).astype(jnp.bfloat16),
        "gain_cross": jnp.clip(1.0 + 0.15 * jax.random.normal(seeds[8], (D,), jnp.float32), 0.25, 1.75).astype(jnp.bfloat16),
        "gain_ffn": jnp.clip(1.0 + 0.15 * jax.random.normal(seeds[9], (D,), jnp.float32), 0.25, 1.75).astype(jnp.bfloat16),
        "self_query": gaussian(seeds[10], (D, D), D ** -0.5, 0.1875, ((0, 32),)),
        "self_key": gaussian(seeds[11], (D, GROUPS * HEAD), D ** -0.5, 0.1875, ((0, 32),)),
        "self_value": gaussian(seeds[12], (D, GROUPS * HEAD), D ** -0.5, 0.1875, ((0, 32),)),
        "self_output": gaussian(seeds[13], (D, D), (D // 16) ** -0.5, 0.75, ((0, 32),)),
        "cross_query": gaussian(seeds[14], (D, D), D ** -0.5, 0.1875, ((0, 32),)),
        "cross_key": gaussian(seeds[15], (D, GROUPS * HEAD), D ** -0.5, 0.1875, ((0, 32),)),
        "cross_value": gaussian(seeds[16], (D, GROUPS * HEAD), D ** -0.5, 0.1875, ((0, 32),)),
        "cross_output": gaussian(seeds[17], (D, D), (max(D // 128, 1)) ** -0.5, 2.0, ((0, 32),)),
        "ffn_gate": gaussian(seeds[18], (D, FF), D ** -0.5, 0.1875, ((1, 8),)),
        "ffn_up": gaussian(seeds[19], (D, FF), D ** -0.5, 0.1875, ((1, 8),)),
        "ffn_down": gaussian(seeds[20], (FF, D), FF ** -0.5, 0.109375, ((0, 8),)),
    }


@jax.custom_vjp
def low(v):
    return lax.optimization_barrier(v.astype(jnp.bfloat16)).astype(jnp.float32)

@jax.custom_vjp
def low_back(v):
    return v

def low_keep(v):
    return (low(v), None)

def low_pass(kept, grad):
    return (grad,)

def back_keep(v):
    return (v, None)

def back_low(kept, grad):
    return (low(grad),)
low.defvjp(low_keep, low_pass)
low_back.defvjp(back_keep, back_low)
norm_epsilon = 1e-06
masked_value = -1e+30

def matmul(left, right):
    return jnp.dot(left, right, precision=lax.Precision.HIGHEST)

def rounded(value):
    return low(low_back(value))

def rms_norm(hidden, gain):
    scale = lax.rsqrt(lax.optimization_barrier(jnp.mean(hidden * hidden, axis=-1, keepdims=True)) + norm_epsilon)
    return low(hidden * scale * gain)

def attend(queries, keys, values, bias, mask):
    group_width = HEADS // GROUPS
    query_heads = queries.reshape(queries.shape[0], GROUPS, group_width, HEAD)
    key_heads = keys.reshape(keys.shape[0], GROUPS, HEAD)
    value_heads = values.reshape(values.shape[0], GROUPS, HEAD)
    scores = HEAD ** (-0.5) * jnp.einsum('qgrd,kgd->grqk', query_heads, key_heads, precision=lax.Precision.HIGHEST) + bias
    scores = low_back(scores)
    scores = jnp.where(mask, scores, masked_value)
    highest = lax.optimization_barrier(jnp.max(scores, axis=-1, keepdims=True))
    weights = jnp.exp(scores - highest)
    probs = low(weights / lax.optimization_barrier(jnp.sum(weights, axis=-1, keepdims=True)))
    mixed = jnp.einsum('grqk,kgd->qgrd', probs, value_heads, precision=lax.Precision.HIGHEST)
    return rounded(mixed.reshape(queries.shape[0], HEADS * HEAD))

def pair_layer(params, inputs, memory_rows, target_length, memory_length, buckets):
    rel_table, gain_self, gain_cross, gain_ffn, self_query, self_key, self_value, self_output, cross_query, cross_key, cross_value, cross_output, ffn_gate, ffn_up, ffn_down = params
    position = jnp.arange(TGT)
    self_mask = (position[None, :] <= position[:, None]) & (position[None, :] < target_length)
    bias = rel_table.reshape(HEADS, BUCKETS)[:, buckets].reshape(GROUPS, HEADS // GROUPS, TGT, TGT)
    normed_one = rms_norm(inputs, gain_self)
    self_mix = attend(rounded(matmul(normed_one, self_query)), rounded(matmul(normed_one, self_key)), rounded(matmul(normed_one, self_value)), bias, self_mask)
    self_branch = low_back(matmul(self_mix, self_output))
    hidden_one = inputs + self_branch
    normed_two = rms_norm(hidden_one, gain_cross)
    cross_mask = (jnp.arange(MEM) < memory_length)[None, :]
    cross_mix = attend(rounded(matmul(normed_two, cross_query)), rounded(matmul(memory_rows, cross_key)), rounded(matmul(memory_rows, cross_value)), 0.0, cross_mask)
    cross_branch = low_back(matmul(cross_mix, cross_output))
    hidden_two = hidden_one + cross_branch
    normed_three = rms_norm(hidden_two, gain_ffn)
    gate_value = low_back(matmul(normed_three, ffn_gate))
    up_value = low_back(matmul(normed_three, ffn_up))
    hidden = low(jax.nn.gelu(gate_value, approximate=True) * up_value)
    ffn_branch = low_back(matmul(hidden, ffn_down))
    hidden_three = hidden_two + ffn_branch
    valid = (position < target_length)[:, None]
    counted = target_length.astype(jnp.float32) * D
    stats = jnp.stack([jnp.sqrt(jnp.sum(jnp.where(valid, field * field, 0.0)) / counted) for field in (hidden_three, self_branch, cross_branch, ffn_branch)])
    return (hidden_three, stats)

def reference(targets, memory, out_grad, target_lengths, memory_lengths, buckets, rel_table, gain_self, gain_cross, gain_ffn, self_query, self_key, self_value, self_output, cross_query, cross_key, cross_value, cross_output, ffn_gate, ffn_up, ffn_down):
    params = tuple((weight.astype(jnp.float32) for weight in (rel_table, gain_self, gain_cross, gain_ffn, self_query, self_key, self_value, self_output, cross_query, cross_key, cross_value, cross_output, ffn_gate, ffn_up, ffn_down)))
    rows_in = targets.astype(jnp.float32).reshape(PAIRS, TGT, D)
    rows_grad = out_grad.astype(jnp.float32).reshape(PAIRS, TGT, D)

    def one_pair(totals, item):
        rows, memory_rows, cotangent, target_length, memory_length = item

        def layer_of(param_values, row_values, memory_values):
            return pair_layer(param_values, row_values, memory_values, target_length, memory_length, buckets)
        result, pullback, stats = jax.vjp(layer_of, params, rows, memory_rows.astype(jnp.float32), has_aux=True)
        param_grads, rows_back, memory_back = pullback(cotangent)
        totals = jax.tree.map(jnp.add, totals, param_grads)
        return (totals, (result.astype(jnp.bfloat16), rows_back.astype(jnp.bfloat16), memory_back.astype(jnp.bfloat16), stats))
    zeros = tuple((jnp.zeros_like(weight) for weight in params))
    totals, (results, rows_back, memory_back, stats) = lax.scan(one_pair, zeros, (rows_in, memory, rows_grad, target_lengths, memory_lengths))
    return (results.reshape(TOKENS, D), rows_back.reshape(TOKENS, D), memory_back, stats, totals[0], totals[1], totals[2], totals[3], totals[4], totals[5], totals[6], totals[7], totals[8], totals[9], totals[10], totals[11], totals[12], totals[13], totals[14])
```

```python
import functools

import jax
import jax.numpy as jnp
from jax import lax
from jax.experimental import pallas as pl
from jax.experimental.pallas import tpu as pltpu
from jax.sharding import PartitionSpec as P

D = 1024
HEADS = 16
HEAD = 64
GROUPS = 8
BUCKETS = 32
TGT = 128
KEYS = GROUPS * HEAD
SMALL = 128

norm_epsilon = 1e-06
masked_value = -1e30
bf16 = jnp.bfloat16
f32 = jnp.float32


def matmul(left, right):
    return jnp.dot(left, right, preferred_element_type=jnp.float32)


def contract(left, right, left_dim, right_dim):
    return lax.dot_general(
        left, right, (((left_dim,), (right_dim,)), ((), ())), preferred_element_type=jnp.float32
    )


def norm_rows(hidden, gain):
    scale = lax.rsqrt(jnp.mean(hidden * hidden, axis=-1, keepdims=True) + norm_epsilon)
    return hidden * scale * gain


def norm_back(hidden, gain, cotangent):
    unused, pullback = jax.vjp(norm_rows, hidden, gain)
    return pullback(cotangent)


def gated(gate_value, up_value):
    return jax.nn.gelu(gate_value, approximate=True) * up_value


def gated_back(gate_value, up_value, cotangent):
    unused, pullback = jax.vjp(gated, gate_value, up_value)
    gate_grad, up_grad = pullback(cotangent)
    return (gate_grad.astype(jnp.bfloat16), up_grad.astype(jnp.bfloat16))


def attention_scores(queries, keys, bias, mask):
    raw = jnp.einsum("pqgre,pkge->pgrqk", queries, keys, preferred_element_type=jnp.float32)
    return jnp.where(mask, raw * HEAD ** (-0.5) + bias, masked_value)


def attention_forward(queries, keys, values, bias, mask):
    scores = attention_scores(queries, keys, bias, mask)
    highest = jnp.max(scores, axis=-1, keepdims=True)
    weights = jnp.exp(scores - highest)
    totals = jnp.sum(weights, axis=-1, keepdims=True)
    probs = (weights / totals).astype(jnp.bfloat16)
    mixed = jnp.einsum("pgrqk,pkge->pqgre", probs, values, preferred_element_type=jnp.float32)
    return (mixed.astype(jnp.bfloat16), highest + jnp.log(totals))


def attention_backward(queries, keys, values, bias, mask, log_totals, mixed_grad):
    scores = attention_scores(queries, keys, bias, mask)
    probs = jnp.exp(scores - log_totals)
    prob_grad = jnp.einsum(
        "pqgre,pkge->pgrqk", mixed_grad, values, preferred_element_type=jnp.float32
    )
    values_grad = jnp.einsum(
        "pgrqk,pqgre->pkge",
        probs.astype(jnp.bfloat16),
        mixed_grad,
        preferred_element_type=jnp.float32,
    )
    inner = jnp.sum(probs * prob_grad, axis=-1, keepdims=True)
    score_grad = (probs * (prob_grad - inner)).astype(jnp.bfloat16)
    queries_grad = jnp.einsum(
        "pgrqk,pkge->pqgre", score_grad, keys, preferred_element_type=jnp.float32
    ) * HEAD ** (-0.5)
    keys_grad = jnp.einsum(
        "pgrqk,pqgre->pkge", score_grad, queries, preferred_element_type=jnp.float32
    ) * HEAD ** (-0.5)
    return (queries_grad, keys_grad, values_grad, score_grad)


def split_terms(value):
    high = value.astype(bf16)
    rest = value - high.astype(f32)
    middle = rest.astype(bf16)
    low = (rest - middle.astype(f32)).astype(bf16)
    return [high, middle, low]


def join_terms(block):
    return (
        block[:HEADS].astype(f32)
        + block[HEADS : 2 * HEADS].astype(f32)
        + block[2 * HEADS : 3 * HEADS].astype(f32)
    )


def both_heads(ref, group):
    start = group * 2 * HEAD
    return jnp.concatenate(
        [ref[start : start + HEAD, :], ref[start + HEAD : start + 2 * HEAD, :]], axis=1
    )


def both_rows(stat, group):
    return jnp.concatenate([stat[2 * group : 2 * group + 1], stat[2 * group + 1 : 2 * group + 2]], axis=1)


def cross_forward_kernel(chunk, info_ref, query_ref, memory_ref, mix_ref, stat_ref):
    pair = pl.program_id(0)
    left = info_ref[chunk, 2 + pair] - info_ref[chunk, 1]
    mask = lax.broadcasted_iota(jnp.int32, (memory_ref.shape[1], 2 * TGT), 0) < left
    for group in range(GROUPS):
        keys = memory_ref[0, :, group * HEAD : (group + 1) * HEAD]
        values = memory_ref[0, :, KEYS + group * HEAD : KEYS + (group + 1) * HEAD]
        scores = jnp.where(mask, matmul(keys, both_heads(query_ref, group)), masked_value)
        highest = jnp.max(scores, axis=0, keepdims=True)
        weights = jnp.exp(scores - highest)
        totals = jnp.sum(weights, axis=0, keepdims=True)
        mixed = contract(weights.astype(bf16), values, 0, 0).T * (1.0 / totals)
        mixed = mixed.astype(bf16)
        start = group * 2 * HEAD
        mix_ref[start : start + HEAD, :] = mixed[:, :TGT]
        mix_ref[start + HEAD : start + 2 * HEAD, :] = mixed[:, TGT:]
        logsum = highest + jnp.log(totals)
        stat_ref[2 * group : 2 * group + 1, :] = logsum[:, :TGT]
        stat_ref[2 * group + 1 : 2 * group + 2, :] = logsum[:, TGT:]
    for place, term in enumerate(split_terms(stat_ref[...])):
        mix_ref[D + place * HEADS : D + (place + 1) * HEADS, :] = term


def cross_forward(chunk, info, queries, memory_parts):
    held, wide = memory_parts.shape[1], memory_parts.shape[2]
    rows = queries.shape[1]
    return pl.pallas_call(
        functools.partial(cross_forward_kernel, chunk),
        grid_spec=pltpu.PrefetchScalarGridSpec(
            num_scalar_prefetch=1,
            grid=(rows // TGT,),
            in_specs=[
                pl.BlockSpec((D, TGT), lambda pair, info: (0, pair)),
                pl.BlockSpec((1, held, wide), lambda pair, info: (info[chunk, 0] + pair, 0, 0)),
            ],
            out_specs=pl.BlockSpec((D + 3 * HEADS, TGT), lambda pair, info: (0, pair)),
            scratch_shapes=[pltpu.VMEM((HEADS, TGT), f32)],
        ),
        out_shape=jax.ShapeDtypeStruct((D + 3 * HEADS, rows), bf16),
        compiler_params=pltpu.CompilerParams(vmem_limit_bytes=32 * 1024 * 1024),
        cost_estimate=pl.CostEstimate(flops=4000000000, bytes_accessed=3000000, transcendentals=0),
        name="cross_forward",
    )(info, queries, memory_parts)


def cross_backward_kernel(
    chunk, info_ref, query_ref, grad_ref, memory_ref, unused_ref, query_grad_ref, memory_grad_ref
):
    pair = pl.program_id(0)
    left = info_ref[chunk, 2 + pair] - info_ref[chunk, 1]
    mask = lax.broadcasted_iota(jnp.int32, (memory_ref.shape[1], 2 * TGT), 0) < left
    logsum = join_terms(grad_ref[D : D + 3 * HEADS, :])
    inner = join_terms(grad_ref[D + 3 * HEADS : D + 6 * HEADS, :])
    for tile in range(GROUPS // 2):
        key_parts, value_parts = [], []
        for group in (2 * tile, 2 * tile + 1):
            keys = memory_ref[0, :, group * HEAD : (group + 1) * HEAD]
            values = memory_ref[0, :, KEYS + group * HEAD : KEYS + (group + 1) * HEAD]
            queries = both_heads(query_ref, group)
            mixed_grad = both_heads(grad_ref, group)
            scores = matmul(keys, queries) - both_rows(logsum, group)
            probs = jnp.exp(jnp.where(mask, scores, masked_value))
            prob_grad = matmul(values, mixed_grad) - both_rows(inner, group)
            score_grad = (probs * prob_grad).astype(bf16)
            value_parts.append(contract(probs.astype(bf16), mixed_grad, 1, 1).astype(bf16))
            key_parts.append(contract(score_grad, queries, 1, 1).astype(bf16))
            query_grad = (contract(keys, score_grad, 0, 0) * HEAD ** (-0.5)).astype(bf16)
            start = group * 2 * HEAD
            query_grad_ref[start : start + HEAD, :] = query_grad[:, :TGT]
            query_grad_ref[start + HEAD : start + 2 * HEAD, :] = query_grad[:, TGT:]
        columns = 2 * HEAD * tile
        memory_grad_ref[0, :, columns : columns + 2 * HEAD] = jnp.concatenate(key_parts, axis=1)
        memory_grad_ref[0, :, KEYS + columns : KEYS + columns + 2 * HEAD] = jnp.concatenate(
            value_parts, axis=1
        )


def cross_backward(chunk, info, queries, grads, memory_parts, memory_grads):
    held, wide = memory_parts.shape[1], memory_parts.shape[2]
    rows = queries.shape[1]
    place = pl.BlockSpec((1, held, wide), lambda pair, info: (info[chunk, 0] + pair, 0, 0))
    return pl.pallas_call(
        functools.partial(cross_backward_kernel, chunk),
        grid_spec=pltpu.PrefetchScalarGridSpec(
            num_scalar_prefetch=1,
            grid=(rows // TGT,),
            in_specs=[
                pl.BlockSpec((D, TGT), lambda pair, info: (0, pair)),
                pl.BlockSpec((D + 6 * HEADS, TGT), lambda pair, info: (0, pair)),
                place,
                pl.BlockSpec(memory_space=pl.ANY),
            ],
            out_specs=[pl.BlockSpec((D, TGT), lambda pair, info: (0, pair)), place],
        ),
        out_shape=[
            jax.ShapeDtypeStruct((D, rows), bf16),
            jax.ShapeDtypeStruct(memory_parts.shape, bf16),
        ],
        input_output_aliases={4: 1},
        compiler_params=pltpu.CompilerParams(vmem_limit_bytes=32 * 1024 * 1024),
        cost_estimate=pl.CostEstimate(flops=6000000000, bytes_accessed=5000000, transcendentals=0),
        name="cross_backward",
    )(info, queries, grads, memory_parts, memory_grads)


def exchange(value, axis, size, mask):
    return lax.ppermute(value, axis, [(place, place ^ mask) for place in range(size)])


def gather_chunks(value, size):
    chunks = [value, exchange(value, "ffn", size, 1)]
    far = [exchange(value, "ffn", size, 2 * step) for step in range(1, size // 2)]
    for one in far:
        chunks += [one, exchange(one, "ffn", size, 1)]
    return chunks


def scatter_chunks(parts, size, join):
    joined = []
    for step in range(size // 2):
        other = exchange(parts[2 * step + 1], "ffn", size, 1)
        joined.append(join([parts[2 * step], other], step == -1))
    arrived = [joined[0]] + [
        exchange(joined[step], "ffn", size, 2 * step) for step in range(1, size // 2)
    ]
    return join(arrived, True)


def join_sums(parts, last):
    total = parts[0].astype(f32)
    for part in parts[1:]:
        total = total + part.astype(f32)
    return total if last else total.astype(bf16)


def join_mixes(parts, last):
    logs = [join_terms(part[D:]) for part in parts]
    highest = functools.reduce(jnp.maximum, logs)
    weights = [jnp.exp(log - highest) for log in logs]
    totals = functools.reduce(jnp.add, weights)
    rows = parts[0].shape[1]
    mixed = functools.reduce(
        jnp.add,
        [
            part[:D].astype(f32).reshape(HEADS, HEAD, rows) * (weight / totals)[:, None, :]
            for part, weight in zip(parts, weights, strict=True)
        ],
    ).reshape(D, rows)
    logsum = highest + jnp.log(totals)
    if last:
        return mixed, logsum
    return jnp.concatenate([mixed.astype(bf16)] + split_terms(logsum), axis=0)


def reduce_blocks(grads, tok_size, ffn_size):
    columns = grads.shape[1]
    me_ffn, me_tok = lax.axis_index("ffn"), lax.axis_index("tok")

    def halves(value, dim, bit):
        first = lax.index_in_dim(value, 0, dim, keepdims=False)
        second = lax.index_in_dim(value, 1, dim, keepdims=False)
        return jnp.where(bit == 0, first, second), jnp.where(bit == 0, second, first)

    rows = grads.shape[0] // (tok_size * ffn_size)
    value = grads.reshape(tok_size, ffn_size // 2, 2, rows, columns)
    kept, sent = halves(value, 2, me_ffn & 1)
    value = kept.astype(f32) + exchange(sent.astype(bf16), "ffn", ffn_size, 1).astype(f32)

    bits = tok_size.bit_length() - 1
    value = value.reshape((2,) * bits + (ffn_size // 2, rows, columns))
    half = columns // 2 // 128 * 128
    sides = []
    for part, order in (
        (value[..., :half], list(range(bits))),
        (value[..., half:], list(range(bits))[::-1]),
    ):
        left = list(range(bits))
        for bit in order:
            dim = left.index(bit)
            left.remove(bit)
            weight = 1 << (bits - 1 - bit)
            kept, sent = halves(part, dim, (me_tok // weight) & 1)
            part = kept.astype(f32) + exchange(sent.astype(bf16), "tok", tok_size, weight).astype(f32)
        sides.append(part)
    value = jnp.concatenate(sides, axis=-1)
    line = me_ffn // 2
    total = lax.dynamic_index_in_dim(value, line, 0, keepdims=False)
    low = value.astype(bf16)
    for step in range(1, ffn_size // 2):
        part = lax.dynamic_index_in_dim(low, line ^ step, 0, keepdims=False)
        total = total + exchange(part, "ffn", ffn_size, 2 * step).astype(f32)
    return total


def on_device(
    tok_size,
    ffn_size,
    targets,
    memory,
    out_grad,
    target_lengths,
    memory_lengths,
    buckets,
    rel_table,
    gain_self,
    gain_cross,
    gain_ffn,
    self_query,
    self_key,
    self_value,
    self_output,
    cross_query,
    cross_key,
    cross_value,
    cross_output,
    ffn_gate,
    ffn_up,
    ffn_down,
):
    pair_count = target_lengths.shape[0]
    row_count = targets.shape[0]
    group_width = HEADS // GROUPS
    held = memory.shape[1]
    devices = tok_size * ffn_size
    me_tok, me_ffn = lax.axis_index("tok"), lax.axis_index("ffn")
    share = self_query.shape[0]
    table_share, gain_share = rel_table.shape[0], gain_self.shape[0]

    small = jnp.concatenate(
        [
            rel_table,
            gain_self,
            gain_cross,
            gain_ffn,
            (memory_lengths // 64).astype(bf16),
            (memory_lengths % 64).astype(bf16),
        ]
    )
    small = jnp.pad(small[None, :], ((0, share - 1), (0, SMALL - small.shape[0])))
    self_pack = jnp.concatenate([self_query, self_key, self_value, self_output, small], axis=1)
    cross_pack = jnp.concatenate([cross_query, cross_key, cross_value, cross_output], axis=1)
    full_self = lax.all_gather(self_pack, ("tok", "ffn"), axis=0, tiled=True)
    full_cross = lax.all_gather(cross_pack, ("tok", "ffn"), axis=0, tiled=True)
    full_self_query = full_self[:, :D]
    full_self_key = full_self[:, D : D + KEYS]
    full_self_value = full_self[:, D + KEYS : D + 2 * KEYS]
    full_self_output = full_self[:, D + 2 * KEYS : 2 * D + 2 * KEYS]
    full_small = full_self[:, 2 * D + 2 * KEYS :].reshape(devices, share, SMALL)[:, 0]
    full_cross_query = full_cross[:, :D]
    full_memory_weight = full_cross[:, D : D + 2 * KEYS]
    full_cross_output = full_cross[:, D + 2 * KEYS :]
    full_table = full_small[:, :table_share].reshape(-1)
    at = table_share
    full_gains = []
    for unused in range(3):
        full_gains.append(full_small[:, at : at + gain_share].reshape(-1).astype(f32))
        at += gain_share
    full_gain_self, full_gain_cross, full_gain_ffn = full_gains
    lengths = full_small[:, at : at + 2 * pair_count].astype(jnp.int32)
    lengths = lengths[:, :pair_count] * 64 + lengths[:, pair_count:]
    lengths = lax.dynamic_index_in_dim(
        lengths.reshape(tok_size, ffn_size, pair_count), me_tok, 0, keepdims=False
    )
    owner = me_ffn ^ jnp.arange(ffn_size)
    info = jnp.concatenate(
        [
            (owner * pair_count)[:, None],
            jnp.broadcast_to(me_ffn * held, (ffn_size, 1)),
            jnp.take(lengths, owner, axis=0),
        ],
        axis=1,
    ).astype(jnp.int32)

    all_cotangent = jnp.concatenate(gather_chunks(out_grad, ffn_size), axis=0)
    memory_flat = memory.reshape(-1, D)

    onehot = (buckets[:, :, None] == jnp.arange(BUCKETS)[None, None, :]).astype(jnp.bfloat16)
    position = jnp.arange(TGT)
    self_bias = jnp.einsum(
        "qkb,hb->hqk",
        onehot,
        full_table.reshape(HEADS, BUCKETS),
        preferred_element_type=jnp.float32,
    ).reshape(1, GROUPS, group_width, TGT, TGT)
    causal = position[None, :] <= position[:, None]
    self_mask = causal[None, None, None] & (
        position[None, None, None, None, :] < target_lengths[:, None, None, None, None]
    )
    inputs = targets.astype(jnp.float32)
    normed_one = norm_rows(inputs, full_gain_self).astype(jnp.bfloat16)
    self_queries = (
        matmul(normed_one, full_self_query)
        .astype(jnp.bfloat16)
        .reshape(pair_count, TGT, GROUPS, group_width, HEAD)
    )
    self_keys = (
        matmul(normed_one, full_self_key)
        .astype(jnp.bfloat16)
        .reshape(pair_count, TGT, GROUPS, HEAD)
    )
    self_values = (
        matmul(normed_one, full_self_value)
        .astype(jnp.bfloat16)
        .reshape(pair_count, TGT, GROUPS, HEAD)
    )
    self_mixed, self_totals = attention_forward(
        self_queries, self_keys, self_values, self_bias, self_mask
    )
    self_flat = self_mixed.reshape(row_count, D)
    self_branch = matmul(self_flat, full_self_output)
    hidden_one = inputs + self_branch
    normed_two = norm_rows(hidden_one, full_gain_cross).astype(jnp.bfloat16)

    cross_queries = (contract(full_cross_query, normed_two, 0, 1).astype(bf16)) * bf16(HEAD ** (-0.5))
    memory_parts = matmul(memory_flat, full_memory_weight).astype(bf16).reshape(-1, held, 2 * KEYS)
    query_chunks = gather_chunks(cross_queries, ffn_size)
    mixed_parts = [
        cross_forward(chunk, info, query_chunks[chunk], memory_parts) for chunk in range(ffn_size)
    ]
    cross_mixed, cross_totals = scatter_chunks(mixed_parts, ffn_size, join_mixes)
    cross_flat = cross_mixed.astype(bf16)
    cross_branch = contract(cross_flat, full_cross_output, 0, 0)
    hidden_two = hidden_one + cross_branch
    normed_three = norm_rows(hidden_two, full_gain_ffn).astype(jnp.bfloat16)

    all_rows = jnp.concatenate(gather_chunks(normed_three, ffn_size), axis=0)
    gate_value = matmul(all_rows, ffn_gate)
    up_value = matmul(all_rows, ffn_up)
    hidden = gated(gate_value, up_value).astype(jnp.bfloat16)
    hidden_grad = matmul(all_cotangent, ffn_down.T)
    gate_grad, up_grad = gated_back(gate_value, up_value, hidden_grad)
    rows_grad = (matmul(gate_grad, ffn_gate.T) + matmul(up_grad, ffn_up.T)).astype(bf16)
    normed_three_grad = scatter_chunks(jnp.split(rows_grad, ffn_size), ffn_size, join_sums)
    branch_part = matmul(hidden, ffn_down).astype(bf16)
    ffn_branch = scatter_chunks(jnp.split(branch_part, ffn_size), ffn_size, join_sums)
    down_part = matmul(hidden.T, all_cotangent)
    gate_part = matmul(all_rows.T, gate_grad)
    up_part = matmul(all_rows.T, up_grad)
    gate_weight_grad, up_weight_grad, down_weight_grad = (
        lax.psum(gate_part.astype(jnp.bfloat16), "tok").astype(jnp.float32),
        lax.psum(up_part.astype(jnp.bfloat16), "tok").astype(jnp.float32),
        lax.psum(down_part.astype(jnp.bfloat16), "tok").astype(jnp.float32),
    )
    hidden_three = hidden_two + ffn_branch
    layer_out = hidden_three.astype(jnp.bfloat16)
    valid = (position[None, :] < target_lengths[:, None])[:, :, None]
    counted = target_lengths.astype(jnp.float32) * D

    def root_mean(field):
        squares = field.reshape(pair_count, TGT, D)
        squares = jnp.where(valid, squares * squares, 0.0)
        return jnp.sqrt(jnp.sum(squares, axis=(1, 2)) / counted)

    rms_values = jnp.stack(
        [
            root_mean(hidden_three),
            root_mean(self_branch),
            root_mean(cross_branch),
            root_mean(ffn_branch),
        ],
        axis=1,
    )

    cotangent = out_grad.astype(jnp.float32)
    norm_three_back, gain_ffn_grad = norm_back(hidden_two, full_gain_ffn, normed_three_grad)
    hidden_two_grad = cotangent + norm_three_back
    cross_branch_low = hidden_two_grad.astype(jnp.bfloat16)
    cross_output_grad = matmul(cross_flat, cross_branch_low)
    cross_mixed_grad = contract(full_cross_output, cross_branch_low, 1, 1).astype(bf16)
    inner = jnp.sum(
        (cross_mixed_grad.astype(f32) * cross_mixed).reshape(HEADS, HEAD, row_count), axis=1
    )
    grad_pack = jnp.concatenate(
        [cross_mixed_grad] + split_terms(cross_totals) + split_terms(inner), axis=0
    )
    grad_chunks = gather_chunks(grad_pack, ffn_size)
    memory_grads = jnp.zeros(memory_parts.shape, bf16)
    query_parts = []
    for chunk in range(ffn_size):
        part, memory_grads = cross_backward(
            chunk, info, query_chunks[chunk], grad_chunks[chunk], memory_parts, memory_grads
        )
        query_parts.append(part)
    cross_queries_low = scatter_chunks(query_parts, ffn_size, join_sums).astype(bf16)
    cross_query_grad = contract(normed_two, cross_queries_low, 0, 1)
    normed_two_grad = contract(cross_queries_low, full_cross_query, 0, 1)
    memory_grads = memory_grads.reshape(-1, 2 * KEYS)
    memory_weight_grad = matmul(memory_flat.T, memory_grads)
    memory_grad = (
        contract(memory_grads, full_memory_weight, 1, 1).astype(jnp.bfloat16).reshape(memory.shape)
    )
    norm_two_back, gain_cross_grad = norm_back(hidden_one, full_gain_cross, normed_two_grad)
    hidden_one_grad = hidden_two_grad + norm_two_back
    self_branch_low = hidden_one_grad.astype(jnp.bfloat16)
    self_output_grad = matmul(self_flat.T, self_branch_low)
    self_mixed_grad = (
        matmul(self_branch_low, full_self_output.T)
        .astype(jnp.bfloat16)
        .reshape(pair_count, TGT, GROUPS, group_width, HEAD)
    )
    self_queries_grad, self_keys_grad, self_values_grad, self_score_grad = attention_backward(
        self_queries, self_keys, self_values, self_bias, self_mask, self_totals, self_mixed_grad
    )
    table_grad = jnp.einsum(
        "pgrqk,qkb->grb", self_score_grad, onehot, preferred_element_type=jnp.float32
    ).reshape(HEADS * BUCKETS)
    queries_low = self_queries_grad.astype(jnp.bfloat16).reshape(row_count, D)
    keys_low = self_keys_grad.astype(jnp.bfloat16).reshape(row_count, KEYS)
    values_low = self_values_grad.astype(jnp.bfloat16).reshape(row_count, KEYS)
    self_query_grad = matmul(normed_one.T, queries_low)
    self_key_grad = matmul(normed_one.T, keys_low)
    self_value_grad = matmul(normed_one.T, values_low)
    normed_one_grad = (
        matmul(queries_low, full_self_query.T)
        + matmul(keys_low, full_self_key.T)
        + matmul(values_low, full_self_value.T)
    )
    norm_one_back, gain_self_grad = norm_back(inputs, full_gain_self, normed_one_grad)
    targets_grad = (hidden_one_grad + norm_one_back).astype(jnp.bfloat16)

    cross_sum = reduce_blocks(
        jnp.concatenate([cross_query_grad, memory_weight_grad, cross_output_grad], axis=1),
        tok_size,
        ffn_size,
    )
    small_grads = jnp.concatenate(
        [
            table_grad.reshape(devices, table_share),
            gain_self_grad.reshape(devices, gain_share),
            gain_cross_grad.reshape(devices, gain_share),
            gain_ffn_grad.reshape(devices, gain_share),
        ],
        axis=1,
    )
    small_grads = jnp.pad(
        small_grads[:, None, :], ((0, 0), (0, share - 1), (0, SMALL - small_grads.shape[1]))
    ).reshape(devices * share, SMALL)
    self_sum = reduce_blocks(
        jnp.concatenate(
            [self_query_grad, self_key_grad, self_value_grad, self_output_grad, small_grads], axis=1
        ),
        tok_size,
        ffn_size,
    )
    small_sum = self_sum[0, 2 * D + 2 * KEYS :]
    gains_at = [table_share + place * gain_share for place in range(4)]
    return (
        layer_out,
        targets_grad,
        memory_grad,
        rms_values,
        small_sum[:table_share],
        small_sum[gains_at[0] : gains_at[1]],
        small_sum[gains_at[1] : gains_at[2]],
        small_sum[gains_at[2] : gains_at[3]],
        self_sum[:, :D],
        self_sum[:, D : D + KEYS],
        self_sum[:, D + KEYS : D + 2 * KEYS],
        self_sum[:, D + 2 * KEYS : 2 * D + 2 * KEYS],
        cross_sum[:, :D],
        cross_sum[:, D : D + KEYS],
        cross_sum[:, D + KEYS : D + 2 * KEYS],
        cross_sum[:, D + 2 * KEYS :],
        gate_weight_grad,
        up_weight_grad,
        down_weight_grad,
    )


def solution(mesh):
    rows = P(("tok", "ffn"), None)
    flat = P(("tok", "ffn"))
    memory = P("tok", "ffn", None)
    columns, inner = P(None, "ffn"), P("ffn", None)
    in_specs = (
        (rows, memory, rows, flat, flat, P()) + (flat,) * 4 + (rows,) * 8 + (columns, columns, inner)
    )
    out_specs = (
        (rows, rows, memory, rows) + (flat,) * 4 + (rows,) * 8 + (columns, columns, inner)
    )
    return jax.shard_map(
        functools.partial(on_device, mesh.shape["tok"], mesh.shape["ffn"]),
        mesh=mesh,
        in_specs=in_specs,
        out_specs=out_specs,
        check_vma=False,
    )
```

```python
import functools

import jax
import jax.numpy as jnp
from jax import lax
from jax.experimental import pallas as pl
from jax.experimental.pallas import tpu as pltpu
from jax.sharding import PartitionSpec as P

D = 1024
HEADS = 16
HEAD = 64
GROUPS = 8
BUCKETS = 32
TGT = 128
KEYS = GROUPS * HEAD
SMALL = 128
VMEM = 56 * 1024 * 1024

norm_epsilon = 1e-06
masked_value = -1e30
bf16 = jnp.bfloat16
f32 = jnp.float32


def matmul(left, right):
    return jnp.dot(left, right, preferred_element_type=jnp.float32)


def contract(left, right, left_dim, right_dim):
    return lax.dot_general(
        left, right, (((left_dim,), (right_dim,)), ((), ())), preferred_element_type=jnp.float32
    )


def vmem_call(body, outs, operands, scalars=(), scratch=(), name=None, flops=1000000000):
    return pl.pallas_call(
        body,
        in_specs=[pl.BlockSpec(memory_space=pltpu.SMEM)] * len(scalars)
        + [pl.BlockSpec(memory_space=pltpu.VMEM)] * len(operands),
        out_specs=[pl.BlockSpec(memory_space=pltpu.VMEM)] * len(outs),
        out_shape=[jax.ShapeDtypeStruct(shape, dtype) for shape, dtype in outs],
        scratch_shapes=list(scratch),
        compiler_params=pltpu.CompilerParams(vmem_limit_bytes=VMEM),
        cost_estimate=pl.CostEstimate(flops=flops, bytes_accessed=8000000, transcendentals=0),
        name=name,
    )(*scalars, *operands)


def inverse_root(hidden):
    return lax.rsqrt(jnp.mean(hidden * hidden, axis=-1, keepdims=True) + norm_epsilon)


def norm_pull(hidden, gain, cotangent):
    scale = inverse_root(hidden)
    weighted = cotangent * gain
    inner = jnp.mean(hidden * weighted, axis=-1, keepdims=True)
    hidden_grad = scale * weighted - hidden * (scale * scale * scale * inner)
    return hidden_grad, jnp.sum(cotangent * hidden * scale, axis=0, keepdims=True)


def self_pieces(pair, group, wide_ref):
    rows = slice(pair * TGT, (pair + 1) * TGT)
    start = group * 2 * HEAD
    queries = jnp.concatenate(
        [wide_ref[rows, start : start + HEAD], wide_ref[rows, start + HEAD : start + 2 * HEAD]],
        axis=0,
    )
    start = D + group * HEAD
    return (
        queries,
        wide_ref[rows, start : start + HEAD],
        wide_ref[rows, start + KEYS : start + KEYS + HEAD],
    )


def self_scores(queries, keys, bias, length):
    raw = contract(keys, queries, 1, 1) * HEAD ** (-0.5) + bias
    key = lax.broadcasted_iota(jnp.int32, (TGT, 2 * TGT), 0)
    query = lax.broadcasted_iota(jnp.int32, (TGT, 2 * TGT), 1) % TGT
    return jnp.where((key <= query) & (key < length), raw, masked_value)


def self_bias(table_ref, bucket_ref, group):
    buckets = bucket_ref[...]
    return jnp.concatenate(
        [
            jnp.take_along_axis(
                jnp.broadcast_to(table_ref[head : head + 1, :], (TGT, TGT)), buckets, axis=1
            )
            for head in (2 * group, 2 * group + 1)
        ],
        axis=1,
    )


def self_forward_kernel(
    length_ref, row_ref, weight_ref, gain_ref, table_ref, bucket_ref, norm_ref, wide_ref, mix_ref, stat_ref
):
    inputs = row_ref[...].astype(f32)
    normed = (inputs * inverse_root(inputs) * gain_ref[0:1, :]).astype(bf16)
    norm_ref[...] = normed
    wide_ref[...] = matmul(normed, weight_ref[:, : D + 2 * KEYS]).astype(bf16)
    for group in range(GROUPS):
        bias = self_bias(table_ref, bucket_ref, group)
        for pair in range(row_ref.shape[0] // TGT):
            queries, keys, values = self_pieces(pair, group, wide_ref)
            scores = self_scores(queries, keys, bias, length_ref[pair])
            highest = jnp.max(scores, axis=0, keepdims=True)
            weights = jnp.exp(scores - highest)
            totals = jnp.sum(weights, axis=0, keepdims=True)
            probs = (weights * (1.0 / totals)).astype(bf16)
            mixed = contract(probs, values, 0, 0).astype(bf16)
            start = group * 2 * HEAD
            mix_ref[pair * TGT : (pair + 1) * TGT, start : start + 2 * HEAD] = jnp.concatenate(
                [mixed[:TGT], mixed[TGT:]], axis=1
            )
            logsum = highest + jnp.log(totals)
            at = pair * HEADS + 2 * group
            stat_ref[at : at + 1, :] = logsum[:, :TGT]
            stat_ref[at + 1 : at + 2, :] = logsum[:, TGT:]


def self_forward(lengths, rows, weights, gains, table, buckets):
    count = rows.shape[0]
    return vmem_call(
        self_forward_kernel,
        [
            ((count, D), bf16),
            ((count, D + 2 * KEYS), bf16),
            ((count, D), bf16),
            ((count // TGT * HEADS, TGT), f32),
        ],
        [rows, weights, gains, table, buckets],
        [lengths],
        name="self_forward",
    )


def self_output_kernel(row_ref, mix_ref, weight_ref, gain_ref, hidden_ref, norm_ref, query_ref, square_ref):
    branch = matmul(mix_ref[...], weight_ref[:, :D])
    square_ref[...] = jnp.sum(branch * branch, axis=1, keepdims=True)
    hidden = row_ref[...].astype(f32) + branch
    hidden_ref[...] = hidden
    normed = (hidden * inverse_root(hidden) * gain_ref[1:2, :]).astype(bf16)
    norm_ref[...] = normed
    queries = matmul(normed, weight_ref[:, D:]).astype(bf16) * bf16(HEAD ** (-0.5))
    query_ref[...] = queries.T


def self_output_part(rows, mixed, weights, gains):
    count = rows.shape[0]
    return vmem_call(
        self_output_kernel,
        [((count, D), f32), ((count, D), bf16), ((D, count), bf16), ((count, 1), f32)],
        [rows, mixed, weights, gains],
        name="self_output",
    )


def cross_join_kernel(
    hidden_ref, gain_ref, weight_ref, *refs
):
    parts, (mix_ref, stat_ref, out_ref, norm_ref, square_ref) = refs[:-5], refs[-5:]
    logs = [join_terms(part[D : D + 3 * HEADS, :]) for part in parts]
    highest = functools.reduce(jnp.maximum, logs)
    weights = [jnp.exp(log - highest) for log in logs]
    totals = functools.reduce(jnp.add, weights)
    stat_ref[...] = highest + jnp.log(totals)
    weights = [weight * (1.0 / totals) for weight in weights]
    for head in range(HEADS):
        at = slice(head * HEAD, (head + 1) * HEAD)
        mix_ref[at, :] = functools.reduce(
            jnp.add,
            [
                part[at, :].astype(f32) * weight[head : head + 1, :]
                for part, weight in zip(parts, weights, strict=True)
            ],
        )
    branch = contract(mix_ref[...].astype(bf16), weight_ref[...], 0, 0)
    square_ref[...] = jnp.sum(branch * branch, axis=1, keepdims=True)
    hidden = hidden_ref[...] + branch
    out_ref[...] = hidden
    norm_ref[...] = (hidden * inverse_root(hidden) * gain_ref[2:3, :]).astype(bf16)


def cross_join(hidden, gains, weights, parts):
    count = hidden.shape[0]
    return vmem_call(
        cross_join_kernel,
        [
            ((D, count), f32),
            ((HEADS, count), f32),
            ((count, D), f32),
            ((count, D), bf16),
            ((count, 1), f32),
        ],
        [hidden, gains, weights, *parts],
        name="cross_join",
    )


def ffn_join_kernel(cotangent_ref, hidden_ref, gain_ref, weight_ref, mix_ref, stat_ref, *refs):
    parts, (grad_ref, low_ref, pack_ref, gain_grad_ref) = refs[:-4], refs[-4:]
    norm_grad = functools.reduce(jnp.add, [part[...].astype(f32) for part in parts])
    back, gain_grad_ref[...] = norm_pull(hidden_ref[...], gain_ref[2:3, :], norm_grad)
    grad = cotangent_ref[...].astype(f32) + back
    grad_ref[...] = grad
    low = grad.astype(bf16)
    low_ref[...] = low
    mixed_grad = contract(weight_ref[...], low, 1, 1).astype(bf16)
    pack_ref[:D, :] = mixed_grad
    product = mixed_grad.astype(f32) * mix_ref[...]
    inner = jnp.concatenate(
        [
            jnp.sum(product[head * HEAD : (head + 1) * HEAD], axis=0, keepdims=True)
            for head in range(HEADS)
        ],
        axis=0,
    )
    for place, term in enumerate(split_terms(stat_ref[...]) + split_terms(inner)):
        pack_ref[D + place * HEADS : D + (place + 1) * HEADS, :] = term


def ffn_join(cotangent, hidden, gains, weights, mixed, stats, parts):
    count = hidden.shape[0]
    return vmem_call(
        ffn_join_kernel,
        [((count, D), f32), ((count, D), bf16), ((D + 6 * HEADS, count), bf16), ((1, D), f32)],
        [cotangent, hidden, gains, weights, mixed, stats, *parts],
        name="ffn_join",
    )


def query_join_kernel(grad_ref, hidden_ref, gain_ref, weight_ref, *refs):
    parts, (sum_ref, out_ref, low_ref, mix_grad_ref, gain_grad_ref) = refs[:-5], refs[-5:]
    queries = functools.reduce(jnp.add, [part[...].astype(f32) for part in parts]).astype(bf16)
    sum_ref[...] = queries
    norm_grad = contract(queries, weight_ref[:, D:], 0, 1)
    back, gain_grad_ref[...] = norm_pull(hidden_ref[...], gain_ref[1:2, :], norm_grad)
    grad = grad_ref[...] + back
    out_ref[...] = grad
    low = grad.astype(bf16)
    low_ref[...] = low
    mix_grad_ref[...] = contract(low, weight_ref[:, :D], 1, 1).astype(bf16)


def query_join(grad, hidden, gains, weights, parts):
    count = hidden.shape[0]
    return vmem_call(
        query_join_kernel,
        [
            ((D, count), bf16),
            ((count, D), f32),
            ((count, D), bf16),
            ((count, D), bf16),
            ((1, D), f32),
        ],
        [grad, hidden, gains, weights, *parts],
        name="query_join",
    )


def self_backward_kernel(
    length_ref,
    mix_grad_ref,
    wide_ref,
    stat_ref,
    table_ref,
    bucket_ref,
    wide_grad_ref,
    table_grad_ref,
    score_ref,
):
    pairs = mix_grad_ref.shape[0] // TGT
    for group in range(GROUPS):
        bias = self_bias(table_ref, bucket_ref, group)
        score_total = None
        for pair in range(pairs):
            queries, keys, values = self_pieces(pair, group, wide_ref)
            rows = slice(pair * TGT, (pair + 1) * TGT)
            start = group * 2 * HEAD
            mixed_grad = jnp.concatenate(
                [
                    mix_grad_ref[rows, start : start + HEAD],
                    mix_grad_ref[rows, start + HEAD : start + 2 * HEAD],
                ],
                axis=0,
            )
            at = pair * HEADS + 2 * group
            logsum = jnp.concatenate([stat_ref[at : at + 1, :], stat_ref[at + 1 : at + 2, :]], axis=1)
            scores = self_scores(queries, keys, bias, length_ref[pair])
            probs = jnp.exp(scores - logsum)
            prob_grad = contract(values, mixed_grad, 1, 1)
            inner = jnp.sum(probs * prob_grad, axis=0, keepdims=True)
            score_grad = (probs * (prob_grad - inner)).astype(bf16)
            value_grad = matmul(probs.astype(bf16), mixed_grad).astype(bf16)
            key_grad = (matmul(score_grad, queries) * HEAD ** (-0.5)).astype(bf16)
            query_grad = (contract(score_grad, keys, 0, 0) * HEAD ** (-0.5)).astype(bf16)
            wide_grad_ref[rows, start : start + 2 * HEAD] = jnp.concatenate(
                [query_grad[:TGT], query_grad[TGT:]], axis=1
            )
            start = D + group * HEAD
            wide_grad_ref[rows, start : start + HEAD] = key_grad
            wide_grad_ref[rows, start + KEYS : start + KEYS + HEAD] = value_grad
            wide = score_grad.astype(f32)
            score_total = wide if score_total is None else score_total + wide
        score_ref[2 * group] = score_total[:, :TGT]
        score_ref[2 * group + 1] = score_total[:, TGT:]
    buckets = bucket_ref[...]
    lane = lax.broadcasted_iota(jnp.int32, (HEADS, TGT), 1)

    def one_bucket(bucket, table_grad):
        inside = buckets == bucket
        sums = jnp.concatenate(
            [
                jnp.sum(jnp.where(inside, score_ref[head], 0.0), axis=0, keepdims=True)
                for head in range(HEADS)
            ],
            axis=0,
        )
        return jnp.where(lane == bucket, jnp.sum(sums, axis=1, keepdims=True), table_grad)

    table_grad_ref[...] = lax.fori_loop(0, BUCKETS, one_bucket, jnp.zeros((HEADS, TGT), f32))


def self_backward(lengths, mix_grad, wide, stats, table, buckets):
    return vmem_call(
        self_backward_kernel,
        [(wide.shape, bf16), ((HEADS, TGT), f32)],
        [mix_grad, wide, stats, table, buckets],
        [lengths],
        [pltpu.VMEM((HEADS, TGT, TGT), f32)],
        name="self_backward",
        flops=8000000000,
    )


def input_grads_kernel(wide_grad_ref, weight_ref, gain_ref, row_ref, grad_ref, out_ref, gain_grad_ref):
    norm_grad = contract(wide_grad_ref[...], weight_ref[:, : D + 2 * KEYS], 1, 1)
    back, gain_grad_ref[...] = norm_pull(row_ref[...].astype(f32), gain_ref[0:1, :], norm_grad)
    out_ref[...] = (grad_ref[...] + back).astype(bf16)


def input_grads(wide_grad, weights, gains, rows, grad):
    return vmem_call(
        input_grads_kernel,
        [(rows.shape, bf16), ((1, D), f32)],
        [wide_grad, weights, gains, rows, grad],
        name="input_grads",
    )


def split_terms(value):
    high = value.astype(bf16)
    rest = value - high.astype(f32)
    middle = rest.astype(bf16)
    low = (rest - middle.astype(f32)).astype(bf16)
    return [high, middle, low]


def join_terms(block):
    return (
        block[:HEADS].astype(f32)
        + block[HEADS : 2 * HEADS].astype(f32)
        + block[2 * HEADS : 3 * HEADS].astype(f32)
    )


def both_heads(ref, group):
    start = group * 2 * HEAD
    return jnp.concatenate(
        [ref[start : start + HEAD, :], ref[start + HEAD : start + 2 * HEAD, :]], axis=1
    )


def both_rows(stat, group):
    return jnp.concatenate([stat[2 * group : 2 * group + 1], stat[2 * group + 1 : 2 * group + 2]], axis=1)


def valid_positions(info_ref, chunk, pair, positions):
    held = positions // 2
    length = info_ref[chunk, 3 + pair]
    place = lax.broadcasted_iota(jnp.int32, (positions, 2 * TGT), 0)
    limit = jnp.where(
        place < held, length - info_ref[chunk, 1], held + length - info_ref[chunk, 2]
    )
    return place < limit


def cross_forward_kernel(chunk, info_ref, query_ref, memory_ref, mix_ref, stat_ref):
    pair = pl.program_id(0)
    mask = valid_positions(info_ref, chunk, pair, memory_ref.shape[1])
    for group in range(GROUPS):
        keys = memory_ref[0, :, group * HEAD : (group + 1) * HEAD]
        values = memory_ref[0, :, KEYS + group * HEAD : KEYS + (group + 1) * HEAD]
        scores = jnp.where(mask, matmul(keys, both_heads(query_ref, group)), masked_value)
        highest = jnp.max(scores, axis=0, keepdims=True)
        weights = jnp.exp(scores - highest)
        totals = jnp.sum(weights, axis=0, keepdims=True)
        mixed = contract(weights.astype(bf16), values, 0, 0).T * (1.0 / totals)
        mixed = mixed.astype(bf16)
        start = group * 2 * HEAD
        mix_ref[start : start + HEAD, :] = mixed[:, :TGT]
        mix_ref[start + HEAD : start + 2 * HEAD, :] = mixed[:, TGT:]
        logsum = highest + jnp.log(totals)
        stat_ref[2 * group : 2 * group + 1, :] = logsum[:, :TGT]
        stat_ref[2 * group + 1 : 2 * group + 2, :] = logsum[:, TGT:]
    for place, term in enumerate(split_terms(stat_ref[...])):
        mix_ref[D + place * HEADS : D + (place + 1) * HEADS, :] = term


def cross_forward(chunk, info, queries, memory_parts):
    positions, wide = memory_parts.shape[1], memory_parts.shape[2]
    rows = queries.shape[1]
    return pl.pallas_call(
        functools.partial(cross_forward_kernel, chunk),
        grid_spec=pltpu.PrefetchScalarGridSpec(
            num_scalar_prefetch=1,
            grid=(rows // TGT,),
            in_specs=[
                pl.BlockSpec((D, TGT), lambda pair, info: (0, pair)),
                pl.BlockSpec((1, positions, wide), lambda pair, info: (info[chunk, 0] + pair, 0, 0)),
            ],
            out_specs=pl.BlockSpec((D + 3 * HEADS, TGT), lambda pair, info: (0, pair)),
            scratch_shapes=[pltpu.VMEM((HEADS, TGT), f32)],
        ),
        out_shape=jax.ShapeDtypeStruct((D + 3 * HEADS, rows), bf16),
        compiler_params=pltpu.CompilerParams(vmem_limit_bytes=VMEM),
        cost_estimate=pl.CostEstimate(flops=6000000000, bytes_accessed=4000000, transcendentals=0),
        name="cross_forward",
    )(info, queries, memory_parts)


def cross_backward_kernel(chunk, info_ref, query_ref, grad_ref, memory_ref, *rest):
    query_grad_ref, memory_grad_ref = rest[-2:]
    pair = pl.program_id(0)
    mask = valid_positions(info_ref, chunk, pair, memory_ref.shape[1])
    logsum = join_terms(grad_ref[D : D + 3 * HEADS, :])
    inner = join_terms(grad_ref[D + 3 * HEADS : D + 6 * HEADS, :])
    for tile in range(GROUPS // 2):
        key_parts, value_parts = [], []
        for group in (2 * tile, 2 * tile + 1):
            keys = memory_ref[0, :, group * HEAD : (group + 1) * HEAD]
            values = memory_ref[0, :, KEYS + group * HEAD : KEYS + (group + 1) * HEAD]
            queries = both_heads(query_ref, group)
            mixed_grad = both_heads(grad_ref, group)
            scores = matmul(keys, queries) - both_rows(logsum, group)
            probs = jnp.exp(jnp.where(mask, scores, masked_value))
            prob_grad = matmul(values, mixed_grad) - both_rows(inner, group)
            score_grad = (probs * prob_grad).astype(bf16)
            value_parts.append(contract(probs.astype(bf16), mixed_grad, 1, 1).astype(bf16))
            key_parts.append(contract(score_grad, queries, 1, 1).astype(bf16))
            query_grad = (contract(keys, score_grad, 0, 0) * HEAD ** (-0.5)).astype(bf16)
            start = group * 2 * HEAD
            query_grad_ref[start : start + HEAD, :] = query_grad[:, :TGT]
            query_grad_ref[start + HEAD : start + 2 * HEAD, :] = query_grad[:, TGT:]
        columns = 2 * HEAD * tile
        memory_grad_ref[0, :, columns : columns + 2 * HEAD] = jnp.concatenate(key_parts, axis=1)
        memory_grad_ref[0, :, KEYS + columns : KEYS + columns + 2 * HEAD] = jnp.concatenate(
            value_parts, axis=1
        )


def cross_backward(chunk, info, queries, grads, memory_parts, *earlier):
    positions, wide = memory_parts.shape[1], memory_parts.shape[2]
    rows = queries.shape[1]
    place = pl.BlockSpec((1, positions, wide), lambda pair, info: (info[chunk, 0] + pair, 0, 0))
    return pl.pallas_call(
        functools.partial(cross_backward_kernel, chunk),
        grid_spec=pltpu.PrefetchScalarGridSpec(
            num_scalar_prefetch=1,
            grid=(rows // TGT,),
            in_specs=[
                pl.BlockSpec((D, TGT), lambda pair, info: (0, pair)),
                pl.BlockSpec((D + 6 * HEADS, TGT), lambda pair, info: (0, pair)),
                place,
            ]
            + [pl.BlockSpec(memory_space=pl.ANY)] * len(earlier),
            out_specs=[pl.BlockSpec((D, TGT), lambda pair, info: (0, pair)), place],
        ),
        out_shape=[
            jax.ShapeDtypeStruct((D, rows), bf16),
            jax.ShapeDtypeStruct(memory_parts.shape, bf16),
        ],
        input_output_aliases={4: 1} if earlier else {},
        compiler_params=pltpu.CompilerParams(vmem_limit_bytes=VMEM),
        cost_estimate=pl.CostEstimate(flops=10000000000, bytes_accessed=8000000, transcendentals=0),
        name="cross_backward",
    )(info, queries, grads, memory_parts, *earlier)


def ffn_kernel(row_ref, cotangent_ref, gate_ref, up_ref, down_ref, *rest):
    row_grad_ref, branch_ref, rows_ref, hidden_ref, gate_grad_ref, up_grad_ref = rest[-6:]
    rows = row_ref[...]
    rows_ref[0] = rows
    gate = matmul(rows, gate_ref[...])
    up = matmul(rows, up_ref[...])
    hidden_grad = contract(cotangent_ref[...], down_ref[...], 1, 1)
    square = gate * gate
    slope = 0.7978845608028654
    bend = jnp.tanh(slope * gate * (1.0 + 0.044715 * square))
    half = 0.5 * (1.0 + bend)
    value = gate * half
    derivative = half + 0.5 * gate * (1.0 - bend * bend) * slope * (1.0 + 3 * 0.044715 * square)
    hidden = (value * up).astype(bf16)
    gate_grad = (hidden_grad * up * derivative).astype(bf16)
    up_grad = (hidden_grad * value).astype(bf16)
    row_grad = contract(gate_grad, gate_ref[...], 1, 1) + contract(up_grad, up_ref[...], 1, 1)
    row_grad_ref[...] = row_grad.astype(bf16)
    branch_ref[...] = matmul(hidden, down_ref[...]).astype(bf16)
    hidden_ref[0] = hidden
    gate_grad_ref[0] = gate_grad
    up_grad_ref[0] = up_grad


def ffn_chunk(chunk, chunks, rows, cotangent, gate, up, down, *earlier):
    count, width = rows.shape
    wide = gate.shape[1]
    kept = [width, wide, wide, wide]
    return pl.pallas_call(
        ffn_kernel,
        grid=(1,),
        in_specs=[
            pl.BlockSpec((count, width), lambda step: (0, 0)),
            pl.BlockSpec((count, width), lambda step: (0, 0)),
            pl.BlockSpec(gate.shape, lambda step: (0, 0)),
            pl.BlockSpec(up.shape, lambda step: (0, 0)),
            pl.BlockSpec(down.shape, lambda step: (0, 0)),
        ]
        + [pl.BlockSpec(memory_space=pl.ANY)] * len(earlier),
        out_specs=[pl.BlockSpec((count, width), lambda step: (0, 0))] * 2
        + [pl.BlockSpec((1, count, size), lambda step: (chunk, 0, 0)) for size in kept],
        out_shape=[jax.ShapeDtypeStruct((count, width), bf16)] * 2
        + [jax.ShapeDtypeStruct((chunks, count, size), bf16) for size in kept],
        input_output_aliases={5 + place: 2 + place for place in range(len(earlier))},
        compiler_params=pltpu.CompilerParams(vmem_limit_bytes=VMEM),
        cost_estimate=pl.CostEstimate(flops=3000000000, bytes_accessed=8000000, transcendentals=0),
        name="ffn_chunk",
    )(rows, cotangent, gate, up, down, *earlier)


def exchange(value, axis, size, mask):
    return lax.ppermute(value, axis, [(place, place ^ mask) for place in range(size)])


def gather_chunks(value, size):
    lines = size // 2
    if lines != 4:
        return [value] + [exchange(value, "ffn", size, 2 * step) for step in range(1, lines)]

    def by_lines(array, pairs):
        pairs = [(2 * old + core, 2 * new + core) for old, new in pairs for core in range(2)]
        return lax.ppermute(array, "ffn", pairs)

    across = exchange(value, "ffn", size, 4)
    beside = exchange(value, "ffn", size, 2)
    middle = by_lines(value, [(1, 2), (2, 1)])
    onward = by_lines(across, [(2, 3), (1, 0)])
    line = lax.axis_index("ffn") // 2
    return [value, beside, across, jnp.where((line == 0) | (line == 3), onward, middle)]


def return_chunks(parts, size):
    return [parts[0]] + [
        exchange(parts[step], "ffn", size, 2 * step) for step in range(1, size // 2)
    ]


def join_sums(parts):
    return functools.reduce(jnp.add, [part.astype(f32) for part in parts])


def reduce_rows(grads, tok_size, ffn_size):
    columns = grads.shape[1]
    me_ffn, me_tok = lax.axis_index("ffn"), lax.axis_index("tok")

    def halves(value, dim, bit):
        first = lax.index_in_dim(value, 0, dim, keepdims=False)
        second = lax.index_in_dim(value, 1, dim, keepdims=False)
        return jnp.where(bit == 0, first, second), jnp.where(bit == 0, second, first)

    rows = grads.shape[0] // (tok_size * ffn_size)
    value = grads.reshape(tok_size, ffn_size // 2, 2, rows, columns)
    kept, sent = halves(value, 2, me_ffn & 1)
    value = kept.astype(f32) + exchange(sent.astype(bf16), "ffn", ffn_size, 1).astype(f32)

    bits = tok_size.bit_length() - 1
    value = value.reshape((2,) * bits + (ffn_size // 2, rows, columns))
    half = columns // 2 // 128 * 128
    sides = []
    for part, order in (
        (value[..., :half], list(range(bits))),
        (value[..., half:], list(range(bits))[::-1]),
    ):
        left = list(range(bits))
        for bit in order:
            dim = left.index(bit)
            left.remove(bit)
            weight = 1 << (bits - 1 - bit)
            kept, sent = halves(part, dim, (me_tok // weight) & 1)
            part = kept.astype(f32) + exchange(sent.astype(bf16), "tok", tok_size, weight).astype(f32)
        sides.append(part)
    value = jnp.concatenate(sides, axis=-1)
    line = me_ffn // 2
    total = lax.dynamic_index_in_dim(value, line, 0, keepdims=False)
    low = value.astype(bf16)
    for step in range(1, ffn_size // 2):
        part = lax.dynamic_index_in_dim(low, line ^ step, 0, keepdims=False)
        total = total + exchange(part, "ffn", ffn_size, 2 * step).astype(f32)
    return total


def memory_forward_kernel(own_ref, other_ref, weight_ref, out_ref):
    pairs, held, width = own_ref.shape
    for place, ref in enumerate((own_ref, other_ref)):
        part = matmul(ref[...].reshape(pairs * held, width), weight_ref[...]).astype(bf16)
        out_ref[:, place] = part.reshape(pairs, held, part.shape[1])


def memory_forward(own, other, weights, column):
    pairs, held, width = own.shape
    step = 4 if pairs % 4 == 0 else 1
    block = pl.BlockSpec((step, held, width), lambda pair: (pair, 0, 0))
    return pl.pallas_call(
        memory_forward_kernel,
        grid=(pairs // step,),
        in_specs=[
            block,
            block,
            pl.BlockSpec((width, 2 * KEYS), lambda pair: (0, column // (2 * KEYS))),
        ],
        out_specs=pl.BlockSpec((step, 2, held, 2 * KEYS), lambda pair: (pair, 0, 0, 0)),
        out_shape=jax.ShapeDtypeStruct((pairs, 2, held, 2 * KEYS), bf16),
        compiler_params=pltpu.CompilerParams(vmem_limit_bytes=VMEM),
        cost_estimate=pl.CostEstimate(flops=8600000000, bytes_accessed=18000000, transcendentals=0),
        name="memory_forward",
    )(own, other, weights)


def memory_backward_kernel(sizes, me_ref, own_ref, other_ref, grad_ref, weight_ref, *rest):
    own_grad_ref, other_grad_ref, sum_ref, total = rest
    step = pl.program_id(0)
    pairs, held, width = own_ref.shape
    for place, (ref, out_ref) in enumerate(((own_ref, own_grad_ref), (other_ref, other_grad_ref))):
        grads = grad_ref[:, place].reshape(pairs * held, grad_ref.shape[3])
        out = contract(grads, weight_ref[...], 1, 1).astype(bf16)
        out_ref[...] = out.reshape(out_ref.shape)
        part = contract(ref[...].reshape(pairs * held, width), grads, 0, 0)
        if place == 0:
            total[...] = jnp.where(step == 0, part, total[...] + part)
        else:
            total[...] += part

    @pl.when(step == pl.num_programs(0) - 1)
    def last():
        store_blocks(sizes, me_ref, sum_ref, 0, total[...])


def memory_backward(sizes, me, own, other, grads, weights, column):
    lines = sizes[1] // 2
    pairs, held, width = own.shape
    step = pairs // lines
    block = pl.BlockSpec((step, held, width), lambda line, me: (line, 0, 0))
    shape = blocks_shape(sizes, 2 * KEYS)
    return pl.pallas_call(
        functools.partial(memory_backward_kernel, sizes),
        grid_spec=pltpu.PrefetchScalarGridSpec(
            num_scalar_prefetch=1,
            grid=(lines,),
            in_specs=[
                block,
                block,
                pl.BlockSpec((step, 2, held, 2 * KEYS), lambda line, me: (line, 0, 0, 0)),
                pl.BlockSpec((width, 2 * KEYS), lambda line, me: (0, column // (2 * KEYS))),
            ],
            out_specs=[
                pl.BlockSpec((1, 1, step, held, width), lambda line, me: (line, me[2], 0, 0, 0)),
                block,
                pl.BlockSpec(shape, lambda line, me: (0,) * len(shape)),
            ],
            scratch_shapes=[pltpu.VMEM((width, 2 * KEYS), f32)],
        ),
        out_shape=[
            jax.ShapeDtypeStruct((lines, 2, step, held, width), bf16),
            jax.ShapeDtypeStruct(own.shape, bf16),
            jax.ShapeDtypeStruct(shape, bf16),
        ],
        compiler_params=pltpu.CompilerParams(vmem_limit_bytes=VMEM),
        cost_estimate=pl.CostEstimate(flops=17200000000, bytes_accessed=28000000, transcendentals=0),
        name="memory_backward",
    )(me, own, other, grads, weights)


def place_pairs_kernel(me_ref, pair_ref, unused_ref, out_ref):
    out_ref[0, 0] = pair_ref[...]


def place_pairs(me, whole, pairs):
    lines, unused, step, held, width = whole.shape
    return pl.pallas_call(
        place_pairs_kernel,
        grid_spec=pltpu.PrefetchScalarGridSpec(
            num_scalar_prefetch=1,
            grid=(lines,),
            in_specs=[
                pl.BlockSpec((step, held, width), lambda line, me: (line, 0, 0)),
                pl.BlockSpec(memory_space=pl.ANY),
            ],
            out_specs=pl.BlockSpec(
                (1, 1, step, held, width), lambda line, me: (line, 1 - me[2], 0, 0, 0)
            ),
        ),
        out_shape=jax.ShapeDtypeStruct(whole.shape, bf16),
        input_output_aliases={2: 0},
        compiler_params=pltpu.CompilerParams(vmem_limit_bytes=VMEM),
        name="place_pairs",
    )(me, pairs, whole)


def blocks_shape(sizes, columns):
    tok_size, ffn_size = sizes
    return (2, tok_size * ffn_size // 2, D // (tok_size * ffn_size), columns)


def store_blocks(sizes, me_ref, out_ref, column, value):
    tok_size, ffn_size = sizes
    rows = D // (tok_size * ffn_size)
    low = value.astype(bf16)
    for block in range(tok_size * ffn_size):
        tok, line, core = block // ffn_size, block % ffn_size // 2, block % 2
        place = (tok ^ me_ref[0]) * (ffn_size // 2) + (line ^ me_ref[1])
        out_ref[core ^ me_ref[2], place, :, column : column + value.shape[1]] = low[
            block * rows : (block + 1) * rows
        ]


def grad_blocks_kernel(sizes, dims, me_ref, *refs):
    out_ref = refs[-1]
    column = 0
    for place, (left_dim, right_dim) in enumerate(dims):
        left, right = refs[2 * place], refs[2 * place + 1]
        for start in range(0, right.shape[1 - right_dim], 512):
            if right_dim == 0:
                part = right[:, start : start + 512]
            else:
                part = right[start : start + 512, :]
            store_blocks(
                sizes, me_ref, out_ref, column, contract(left[...], part, left_dim, right_dim)
            )
            column += 512
    for ref in refs[2 * len(dims) : -1]:
        if len(ref.shape) == 4:
            out_ref[:, :, :, column : column + ref.shape[3]] = ref[...]
            column += ref.shape[3]
        else:
            filled = jnp.concatenate(
                [ref[...], jnp.zeros((SMALL - ref.shape[0], ref.shape[1]), f32)], axis=0
            )
            store_blocks(sizes, me_ref, out_ref, column, filled.T)
            column += SMALL


def grad_blocks(sizes, me, products, *extra):
    operands = [array for left, right, unused, also in products for array in (left, right)]
    columns = sum(right.shape[1 - dim] for unused, right, also, dim in products)
    for array in extra:
        operands.append(array)
        columns += array.shape[3] if array.ndim == 4 else SMALL
    return pl.pallas_call(
        functools.partial(grad_blocks_kernel, sizes, [(one[2], one[3]) for one in products]),
        in_specs=[pl.BlockSpec(memory_space=pltpu.SMEM)]
        + [pl.BlockSpec(memory_space=pltpu.VMEM)] * len(operands),
        out_specs=pl.BlockSpec(memory_space=pltpu.VMEM),
        out_shape=jax.ShapeDtypeStruct(blocks_shape(sizes, columns), bf16),
        compiler_params=pltpu.CompilerParams(vmem_limit_bytes=VMEM),
        name="grad_blocks",
    )(me, *operands)


def plus(*parts):
    return functools.reduce(jnp.add, [part.astype(f32) for part in parts]).astype(bf16)


def reduce_core(sizes, blocks):
    lines = sizes[1] // 2
    other = exchange(blocks[1], "ffn", sizes[1], 1)
    return [
        plus(blocks[0, tok * lines : (tok + 1) * lines], other[tok * lines : (tok + 1) * lines])
        for tok in range(4)
    ]


def reduce_corner(sizes, parts):
    own, by_x, by_y, across = parts
    half = sizes[1] // 4
    top = exchange(across[:half], "tok", sizes[0], 1)
    bottom = exchange(across[half:], "tok", sizes[0], 2)
    by_x = jnp.concatenate([by_x[:half], plus(by_x[half:], bottom)], axis=0)
    by_y = jnp.concatenate([plus(by_y[:half], top), by_y[half:]], axis=0)
    return [own, by_x, by_y]


def reduce_sides(sizes, parts):
    own, by_x, by_y = parts
    return plus(own, exchange(by_x, "tok", sizes[0], 1), exchange(by_y, "tok", sizes[0], 2))


def reduce_line(sizes, total):
    parts = [total[0]] + [
        exchange(total[step], "ffn", sizes[1], 2 * step) for step in range(1, sizes[1] // 2)
    ]
    return functools.reduce(jnp.add, [part.astype(f32) for part in parts])


def place_rows_kernel(sizes, share, me_ref, *refs):
    tok_size, ffn_size = sizes
    lines = ffn_size // 2
    half = lines // 2
    out_ref, sems = refs[-2:]
    copies = []
    for core in range(2):
        line_ref, x_ref, y_ref, top_ref, bottom_ref = refs[5 * core : 5 * core + 5]
        for tok in range(4):
            for line in range(lines):
                if tok < 3:
                    source = (line_ref, x_ref, y_ref)[tok].at[line]
                else:
                    source = top_ref.at[line] if line < half else bottom_ref.at[line - half]
                block = ((tok ^ me_ref[0]) * lines + (line ^ me_ref[1])) * 2 + (core ^ me_ref[2])
                target = out_ref.at[pl.ds(pl.multiple_of(block * share, share), share), :]
                copies.append(pltpu.make_async_copy(source, target, sems.at[len(copies)]))
    for copy in copies:
        copy.start()
    for copy in copies:
        copy.wait()


def place_rows(sizes, me, held, share, columns):
    count = sizes[0] * sizes[1]
    return pl.pallas_call(
        functools.partial(place_rows_kernel, sizes, share),
        in_specs=[pl.BlockSpec(memory_space=pltpu.SMEM)]
        + [pl.BlockSpec(memory_space=pl.ANY)] * len(held),
        out_specs=pl.BlockSpec(memory_space=pltpu.VMEM),
        out_shape=jax.ShapeDtypeStruct((count * share, columns), bf16),
        scratch_shapes=[pltpu.SemaphoreType.DMA((count,))],
        compiler_params=pltpu.CompilerParams(vmem_limit_bytes=VMEM),
        name="place_rows",
    )(me, *held)


def after(values, earlier):
    return lax.optimization_barrier((values, earlier))[0]


def gather_blocks(sizes, me, packs, between):
    tok_size, ffn_size = sizes
    lines = ffn_size // 2
    half = lines // 2
    stages = [(), (), (), ()]
    for place, pack in enumerate(packs):
        share, columns = pack.shape
        pack = after(pack, stages[0])
        line = [pack] + [exchange(pack, "ffn", ffn_size, 2 * step) for step in range(1, lines)]
        stages[0] = line
        line = jnp.stack(after(line, stages[1]))
        by_x = exchange(line, "tok", tok_size, 1)
        by_y = exchange(line, "tok", tok_size, 2)
        stages[1] = [by_x, by_y]
        by_x, by_y = after([by_x, by_y], stages[2])
        top = exchange(by_y[:half], "tok", tok_size, 1)
        bottom = exchange(by_x[half:], "tok", tok_size, 2)
        stages[2] = [top, bottom]
        held = after([line, by_x, by_y, top, bottom], stages[3])
        held = held + [exchange(one, "ffn", ffn_size, 1) for one in held]
        stages[3] = between(place, place_rows(sizes, me, held, share, columns), stages[0])


def on_device(
    tok_size,
    ffn_size,
    targets,
    memory,
    out_grad,
    target_lengths,
    memory_lengths,
    buckets,
    rel_table,
    gain_self,
    gain_cross,
    gain_ffn,
    self_query,
    self_key,
    self_value,
    self_output,
    cross_query,
    cross_key,
    cross_value,
    cross_output,
    ffn_gate,
    ffn_up,
    ffn_down,
):
    pair_count = target_lengths.shape[0]
    row_count = targets.shape[0]
    held = memory.shape[1]
    devices = tok_size * ffn_size
    me_tok, me_ffn = lax.axis_index("tok"), lax.axis_index("ffn")
    share = self_query.shape[0]
    table_share = rel_table.shape[0]

    sizes = (tok_size, ffn_size)
    direct = tok_size == 4 and share % 16 == 0
    me = jnp.stack([me_tok, me_ffn // 2, me_ffn % 2]).astype(jnp.int32)
    per_row = [
        jnp.pad(part.astype(bf16), (0, share - part.shape[0]))
        for part in (gain_self, gain_cross, gain_ffn, rel_table, memory_lengths // 64, memory_lengths % 64)
    ]
    small = jnp.pad(jnp.stack(per_row, axis=1), ((0, 0), (0, SMALL - len(per_row))))

    core = me_ffn % 2
    lines = ffn_size // 2

    def by_parity(array, parity):
        array = array.reshape((lines, 2, pair_count) + array.shape[1:])
        array = lax.dynamic_index_in_dim(array, parity, 1, keepdims=False)
        return array.reshape((lines * pair_count,) + array.shape[2:])

    memory_own = by_parity(memory, core)
    memory_other = exchange(by_parity(memory, 1 - core), "ffn", ffn_size, 1)
    both_gate = jnp.concatenate([ffn_gate, exchange(ffn_gate, "ffn", ffn_size, 1)], axis=1)
    both_up = jnp.concatenate([ffn_up, exchange(ffn_up, "ffn", ffn_size, 1)], axis=1)
    both_down = jnp.concatenate([ffn_down, exchange(ffn_down, "ffn", ffn_size, 1)], axis=0)

    packs = [
        jnp.concatenate(parts, axis=1)
        for parts in (
            [self_query, self_key, self_value, small],
            [self_output, cross_query],
            [cross_key, cross_value, cross_output],
        )
    ]
    buckets = buckets.T
    kept = {}

    def begin(place, pack, begun):
        if place == 0:
            full_small = pack[:, D + 2 * KEYS : D + 2 * KEYS + len(per_row)].T.astype(f32)
            table = full_small[3].reshape(devices, share)[:, :table_share].reshape(HEADS, BUCKETS)
            kept["table"] = jnp.pad(table, ((0, 0), (0, TGT - BUCKETS)))
            lengths = (full_small[4] * 64 + full_small[5]).astype(jnp.int32)
            kept["lengths"] = lengths.reshape(devices, share)[:, :pair_count]
            kept["gains"] = full_small[:3]
            kept["self"] = self_forward(
                target_lengths,
                after(targets, (both_gate, both_up, both_down, memory_other, memory_own)),
                pack,
                kept["gains"],
                kept["table"],
                buckets,
            )
            result = kept["self"][2]
        elif place == 1:
            kept["output"] = self_output_part(targets, kept["self"][2], pack, kept["gains"])
            result = kept["output"][2]
        else:
            kept["cotangents"] = gather_chunks(after(out_grad, begun), ffn_size)
            kept["memory"] = memory_forward(memory_own, memory_other, pack, 0)
            result = kept["memory"]
        kept[place] = pack
        return result

    if direct:
        gather_blocks(sizes, me, packs, begin)
    else:
        for place, pack in enumerate(packs):
            begin(place, lax.all_gather(pack, ("tok", "ffn"), axis=0, tiled=True), pack)
    full_first, full_second, full_third = kept[0], kept[1], kept[2]
    gains, table, lengths = kept["gains"], kept["table"], kept["lengths"]
    cotangent_chunks = kept["cotangents"]
    normed_one, self_wide, self_mixed, self_stats = kept["self"]
    hidden_one, normed_two, cross_queries, self_squares = kept["output"]
    memory_parts = kept["memory"].reshape(-1, 2 * held, 2 * KEYS)
    cross_weight = full_third[:, 2 * KEYS :]
    lengths = lax.dynamic_index_in_dim(
        lengths.reshape(tok_size, ffn_size, pair_count), me_tok, 0, keepdims=False
    )
    owner = me_ffn ^ (2 * jnp.arange(lines))
    info = jnp.concatenate(
        [
            (owner // 2 * pair_count)[:, None],
            jnp.broadcast_to(me_ffn * held, (lines, 1)),
            jnp.broadcast_to((me_ffn ^ 1) * held, (lines, 1)),
            jnp.take(lengths, owner, axis=0),
        ],
        axis=1,
    ).astype(jnp.int32)


    position = jnp.arange(TGT)

    cross_queries = after(cross_queries, cotangent_chunks)
    query_chunks = gather_chunks(cross_queries, ffn_size)
    mixed_parts = []
    for chunk in range(lines):
        chunk_queries = query_chunks[chunk]
        if chunk:
            chunk_queries = after(chunk_queries, mixed_parts[-1])
        mixed_parts.append(cross_forward(chunk, info, chunk_queries, memory_parts))
    cross_mixed, cross_stats, hidden_two, normed_three, cross_squares = cross_join(
        hidden_one, gains, cross_weight, return_chunks(mixed_parts, ffn_size)
    )

    row_chunks = gather_chunks(normed_three, ffn_size)
    earlier, row_parts, branch_parts = [], [], []
    for chunk in range(lines):
        row_part, branch_part, *earlier = ffn_chunk(
            chunk,
            lines,
            row_chunks[chunk],
            cotangent_chunks[chunk],
            both_gate,
            both_up,
            both_down,
            *earlier,
        )
        row_parts.append(row_part)
        branch_parts.append(branch_part)
    row_parts = return_chunks(row_parts, ffn_size)
    all_rows, hidden, gate_grad, up_grad = [
        array.reshape(lines * row_count, array.shape[2]) for array in earlier
    ]
    all_cotangent = jnp.concatenate(cotangent_chunks, axis=0)
    units = ffn_gate.shape[1]
    weight_grads = []
    for part, dim in (
        (contract(all_rows, gate_grad, 0, 0), 1),
        (contract(all_rows, up_grad, 0, 0), 1),
        (contract(hidden, all_cotangent, 0, 0), 0),
    ):
        kept = lax.slice_in_dim(part, 0, units, axis=dim)
        sent = lax.slice_in_dim(part, units, 2 * units, axis=dim).astype(bf16)
        weight_grads.append((kept + exchange(sent, "ffn", ffn_size, 1).astype(f32)).astype(bf16))
    weight_sums = [lax.psum(part, "tok") for part in weight_grads]
    gate_weight_grad, up_weight_grad, down_weight_grad = [part.astype(f32) for part in weight_sums]

    row_parts = row_parts[:2] + after(row_parts[2:], weight_grads)
    hidden_two_grad, cross_low, grad_pack, gain_ffn_grad = ffn_join(
        out_grad, hidden_two, gains, cross_weight, cross_mixed, cross_stats, row_parts
    )
    output_product = (cross_mixed.astype(bf16), cross_low, 1, 0)
    stage = [grad_blocks(sizes, me, [output_product])] if direct else [()]
    grad_chunks = gather_chunks(grad_pack, ffn_size)
    earlier = []
    query_parts = []
    reductions = [reduce_core, reduce_corner, reduce_sides, reduce_line]
    for chunk in range(lines):
        part, memory_grads = cross_backward(
            chunk,
            info,
            after(query_chunks[chunk], stage[-1]),
            grad_chunks[chunk],
            memory_parts,
            *earlier,
        )
        earlier = [memory_grads]
        query_parts.append(part)
        if direct and chunk < 4:
            stage.append(reductions[chunk](sizes, stage[-1]))
    for reduction in reductions[lines:] if direct else ():
        stage.append(reduction(sizes, stage[-1]))
    output_sum = stage[-1]
    query_parts = return_chunks(query_parts, ffn_size)
    memory_grad, other_grad, memory_sum = memory_backward(
        sizes,
        me,
        memory_own,
        memory_other,
        after(memory_grads, query_parts[1]).reshape(-1, 2, held, 2 * KEYS),
        full_third,
        0,
    )
    query_parts = query_parts[:2] + after(query_parts[2:], (memory_sum, output_sum, weight_sums))
    query_grads, hidden_one_grad, self_low, mix_grad, gain_cross_grad = query_join(
        hidden_two_grad, hidden_one, gains, full_second, query_parts
    )
    other_grad = exchange(other_grad, "ffn", ffn_size, 1)
    memory_grad = place_pairs(me, memory_grad, other_grad).reshape(memory.shape)
    products = [(normed_two, query_grads, 0, 1), (self_mixed, self_low, 0, 0)]
    middle = ()
    if direct:
        middle = grad_blocks(sizes, me, products, memory_sum)
        mix_grad = after(mix_grad, (middle, other_grad))
        middle = reduce_core(sizes, middle)
    wide_grad, table_grad = self_backward(
        target_lengths, mix_grad, self_wide, self_stats, table, buckets
    )
    wide_grad = after(wide_grad, middle)
    targets_grad, gain_self_grad = input_grads(wide_grad, full_first, gains, targets, hidden_one_grad)

    branch_parts = after(branch_parts, query_grads)
    ffn_branch = join_sums(return_chunks(branch_parts, ffn_size))
    hidden_three = hidden_two + ffn_branch
    layer_out = hidden_three.astype(jnp.bfloat16)
    valid = position[None, :] < target_lengths[:, None]
    counted = target_lengths.astype(jnp.float32) * D
    squares = [
        jnp.sum(hidden_three * hidden_three, axis=1),
        self_squares[:, 0],
        cross_squares[:, 0],
        jnp.sum(ffn_branch * ffn_branch, axis=1),
    ]
    squares = jnp.stack([part.reshape(pair_count, TGT) for part in squares], axis=1)
    squares = jnp.sum(jnp.where(valid[:, None, :], squares, 0.0), axis=2)
    rms_values = jnp.sqrt(squares / counted[:, None])

    table_grad = jnp.pad(
        table_grad[:, :BUCKETS].reshape(devices, table_share), ((0, 0), (0, share - table_share))
    )
    small_rows = jnp.concatenate(
        [gain_self_grad, gain_cross_grad, gain_ffn_grad, table_grad.reshape(1, D), jnp.zeros((4, D), f32)]
    )
    last_product = (normed_one, wide_grad, 0, 0)
    if direct:
        middle = reduce_corner(sizes, middle)
        first = grad_blocks(sizes, me, [last_product], after(small_rows, middle))
        first = reduce_core(sizes, first)
        middle = reduce_sides(sizes, middle)
        first = reduce_corner(sizes, first)
        first = reduce_sides(sizes, first)
        middle_sum = reduce_line(sizes, middle)
        first_sum = reduce_line(sizes, first)
    else:
        order = [(block // ffn_size, block % ffn_size // 2, block % 2) for block in range(devices)]
        memory_rows = jnp.concatenate(
            [
                memory_sum[core ^ me[2], (tok ^ me[0]) * (ffn_size // 2) + (line ^ me[1])]
                for tok, line, core in order
            ]
        )
        output_sum, middle_sum, first_sum = [
            reduce_rows(jnp.concatenate(parts, axis=1), tok_size, ffn_size)
            for parts in (
                [contract(*output_product)],
                [contract(*one) for one in products] + [memory_rows],
                [contract(*last_product), jnp.pad(small_rows.T, ((0, 0), (0, SMALL - 8)))],
            )
        ]
    small_sum = first_sum[:, D + 2 * KEYS :]
    return (
        layer_out,
        targets_grad,
        memory_grad,
        rms_values,
        small_sum[:table_share, 3],
        small_sum[:, 0],
        small_sum[:, 1],
        small_sum[:, 2],
        first_sum[:, :D],
        first_sum[:, D : D + KEYS],
        first_sum[:, D + KEYS : D + 2 * KEYS],
        middle_sum[:, D : 2 * D],
        middle_sum[:, :D],
        middle_sum[:, 2 * D : 2 * D + KEYS],
        middle_sum[:, 2 * D + KEYS :],
        output_sum,
        gate_weight_grad,
        up_weight_grad,
        down_weight_grad,
    )


def solution(mesh):
    rows = P(("tok", "ffn"), None)
    flat = P(("tok", "ffn"))
    memory = P("tok", "ffn", None)
    columns, inner = P(None, "ffn"), P("ffn", None)
    in_specs = (
        (rows, memory, rows, flat, flat, P()) + (flat,) * 4 + (rows,) * 8 + (columns, columns, inner)
    )
    out_specs = (
        (rows, rows, memory, rows) + (flat,) * 4 + (rows,) * 8 + (columns, columns, inner)
    )
    return jax.shard_map(
        functools.partial(on_device, mesh.shape["tok"], mesh.shape["ffn"]),
        mesh=mesh,
        in_specs=in_specs,
        out_specs=out_specs,
        check_vma=False,
    )
```

```python
import functools

import jax
import jax.numpy as jnp
from jax import lax
from jax.experimental import pallas as pl
from jax.experimental.pallas import tpu as pltpu
from jax.sharding import PartitionSpec as P

D = 1024
HEADS = 16
HEAD = 64
GROUPS = 8
BUCKETS = 32
TGT = 128
KEYS = GROUPS * HEAD
SMALL = 128
VMEM = 56 * 1024 * 1024

norm_epsilon = 1e-06
masked_value = -1e30
bf16 = jnp.bfloat16
f32 = jnp.float32


def matmul(left, right):
    return jnp.dot(left, right, preferred_element_type=jnp.float32)


def contract(left, right, left_dim, right_dim):
    return lax.dot_general(
        left, right, (((left_dim,), (right_dim,)), ((), ())), preferred_element_type=jnp.float32
    )


def vmem_call(body, outs, operands, scalars=(), scratch=(), name=None, flops=1000000000):
    specs = [
        one[1] if isinstance(one, tuple) else pl.BlockSpec(memory_space=pltpu.VMEM) for one in operands
    ]
    operands = [one[0] if isinstance(one, tuple) else one for one in operands]
    return pl.pallas_call(
        body,
        in_specs=[pl.BlockSpec(memory_space=pltpu.SMEM)] * len(scalars) + specs,
        out_specs=[pl.BlockSpec(memory_space=pltpu.VMEM)] * len(outs),
        out_shape=[jax.ShapeDtypeStruct(shape, dtype) for shape, dtype in outs],
        scratch_shapes=list(scratch),
        compiler_params=pltpu.CompilerParams(vmem_limit_bytes=VMEM),
        cost_estimate=pl.CostEstimate(flops=flops, bytes_accessed=8000000, transcendentals=0),
        name=name,
    )(*scalars, *operands)


def inverse_root(hidden):
    return lax.rsqrt(jnp.mean(hidden * hidden, axis=-1, keepdims=True) + norm_epsilon)


def norm_pull(hidden, gain, cotangent):
    scale = inverse_root(hidden)
    weighted = cotangent * gain
    inner = jnp.mean(hidden * weighted, axis=-1, keepdims=True)
    hidden_grad = scale * weighted - hidden * (scale * scale * scale * inner)
    return hidden_grad, jnp.sum(cotangent * hidden * scale, axis=0, keepdims=True)


def self_pieces(pair, group, wide_ref):
    rows = slice(pair * TGT, (pair + 1) * TGT)
    start = group * 2 * HEAD
    queries = jnp.concatenate(
        [wide_ref[rows, start : start + HEAD], wide_ref[rows, start + HEAD : start + 2 * HEAD]],
        axis=0,
    )
    start = D + group * HEAD
    return (
        queries,
        wide_ref[rows, start : start + HEAD],
        wide_ref[rows, start + KEYS : start + KEYS + HEAD],
    )


def self_scores(queries, keys, bias, length):
    raw = contract(keys, queries, 1, 1) * HEAD ** (-0.5) + bias
    key = lax.broadcasted_iota(jnp.int32, (TGT, 2 * TGT), 0)
    query = lax.broadcasted_iota(jnp.int32, (TGT, 2 * TGT), 1) % TGT
    return jnp.where((key <= query) & (key < length), raw, masked_value)


def self_bias(small_ref, lane_ref, group):
    lanes = lane_ref[...]
    source = jnp.broadcast_to(small_ref[3:4, group * TGT : (group + 1) * TGT], (TGT, TGT))
    return jnp.concatenate(
        [jnp.take_along_axis(source, lanes + head * HEAD, axis=1) for head in range(2)], axis=1
    )


def self_forward_kernel(sizes, share, me_ref, length_ref, row_ref, lane_ref, *refs):
    pieces, refs = refs[:-7], refs[-7:]
    norm_ref, wide_ref, mix_ref, stat_ref, small_ref, weight_ref, sems = refs
    inputs = row_ref[...].astype(f32)
    place_pieces(sizes, share, me_ref, pieces, 0, weight_ref, sems)
    small = weight_ref[:, D + 2 * KEYS :].astype(f32).T
    small_ref[...] = small[:8]
    normed = (inputs * inverse_root(inputs) * small[0:1, :]).astype(bf16)
    norm_ref[...] = normed
    wide_ref[...] = matmul(normed, weight_ref[:, : D + 2 * KEYS]).astype(bf16)
    for group in range(GROUPS):
        bias = self_bias(small_ref, lane_ref, group)
        for pair in range(row_ref.shape[0] // TGT):
            queries, keys, values = self_pieces(pair, group, wide_ref)
            scores = self_scores(queries, keys, bias, length_ref[pair])
            highest = jnp.max(scores, axis=0, keepdims=True)
            weights = jnp.exp(scores - highest)
            totals = jnp.sum(weights, axis=0, keepdims=True)
            probs = (weights * (1.0 / totals)).astype(bf16)
            mixed = contract(probs, values, 0, 0).astype(bf16)
            start = group * 2 * HEAD
            mix_ref[pair * TGT : (pair + 1) * TGT, start : start + 2 * HEAD] = jnp.concatenate(
                [mixed[:TGT], mixed[TGT:]], axis=1
            )
            logsum = highest + jnp.log(totals)
            at = pair * HEADS + 2 * group
            stat_ref[at : at + 1, :] = logsum[:, :TGT]
            stat_ref[at + 1 : at + 2, :] = logsum[:, TGT:]


ANYWHERE = pl.BlockSpec(memory_space=pl.ANY)


def self_forward(sizes, share, me, lengths, rows, lanes, pieces):
    count = rows.shape[0]
    return vmem_call(
        functools.partial(self_forward_kernel, sizes, share),
        [
            ((count, D), bf16),
            ((count, D + 2 * KEYS), bf16),
            ((count, D), bf16),
            ((count // TGT * HEADS, TGT), f32),
            ((8, D), f32),
        ],
        [rows, lanes] + [(piece, ANYWHERE) for piece in pieces],
        [me, lengths],
        [pltpu.VMEM((D, D + 2 * KEYS + SMALL), bf16), pltpu.SemaphoreType.DMA((sizes[0] * sizes[1],))],
        name="self_forward",
    )


def self_output_kernel(sizes, share, me_ref, row_ref, mix_ref, small_ref, *refs):
    pieces, refs = refs[:-6], refs[-6:]
    hidden_ref, norm_ref, query_ref, square_ref, weight_ref, sems = refs
    place_pieces(sizes, share, me_ref, pieces, D + 2 * KEYS + SMALL, weight_ref, sems)
    branch = matmul(mix_ref[...], weight_ref[:, :D])
    square_ref[...] = jnp.sum(branch * branch, axis=1, keepdims=True)
    hidden = row_ref[...].astype(f32) + branch
    hidden_ref[...] = hidden
    normed = (hidden * inverse_root(hidden) * small_ref[1:2, :]).astype(bf16)
    norm_ref[...] = normed
    queries = matmul(normed, weight_ref[:, D:]).astype(bf16) * bf16(HEAD ** (-0.5))
    query_ref[...] = queries.T


def self_output_part(sizes, share, me, rows, mixed, small, pieces):
    count = rows.shape[0]
    return vmem_call(
        functools.partial(self_output_kernel, sizes, share),
        [((count, D), f32), ((count, D), bf16), ((D, count), bf16), ((count, 1), f32)],
        [rows, mixed, small] + [(piece, ANYWHERE) for piece in pieces],
        [me],
        [pltpu.VMEM((D, 2 * D), bf16), pltpu.SemaphoreType.DMA((sizes[0] * sizes[1],))],
        name="self_output",
    )


def cross_join_kernel(
    hidden_ref, gain_ref, weight_ref, *refs
):
    parts, (mix_ref, stat_ref, out_ref, norm_ref, square_ref) = refs[:-5], refs[-5:]
    logs = [join_terms(part[D : D + 3 * HEADS, :]) for part in parts]
    highest = functools.reduce(jnp.maximum, logs)
    weights = [jnp.exp(log - highest) for log in logs]
    totals = functools.reduce(jnp.add, weights)
    stat_ref[...] = highest + jnp.log(totals)
    weights = [weight * (1.0 / totals) for weight in weights]
    for head in range(HEADS):
        at = slice(head * HEAD, (head + 1) * HEAD)
        mix_ref[at, :] = functools.reduce(
            jnp.add,
            [
                part[at, :].astype(f32) * weight[head : head + 1, :]
                for part, weight in zip(parts, weights, strict=True)
            ],
        )
    branch = contract(mix_ref[...].astype(bf16), weight_ref[...], 0, 0)
    square_ref[...] = jnp.sum(branch * branch, axis=1, keepdims=True)
    hidden = hidden_ref[...] + branch
    out_ref[...] = hidden
    norm_ref[...] = (hidden * inverse_root(hidden) * gain_ref[2:3, :]).astype(bf16)


def cross_join(hidden, gains, weights, parts):
    count = hidden.shape[0]
    return vmem_call(
        cross_join_kernel,
        [
            ((D, count), f32),
            ((HEADS, count), f32),
            ((count, D), f32),
            ((count, D), bf16),
            ((count, 1), f32),
        ],
        [hidden, gains, weights, *parts],
        name="cross_join",
    )


def ffn_join_kernel(cotangent_ref, hidden_ref, gain_ref, weight_ref, mix_ref, stat_ref, *refs):
    parts, (grad_ref, low_ref, pack_ref, gain_grad_ref) = refs[:-4], refs[-4:]
    norm_grad = functools.reduce(jnp.add, [part[...].astype(f32) for part in parts])
    back, gain_grad_ref[...] = norm_pull(hidden_ref[...], gain_ref[2:3, :], norm_grad)
    grad = cotangent_ref[...].astype(f32) + back
    grad_ref[...] = grad
    low = grad.astype(bf16)
    low_ref[...] = low
    mixed_grad = contract(weight_ref[...], low, 1, 1).astype(bf16)
    pack_ref[:D, :] = mixed_grad
    product = mixed_grad.astype(f32) * mix_ref[...]
    inner = jnp.concatenate(
        [
            jnp.sum(product[head * HEAD : (head + 1) * HEAD], axis=0, keepdims=True)
            for head in range(HEADS)
        ],
        axis=0,
    )
    for place, term in enumerate(split_terms(stat_ref[...]) + split_terms(inner)):
        pack_ref[D + place * HEADS : D + (place + 1) * HEADS, :] = term


def ffn_join(cotangent, hidden, gains, weights, mixed, stats, parts):
    count = hidden.shape[0]
    return vmem_call(
        ffn_join_kernel,
        [((count, D), f32), ((count, D), bf16), ((D + 6 * HEADS, count), bf16), ((1, D), f32)],
        [cotangent, hidden, gains, weights, mixed, stats, *parts],
        name="ffn_join",
    )


def query_join_kernel(grad_ref, hidden_ref, gain_ref, weight_ref, *refs):
    parts, (sum_ref, out_ref, low_ref, mix_grad_ref, gain_grad_ref) = refs[:-5], refs[-5:]
    queries = functools.reduce(jnp.add, [part[...].astype(f32) for part in parts]).astype(bf16)
    sum_ref[...] = queries
    norm_grad = contract(queries, weight_ref[:, D:], 0, 1)
    back, gain_grad_ref[...] = norm_pull(hidden_ref[...], gain_ref[1:2, :], norm_grad)
    grad = grad_ref[...] + back
    out_ref[...] = grad
    low = grad.astype(bf16)
    low_ref[...] = low
    mix_grad_ref[...] = contract(low, weight_ref[:, :D], 1, 1).astype(bf16)


def query_join(grad, hidden, gains, weights, parts):
    count = hidden.shape[0]
    return vmem_call(
        query_join_kernel,
        [
            ((D, count), bf16),
            ((count, D), f32),
            ((count, D), bf16),
            ((count, D), bf16),
            ((1, D), f32),
        ],
        [grad, hidden, gains, weights, *parts],
        name="query_join",
    )


def self_backward_kernel(
    length_ref,
    mix_grad_ref,
    wide_ref,
    stat_ref,
    small_ref,
    lane_ref,
    bucket_ref,
    wide_grad_ref,
    table_grad_ref,
    score_ref,
):
    pairs = mix_grad_ref.shape[0] // TGT
    for group in range(GROUPS):
        bias = self_bias(small_ref, lane_ref, group)
        score_total = None
        for pair in range(pairs):
            queries, keys, values = self_pieces(pair, group, wide_ref)
            rows = slice(pair * TGT, (pair + 1) * TGT)
            start = group * 2 * HEAD
            mixed_grad = jnp.concatenate(
                [
                    mix_grad_ref[rows, start : start + HEAD],
                    mix_grad_ref[rows, start + HEAD : start + 2 * HEAD],
                ],
                axis=0,
            )
            at = pair * HEADS + 2 * group
            logsum = jnp.concatenate([stat_ref[at : at + 1, :], stat_ref[at + 1 : at + 2, :]], axis=1)
            scores = self_scores(queries, keys, bias, length_ref[pair])
            probs = jnp.exp(scores - logsum)
            prob_grad = contract(values, mixed_grad, 1, 1)
            inner = jnp.sum(probs * prob_grad, axis=0, keepdims=True)
            score_grad = (probs * (prob_grad - inner)).astype(bf16)
            value_grad = matmul(probs.astype(bf16), mixed_grad).astype(bf16)
            key_grad = (matmul(score_grad, queries) * HEAD ** (-0.5)).astype(bf16)
            query_grad = (contract(score_grad, keys, 0, 0) * HEAD ** (-0.5)).astype(bf16)
            wide_grad_ref[rows, start : start + 2 * HEAD] = jnp.concatenate(
                [query_grad[:TGT], query_grad[TGT:]], axis=1
            )
            start = D + group * HEAD
            wide_grad_ref[rows, start : start + HEAD] = key_grad
            wide_grad_ref[rows, start + KEYS : start + KEYS + HEAD] = value_grad
            wide = score_grad.astype(f32)
            score_total = wide if score_total is None else score_total + wide
        score_ref[2 * group] = score_total[:, :TGT]
        score_ref[2 * group + 1] = score_total[:, TGT:]
    buckets = bucket_ref[...]
    lane = lax.broadcasted_iota(jnp.int32, (HEADS, TGT), 1)

    def one_bucket(bucket, table_grad):
        inside = buckets == bucket
        sums = jnp.concatenate(
            [
                jnp.sum(jnp.where(inside, score_ref[head], 0.0), axis=0, keepdims=True)
                for head in range(HEADS)
            ],
            axis=0,
        )
        return jnp.where(lane == bucket, jnp.sum(sums, axis=1, keepdims=True), table_grad)

    table_grad_ref[...] = lax.fori_loop(0, BUCKETS, one_bucket, jnp.zeros((HEADS, TGT), f32))


def self_backward(lengths, mix_grad, wide, stats, small, lanes, buckets):
    return vmem_call(
        self_backward_kernel,
        [(wide.shape, bf16), ((HEADS, TGT), f32)],
        [mix_grad, wide, stats, small, lanes, buckets],
        [lengths],
        [pltpu.VMEM((HEADS, TGT, TGT), f32)],
        name="self_backward",
        flops=8000000000,
    )


def input_grads_kernel(wide_grad_ref, weight_ref, gain_ref, row_ref, grad_ref, out_ref, gain_grad_ref):
    norm_grad = contract(wide_grad_ref[...], weight_ref[...], 1, 1)
    back, gain_grad_ref[...] = norm_pull(row_ref[...].astype(f32), gain_ref[0:1, :], norm_grad)
    out_ref[...] = (grad_ref[...] + back).astype(bf16)


def input_grads(wide_grad, weights, gains, rows, grad):
    return vmem_call(
        input_grads_kernel,
        [(rows.shape, bf16), ((1, D), f32)],
        [wide_grad, weights, gains, rows, grad],
        name="input_grads",
    )


def split_terms(value):
    high = value.astype(bf16)
    rest = value - high.astype(f32)
    middle = rest.astype(bf16)
    low = (rest - middle.astype(f32)).astype(bf16)
    return [high, middle, low]


def join_terms(block):
    return (
        block[:HEADS].astype(f32)
        + block[HEADS : 2 * HEADS].astype(f32)
        + block[2 * HEADS : 3 * HEADS].astype(f32)
    )


def both_heads(ref, group):
    start = group * 2 * HEAD
    return jnp.concatenate(
        [ref[start : start + HEAD, :], ref[start + HEAD : start + 2 * HEAD, :]], axis=1
    )


def both_rows(stat, group):
    return jnp.concatenate([stat[2 * group : 2 * group + 1], stat[2 * group + 1 : 2 * group + 2]], axis=1)


def valid_positions(info_ref, chunk, pair, positions):
    held = positions // 2
    length = info_ref[chunk, 3 + pair]
    place = lax.broadcasted_iota(jnp.int32, (positions, 2 * TGT), 0)
    limit = jnp.where(
        place < held, length - info_ref[chunk, 1], held + length - info_ref[chunk, 2]
    )
    return place < limit


def cross_forward_kernel(chunk, info_ref, query_ref, memory_ref, mix_ref, stat_ref):
    pair = pl.program_id(0)
    mask = valid_positions(info_ref, chunk, pair, memory_ref.shape[1])
    for group in range(GROUPS):
        keys = memory_ref[0, :, group * HEAD : (group + 1) * HEAD]
        values = memory_ref[0, :, KEYS + group * HEAD : KEYS + (group + 1) * HEAD]
        scores = jnp.where(mask, matmul(keys, both_heads(query_ref, group)), masked_value)
        highest = jnp.max(scores, axis=0, keepdims=True)
        weights = jnp.exp(scores - highest)
        totals = jnp.sum(weights, axis=0, keepdims=True)
        mixed = contract(weights.astype(bf16), values, 0, 0).T * (1.0 / totals)
        mixed = mixed.astype(bf16)
        start = group * 2 * HEAD
        mix_ref[start : start + HEAD, :] = mixed[:, :TGT]
        mix_ref[start + HEAD : start + 2 * HEAD, :] = mixed[:, TGT:]
        logsum = highest + jnp.log(totals)
        stat_ref[2 * group : 2 * group + 1, :] = logsum[:, :TGT]
        stat_ref[2 * group + 1 : 2 * group + 2, :] = logsum[:, TGT:]
    for place, term in enumerate(split_terms(stat_ref[...])):
        mix_ref[D + place * HEADS : D + (place + 1) * HEADS, :] = term


def cross_forward(chunk, info, queries, memory_parts):
    positions, wide = memory_parts.shape[1], memory_parts.shape[2]
    rows = queries.shape[1]
    return pl.pallas_call(
        functools.partial(cross_forward_kernel, chunk),
        grid_spec=pltpu.PrefetchScalarGridSpec(
            num_scalar_prefetch=1,
            grid=(rows // TGT,),
            in_specs=[
                pl.BlockSpec((D, TGT), lambda pair, info: (0, pair)),
                pl.BlockSpec((1, positions, wide), lambda pair, info: (info[chunk, 0] + pair, 0, 0)),
            ],
            out_specs=pl.BlockSpec((D + 3 * HEADS, TGT), lambda pair, info: (0, pair)),
            scratch_shapes=[pltpu.VMEM((HEADS, TGT), f32)],
        ),
        out_shape=jax.ShapeDtypeStruct((D + 3 * HEADS, rows), bf16),
        compiler_params=pltpu.CompilerParams(vmem_limit_bytes=VMEM),
        cost_estimate=pl.CostEstimate(flops=6000000000, bytes_accessed=4000000, transcendentals=0),
        name="cross_forward",
    )(info, queries, memory_parts)


def cross_backward_kernel(chunk, info_ref, query_ref, grad_ref, memory_ref, *rest):
    query_grad_ref, memory_grad_ref = rest[-2:]
    pair = pl.program_id(0)
    mask = valid_positions(info_ref, chunk, pair, memory_ref.shape[1])
    logsum = join_terms(grad_ref[D : D + 3 * HEADS, :])
    inner = join_terms(grad_ref[D + 3 * HEADS : D + 6 * HEADS, :])
    for tile in range(GROUPS // 2):
        key_parts, value_parts = [], []
        for group in (2 * tile, 2 * tile + 1):
            keys = memory_ref[0, :, group * HEAD : (group + 1) * HEAD]
            values = memory_ref[0, :, KEYS + group * HEAD : KEYS + (group + 1) * HEAD]
            queries = both_heads(query_ref, group)
            mixed_grad = both_heads(grad_ref, group)
            scores = matmul(keys, queries) - both_rows(logsum, group)
            probs = jnp.exp(jnp.where(mask, scores, masked_value))
            prob_grad = matmul(values, mixed_grad) - both_rows(inner, group)
            score_grad = (probs * prob_grad).astype(bf16)
            value_parts.append(contract(probs.astype(bf16), mixed_grad, 1, 1).astype(bf16))
            key_parts.append(contract(score_grad, queries, 1, 1).astype(bf16))
            query_grad = (contract(keys, score_grad, 0, 0) * HEAD ** (-0.5)).astype(bf16)
            start = group * 2 * HEAD
            query_grad_ref[start : start + HEAD, :] = query_grad[:, :TGT]
            query_grad_ref[start + HEAD : start + 2 * HEAD, :] = query_grad[:, TGT:]
        columns = 2 * HEAD * tile
        memory_grad_ref[0, :, columns : columns + 2 * HEAD] = jnp.concatenate(key_parts, axis=1)
        memory_grad_ref[0, :, KEYS + columns : KEYS + columns + 2 * HEAD] = jnp.concatenate(
            value_parts, axis=1
        )


def cross_backward(chunk, info, queries, grads, memory_parts, *earlier):
    positions, wide = memory_parts.shape[1], memory_parts.shape[2]
    rows = queries.shape[1]
    place = pl.BlockSpec((1, positions, wide), lambda pair, info: (info[chunk, 0] + pair, 0, 0))
    return pl.pallas_call(
        functools.partial(cross_backward_kernel, chunk),
        grid_spec=pltpu.PrefetchScalarGridSpec(
            num_scalar_prefetch=1,
            grid=(rows // TGT,),
            in_specs=[
                pl.BlockSpec((D, TGT), lambda pair, info: (0, pair)),
                pl.BlockSpec((D + 6 * HEADS, TGT), lambda pair, info: (0, pair)),
                place,
            ]
            + [pl.BlockSpec(memory_space=pl.ANY)] * len(earlier),
            out_specs=[pl.BlockSpec((D, TGT), lambda pair, info: (0, pair)), place],
        ),
        out_shape=[
            jax.ShapeDtypeStruct((D, rows), bf16),
            jax.ShapeDtypeStruct(memory_parts.shape, bf16),
        ],
        input_output_aliases={4: 1} if earlier else {},
        compiler_params=pltpu.CompilerParams(vmem_limit_bytes=VMEM),
        cost_estimate=pl.CostEstimate(flops=10000000000, bytes_accessed=8000000, transcendentals=0),
        name="cross_backward",
    )(info, queries, grads, memory_parts, *earlier)


def ffn_kernel(me_ref, row_ref, cotangent_ref, gate_ref, up_ref, down_ref, *rest):
    row_grad_ref, branch_ref, rows_ref, kept_cotangent_ref, hidden_ref, gate_grad_ref, up_grad_ref = rest[
        -7:
    ]
    rows = row_ref[...]
    rows_ref[0] = rows
    gate = matmul(rows, gate_ref[...])
    up = matmul(rows, up_ref[...])
    cotangent = cotangent_ref[0]
    kept_cotangent_ref[0] = cotangent
    hidden_grad = contract(cotangent, down_ref[...], 1, 1)
    square = gate * gate
    slope = 0.7978845608028654
    bend = jnp.tanh(slope * gate * (1.0 + 0.044715 * square))
    half = 0.5 * (1.0 + bend)
    value = gate * half
    derivative = half + 0.5 * gate * (1.0 - bend * bend) * slope * (1.0 + 3 * 0.044715 * square)
    hidden = (value * up).astype(bf16)
    gate_grad = (hidden_grad * up * derivative).astype(bf16)
    up_grad = (hidden_grad * value).astype(bf16)
    row_grad = contract(gate_grad, gate_ref[...], 1, 1) + contract(up_grad, up_ref[...], 1, 1)
    row_grad_ref[...] = row_grad.astype(bf16)
    branch_ref[0] = matmul(hidden, down_ref[...]).astype(bf16)
    hidden_ref[0] = hidden
    gate_grad_ref[0] = gate_grad
    up_grad_ref[0] = up_grad


def ffn_chunk(chunk, chunks, me, rows, cotangent, gate, up, down, *earlier):
    count, width = rows.shape
    wide = gate.shape[1]
    kept = [width, width, width, wide, wide, wide]
    by_line = pl.BlockSpec((1, count, width), lambda step, me: (me[1] ^ chunk, 0, 0))

    def whole(array):
        return pl.BlockSpec(array.shape, lambda step, me: (0, 0))

    return pl.pallas_call(
        ffn_kernel,
        grid_spec=pltpu.PrefetchScalarGridSpec(
            num_scalar_prefetch=1,
            grid=(1,),
            in_specs=[whole(rows), by_line]
            + [whole(array) for array in (gate, up, down)]
            + [ANYWHERE] * len(earlier),
            out_specs=[whole(rows), by_line]
            + [pl.BlockSpec((1, count, size), lambda step, me: (chunk, 0, 0)) for size in kept[1:]],
        ),
        out_shape=[jax.ShapeDtypeStruct((count, width), bf16)]
        + [jax.ShapeDtypeStruct((chunks, count, size), bf16) for size in kept],
        input_output_aliases={6 + place: 1 + place for place in range(len(earlier))},
        compiler_params=pltpu.CompilerParams(vmem_limit_bytes=VMEM),
        cost_estimate=pl.CostEstimate(flops=3000000000, bytes_accessed=8000000, transcendentals=0),
        name="ffn_chunk",
    )(me, rows, cotangent, gate, up, down, *earlier)


def exchange(value, axis, size, mask):
    return lax.ppermute(value, axis, [(place, place ^ mask) for place in range(size)])


def visit_chunks(value, size, work):
    lines = size // 2

    def by_lines(array, pairs):
        pairs = [(2 * old + core, 2 * new + core) for old, new in pairs for core in range(2)]
        return lax.ppermute(array, "ffn", pairs)

    if lines != 4:
        chunks = [value] + [exchange(value, "ffn", size, 2 * step) for step in range(1, lines)]
        return [work(chunk, one) for chunk, one in enumerate(chunks)]
    across = exchange(value, "ffn", size, 4)
    beside = exchange(value, "ffn", size, 2)
    middle = by_lines(value, [(1, 2), (2, 1)])
    results = [work(0, value)]
    across = after(across, results[0])
    onward = by_lines(across, [(2, 3), (1, 0)])
    results.append(work(1, after(beside, across)))
    results.append(work(2, across))
    line = lax.axis_index("ffn") // 2
    results.append(work(3, jnp.where((line == 0) | (line == 3), onward, middle)))
    return results


def return_chunks(parts, size):
    return [parts[0]] + [
        exchange(parts[step], "ffn", size, 2 * step) for step in range(1, size // 2)
    ]


def reduce_rows(grads, tok_size, ffn_size):
    columns = grads.shape[1]
    me_ffn, me_tok = lax.axis_index("ffn"), lax.axis_index("tok")

    def halves(value, dim, bit):
        first = lax.index_in_dim(value, 0, dim, keepdims=False)
        second = lax.index_in_dim(value, 1, dim, keepdims=False)
        return jnp.where(bit == 0, first, second), jnp.where(bit == 0, second, first)

    rows = grads.shape[0] // (tok_size * ffn_size)
    value = grads.reshape(tok_size, ffn_size // 2, 2, rows, columns)
    kept, sent = halves(value, 2, me_ffn & 1)
    value = kept.astype(f32) + exchange(sent.astype(bf16), "ffn", ffn_size, 1).astype(f32)

    bits = tok_size.bit_length() - 1
    value = value.reshape((2,) * bits + (ffn_size // 2, rows, columns))
    half = columns // 2 // 128 * 128
    sides = []
    for part, order in (
        (value[..., :half], list(range(bits))),
        (value[..., half:], list(range(bits))[::-1]),
    ):
        left = list(range(bits))
        for bit in order:
            dim = left.index(bit)
            left.remove(bit)
            weight = 1 << (bits - 1 - bit)
            kept, sent = halves(part, dim, (me_tok // weight) & 1)
            part = kept.astype(f32) + exchange(sent.astype(bf16), "tok", tok_size, weight).astype(f32)
        sides.append(part)
    value = jnp.concatenate(sides, axis=-1)
    line = me_ffn // 2
    total = lax.dynamic_index_in_dim(value, line, 0, keepdims=False)
    low = value.astype(bf16)
    for step in range(1, ffn_size // 2):
        part = lax.dynamic_index_in_dim(low, line ^ step, 0, keepdims=False)
        total = total + exchange(part, "ffn", ffn_size, 2 * step).astype(f32)
    return total


def memory_forward_kernel(me_ref, own_ref, other_ref, weight_ref, out_ref):
    pairs, held, width = other_ref.shape
    for place, rows in enumerate((own_ref[0, 0], other_ref[...])):
        part = matmul(rows.reshape(pairs * held, width), weight_ref[...]).astype(bf16)
        out_ref[:, place] = part.reshape(pairs, held, part.shape[1])


def own_pairs(memory):
    unused, also, step, held, width = memory.shape
    return pl.BlockSpec((1, 1, step, held, width), lambda line, me: (line, me[2], 0, 0, 0))


def memory_forward(me, memory, other, weights):
    lines, unused, step, held, width = memory.shape
    return pl.pallas_call(
        memory_forward_kernel,
        grid_spec=pltpu.PrefetchScalarGridSpec(
            num_scalar_prefetch=1,
            grid=(lines,),
            in_specs=[
                own_pairs(memory),
                pl.BlockSpec((step, held, width), lambda line, me: (line, 0, 0)),
                pl.BlockSpec((width, 2 * KEYS), lambda line, me: (0, 0)),
            ],
            out_specs=pl.BlockSpec((step, 2, held, 2 * KEYS), lambda line, me: (line, 0, 0, 0)),
        ),
        out_shape=jax.ShapeDtypeStruct((lines * step, 2, held, 2 * KEYS), bf16),
        compiler_params=pltpu.CompilerParams(vmem_limit_bytes=VMEM),
        cost_estimate=pl.CostEstimate(flops=8600000000, bytes_accessed=18000000, transcendentals=0),
        name="memory_forward",
    )(me, memory, other, weights)


def memory_backward_kernel(
    sizes, me_ref, own_ref, other_ref, grad_ref, weight_ref, mix_ref, low_ref, *rest
):
    own_grad_ref, other_grad_ref, kept_ref, sent_ref, total = rest
    step = pl.program_id(0)
    pairs, held, width = other_ref.shape
    for place, (rows, out_ref) in enumerate(
        ((own_ref[0, 0], own_grad_ref), (other_ref[...], other_grad_ref))
    ):
        grads = grad_ref[:, place].reshape(pairs * held, grad_ref.shape[3])
        out = contract(grads, weight_ref[...], 1, 1).astype(bf16)
        out_ref[...] = out.reshape(out_ref.shape)
        part = contract(rows.reshape(pairs * held, width), grads, 0, 0)
        if place == 0:
            total[...] = jnp.where(step == 0, part, total[...] + part)
        else:
            total[...] += part

    @pl.when(step == 0)
    def first():
        low = low_ref[...]
        for start in range(0, low.shape[1], 512):
            part = matmul(mix_ref[...].astype(bf16), low[:, start : start + 512])
            store_blocks(sizes, me_ref, kept_ref, sent_ref, 2 * KEYS + start, part)

    @pl.when(step == pl.num_programs(0) - 1)
    def last():
        store_blocks(sizes, me_ref, kept_ref, sent_ref, 0, total[...])


def memory_backward(sizes, me, memory, other, grads, weights, mixed, low):
    lines, unused, step, held, width = memory.shape
    block = pl.BlockSpec((step, held, width), lambda line, me: (line, 0, 0))
    shape = blocks_shape(sizes, 2 * KEYS + low.shape[1])
    return pl.pallas_call(
        functools.partial(memory_backward_kernel, sizes),
        grid_spec=pltpu.PrefetchScalarGridSpec(
            num_scalar_prefetch=1,
            grid=(lines,),
            in_specs=[
                own_pairs(memory),
                block,
                pl.BlockSpec((step, 2, held, 2 * KEYS), lambda line, me: (line, 0, 0, 0)),
                pl.BlockSpec((width, 2 * KEYS), lambda line, me: (0, 0)),
                pl.BlockSpec(mixed.shape, lambda line, me: (0, 0)),
                pl.BlockSpec(low.shape, lambda line, me: (0, 0)),
            ],
            out_specs=[
                own_pairs(memory),
                block,
            ]
            + [pl.BlockSpec(shape, lambda line, me: (0,) * len(shape))] * 2,
            scratch_shapes=[pltpu.VMEM((width, 2 * KEYS), f32)],
        ),
        out_shape=[
            jax.ShapeDtypeStruct(memory.shape, bf16),
            jax.ShapeDtypeStruct(other.shape, bf16),
            jax.ShapeDtypeStruct(shape, bf16),
            jax.ShapeDtypeStruct(shape, bf16),
        ],
        compiler_params=pltpu.CompilerParams(vmem_limit_bytes=VMEM),
        cost_estimate=pl.CostEstimate(flops=17200000000, bytes_accessed=28000000, transcendentals=0),
        name="memory_backward",
    )(me, memory, other, grads, weights, mixed, low)


def place_pairs_kernel(me_ref, pair_ref, unused_ref, out_ref):
    out_ref[0, 0] = pair_ref[...]


def place_pairs(me, whole, pairs):
    lines, unused, step, held, width = whole.shape
    return pl.pallas_call(
        place_pairs_kernel,
        grid_spec=pltpu.PrefetchScalarGridSpec(
            num_scalar_prefetch=1,
            grid=(lines,),
            in_specs=[
                pl.BlockSpec((step, held, width), lambda line, me: (line, 0, 0)),
                pl.BlockSpec(memory_space=pl.ANY),
            ],
            out_specs=pl.BlockSpec(
                (1, 1, step, held, width), lambda line, me: (line, 1 - me[2], 0, 0, 0)
            ),
        ),
        out_shape=jax.ShapeDtypeStruct(whole.shape, bf16),
        input_output_aliases={2: 0},
        compiler_params=pltpu.CompilerParams(vmem_limit_bytes=VMEM),
        name="place_pairs",
    )(me, pairs, whole)


def blocks_shape(sizes, columns):
    tok_size, ffn_size = sizes
    return (tok_size * ffn_size // 2, D // (tok_size * ffn_size), columns)


def store_blocks(sizes, me_ref, kept_ref, sent_ref, column, value):
    tok_size, ffn_size = sizes
    rows = D // (tok_size * ffn_size)
    low = value.astype(bf16)
    columns = slice(column, column + value.shape[1])
    for block in range(0, tok_size * ffn_size, 2):
        tok, line = block // ffn_size, block % ffn_size // 2
        place = (tok ^ me_ref[0]) * (ffn_size // 2) + (line ^ me_ref[1])
        first = low[block * rows : (block + 1) * rows]
        second = low[(block + 1) * rows : (block + 2) * rows]
        kept_ref[place, :, columns] = jnp.where(me_ref[2] == 0, first, second)
        sent_ref[place, :, columns] = jnp.where(me_ref[2] == 0, second, first)


def grad_blocks_kernel(sizes, dims, me_ref, *refs):
    kept_ref, sent_ref = refs[-2:]
    column = 0
    for place, (left_dim, right_dim) in enumerate(dims):
        left, right = refs[2 * place], refs[2 * place + 1]
        for start in range(0, right.shape[1 - right_dim], 512):
            if right_dim == 0:
                part = right[:, start : start + 512]
            else:
                part = right[start : start + 512, :]
            product = contract(left[...], part, left_dim, right_dim)
            store_blocks(sizes, me_ref, kept_ref, sent_ref, column, product)
            column += 512
    extra = refs[2 * len(dims) : -2]
    if len(extra) == 2:
        kept_ref[:, :, column:] = extra[0][...]
        sent_ref[:, :, column:] = extra[1][...]
    elif extra:
        rows = extra[0][...]
        filled = jnp.concatenate([rows, jnp.zeros((SMALL - rows.shape[0], D), f32)], axis=0)
        store_blocks(sizes, me_ref, kept_ref, sent_ref, column, filled.T)


def grad_blocks(sizes, me, products, *extra):
    operands = [array for left, right, unused, also in products for array in (left, right)]
    columns = sum(right.shape[1 - dim] for unused, right, also, dim in products)
    operands += extra
    if extra:
        columns += extra[0].shape[2] if extra[0].ndim == 3 else SMALL
    return pl.pallas_call(
        functools.partial(grad_blocks_kernel, sizes, [(one[2], one[3]) for one in products]),
        in_specs=[pl.BlockSpec(memory_space=pltpu.SMEM)]
        + [pl.BlockSpec(memory_space=pltpu.VMEM)] * len(operands),
        out_specs=[pl.BlockSpec(memory_space=pltpu.VMEM)] * 2,
        out_shape=[jax.ShapeDtypeStruct(blocks_shape(sizes, columns), bf16)] * 2,
        compiler_params=pltpu.CompilerParams(vmem_limit_bytes=VMEM),
        name="grad_blocks",
    )(me, *operands)


def plus(*parts):
    return functools.reduce(jnp.add, [part.astype(f32) for part in parts]).astype(bf16)


def reduce_core(sizes, blocks, earlier=()):
    lines = sizes[1] // 2
    kept, sent = blocks
    other = after(exchange(sent, "ffn", sizes[1], 1), earlier)
    return [
        plus(kept[tok * lines : (tok + 1) * lines], other[tok * lines : (tok + 1) * lines])
        for tok in range(4)
    ]


def reduce_corner(sizes, parts, earlier=()):
    own, by_x, by_y, across = parts
    half = sizes[1] // 4
    top = exchange(across[:half], "tok", sizes[0], 1)
    bottom = exchange(across[half:], "tok", sizes[0], 2)
    top, bottom = after([top, bottom], earlier)
    by_x = jnp.concatenate([by_x[:half], plus(by_x[half:], bottom)], axis=0)
    by_y = jnp.concatenate([plus(by_y[:half], top), by_y[half:]], axis=0)
    return [own, by_x, by_y]


def reduce_sides(sizes, parts, earlier=()):
    own, by_x, by_y = parts
    arrived = [exchange(by_x, "tok", sizes[0], 1), exchange(by_y, "tok", sizes[0], 2)]
    return plus(own, *after(arrived, earlier))


def reduce_line(sizes, total, earlier=()):
    parts = [total[0]] + [
        exchange(total[step], "ffn", sizes[1], 2 * step) for step in range(1, sizes[1] // 2)
    ]
    parts = after(parts, earlier)
    return functools.reduce(jnp.add, [part.astype(f32) for part in parts])


def place_pieces(sizes, share, me_ref, pieces, column, target_ref, sems):
    columns = pl.ds(column, target_ref.shape[1])
    copies = []
    if len(pieces) == 1:
        copies.append(pltpu.make_async_copy(pieces[0].at[:, columns], target_ref, sems.at[0]))
    else:
        lines = sizes[1] // 2
        half = lines // 2
        for core in range(2):
            line_ref, x_ref, y_ref, top_ref, bottom_ref = pieces[5 * core : 5 * core + 5]
            for tok in range(4):
                for line in range(lines):
                    if tok < 3:
                        source = (line_ref, x_ref, y_ref)[tok].at[line]
                    else:
                        source = top_ref.at[line] if line < half else bottom_ref.at[line - half]
                    block = ((tok ^ me_ref[0]) * lines + (line ^ me_ref[1])) * 2 + (core ^ me_ref[2])
                    target = target_ref.at[pl.ds(pl.multiple_of(block * share, share), share), :]
                    copies.append(
                        pltpu.make_async_copy(source.at[:, columns], target, sems.at[len(copies)])
                    )
    for copy in copies:
        copy.start()
    for copy in copies:
        copy.wait()


def place_rows_kernel(sizes, share, starts, me_ref, *refs):
    pieces, outs, sems = refs[: -len(starts) - 1], refs[-len(starts) - 1 : -1], refs[-1]
    for column, out_ref in zip(starts, outs, strict=True):
        place_pieces(sizes, share, me_ref, pieces, column, out_ref, sems)


def place_rows(sizes, share, me, pieces, starts, columns):
    return vmem_call(
        functools.partial(place_rows_kernel, sizes, share, starts),
        [((sizes[0] * sizes[1] * share, columns), bf16) for unused in starts],
        [(piece, ANYWHERE) for piece in pieces],
        [me],
        [pltpu.SemaphoreType.DMA((sizes[0] * sizes[1],))],
        name="place_rows",
    )


def after(values, earlier):
    return lax.optimization_barrier((values, earlier))[0]


def gather_pieces(sizes, pack, beside):
    tok_size, ffn_size = sizes
    lines = ffn_size // 2
    half = lines // 2
    line = [pack] + [exchange(pack, "ffn", ffn_size, 2 * step) for step in range(1, lines)]
    line, extra = lax.optimization_barrier((line, beside(())))
    begun = line
    line = jnp.stack(line)
    by_x = exchange(line, "tok", tok_size, 1)
    by_y = exchange(line, "tok", tok_size, 2)
    top = exchange(by_y[:half], "tok", tok_size, 1)
    bottom = exchange(by_x[half:], "tok", tok_size, 2)
    held = [line, by_x, by_y, top, bottom]
    return held + [exchange(one, "ffn", ffn_size, 1) for one in held], extra, begun


def on_device(
    tok_size,
    ffn_size,
    targets,
    memory,
    out_grad,
    target_lengths,
    memory_lengths,
    buckets,
    rel_table,
    gain_self,
    gain_cross,
    gain_ffn,
    self_query,
    self_key,
    self_value,
    self_output,
    cross_query,
    cross_key,
    cross_value,
    cross_output,
    ffn_gate,
    ffn_up,
    ffn_down,
):
    pair_count = target_lengths.shape[0]
    row_count = targets.shape[0]
    held = memory.shape[1]
    devices = tok_size * ffn_size
    me_tok, me_ffn = lax.axis_index("tok"), lax.axis_index("ffn")
    share = self_query.shape[0]
    table_share = rel_table.shape[0]

    sizes = (tok_size, ffn_size)
    direct = tok_size == 4 and share % 16 == 0
    me = jnp.stack([me_tok, me_ffn // 2, me_ffn % 2]).astype(jnp.int32)
    per_row = [
        jnp.pad(part.astype(bf16), (0, share - part.shape[0]))
        for part in (gain_self, gain_cross, gain_ffn, rel_table, memory_lengths // 64, memory_lengths % 64)
    ]
    small = jnp.pad(jnp.stack(per_row, axis=1), ((0, 0), (0, SMALL - len(per_row))))

    core = me_ffn % 2
    lines = ffn_size // 2
    both = ("tok", "ffn")
    pack = jnp.concatenate(
        [self_query, self_key, self_value, small, self_output, cross_query, cross_key, cross_value],
        axis=1,
    )
    same_core = [[2 * line + one for line in range(lines)] for one in range(2)]
    memory_lines = memory.reshape(lines, 2, pair_count, held, D)

    def swap_memory(begun):
        sent = lax.dynamic_index_in_dim(after(memory_lines, begun), 1 - core, 1, keepdims=False)
        return exchange(sent.reshape(lines * pair_count, held, D), "ffn", ffn_size, 1)

    if direct:
        pieces, memory_other, begun = gather_pieces(sizes, pack, swap_memory)
    else:
        pieces = [lax.all_gather(pack, both, axis=0, tiled=True)]
        memory_other = swap_memory(pieces)
        begun = pieces
    cotangents = lax.all_gather(
        after(out_grad, begun),
        "ffn",
        axis=0,
        tiled=False,
        axis_index_groups=same_core,
    )

    per_table = BUCKETS * HEADS // devices
    buckets = buckets.T
    lanes_of = buckets // per_table * (2 * per_table) + buckets % per_table
    normed_one, self_wide, self_mixed, self_stats, small_rows = self_forward(
        sizes, share, me, target_lengths, targets, lanes_of, pieces
    )
    hidden_one, normed_two, cross_queries, self_squares = self_output_part(
        sizes, share, me, targets, self_mixed, small_rows, pieces
    )
    gains = small_rows[:3]
    lengths = (small_rows[4] * 64 + small_rows[5]).astype(jnp.int32)
    lengths = lengths.reshape(devices, share)[:, :pair_count]
    (memory_weights,) = place_rows(
        sizes, share, me, after(pieces, cross_queries), (3 * D + 2 * KEYS + SMALL,), 2 * KEYS
    )
    memory_parts = memory_forward(me, memory_lines, memory_other, memory_weights)
    memory_parts = memory_parts.reshape(-1, 2 * held, 2 * KEYS)
    lengths = lax.dynamic_index_in_dim(
        lengths.reshape(tok_size, ffn_size, pair_count), me_tok, 0, keepdims=False
    )
    owner = me_ffn ^ (2 * jnp.arange(lines))
    info = jnp.concatenate(
        [
            (owner // 2 * pair_count)[:, None],
            jnp.broadcast_to(me_ffn * held, (lines, 1)),
            jnp.broadcast_to((me_ffn ^ 1) * held, (lines, 1)),
            jnp.take(lengths, owner, axis=0),
        ],
        axis=1,
    ).astype(jnp.int32)


    position = jnp.arange(TGT)

    query_chunks, mixed_parts, kept = [], [], {}
    kept["output"] = lax.all_gather(
        after(cross_output, (self_mixed, cotangents)), both, axis=0, tiled=True
    )

    def visit_forward(chunk, chunk_queries):
        query_chunks.append(chunk_queries)
        if chunk:
            chunk_queries = after(chunk_queries, mixed_parts[-1])
        if chunk == lines - 1:
            chunk_queries = after(chunk_queries, (kept["placed"], kept["units"]))
        mixed_parts.append(cross_forward(chunk, info, chunk_queries, memory_parts))
        if chunk == 1:
            held_pieces, units = after((pieces, (ffn_gate, ffn_up, ffn_down)), mixed_parts[1])
            kept["placed"] = place_rows(
                sizes, share, me, held_pieces, (0, D + 2 * KEYS + SMALL), 2 * D
            )
            kept["units"] = [
                jnp.concatenate([array, exchange(array, "ffn", ffn_size, 1)], axis=dim)
                for array, dim in zip(units, (1, 1, 0), strict=True)
            ]
        return mixed_parts[-1]

    visit_chunks(cross_queries, ffn_size, visit_forward)
    output_weights = kept["output"]
    full_first, full_second = kept["placed"]
    both_gate, both_up, both_down = kept["units"]
    cross_mixed, cross_stats, hidden_two, normed_three, cross_squares = cross_join(
        hidden_one, gains, output_weights, return_chunks(mixed_parts, ffn_size)
    )

    earlier, row_parts = [], []

    def visit_ffn(chunk, rows):
        row_part, *earlier[:] = ffn_chunk(
            chunk, lines, me, rows, cotangents, both_gate, both_up, both_down, *earlier
        )
        row_parts.append(row_part)
        return row_part

    visit_chunks(normed_three, ffn_size, visit_ffn)
    row_parts = return_chunks(row_parts, ffn_size)
    branch_part, all_rows, all_cotangent, hidden, gate_grad, up_grad = [
        array.reshape(lines * row_count, array.shape[2]) for array in after(earlier, row_parts[1])
    ]
    units = ffn_gate.shape[1]
    weight_grads = []
    for part, dim in (
        (contract(all_rows, gate_grad, 0, 0), 1),
        (contract(all_rows, up_grad, 0, 0), 1),
        (contract(hidden, all_cotangent, 0, 0), 0),
    ):
        kept = lax.slice_in_dim(part, 0, units, axis=dim)
        sent = lax.slice_in_dim(part, units, 2 * units, axis=dim).astype(bf16)
        weight_grads.append((kept + exchange(sent, "ffn", ffn_size, 1).astype(f32)).astype(bf16))
    weight_sums = [lax.psum(part, "tok") for part in weight_grads]
    gate_weight_grad, up_weight_grad, down_weight_grad = [part.astype(f32) for part in weight_sums]

    row_parts = row_parts[:2] + after(row_parts[2:], weight_grads)
    hidden_two_grad, cross_low, grad_pack, gain_ffn_grad = ffn_join(
        out_grad, hidden_two, gains, output_weights, cross_mixed, cross_stats, row_parts
    )
    earlier, query_parts = [], []

    def visit_backward(chunk, grads):
        part, *earlier[:] = cross_backward(
            chunk, info, query_chunks[chunk], grads, memory_parts, *earlier
        )
        query_parts.append(part)
        return part

    visit_chunks(grad_pack, ffn_size, visit_backward)
    memory_grads = earlier[0]
    query_parts = return_chunks(query_parts, ffn_size)
    memory_grad, other_grad, *memory_sum = memory_backward(
        sizes,
        me,
        memory_lines,
        memory_other,
        after(memory_grads, query_parts[1]).reshape(-1, 2, held, 2 * KEYS),
        memory_weights,
        cross_mixed,
        cross_low,
    )
    query_parts = query_parts[:2] + after(query_parts[2:], (memory_sum, weight_sums))
    query_grads, hidden_one_grad, self_low, mix_grad, gain_cross_grad = query_join(
        hidden_two_grad, hidden_one, gains, full_second, query_parts
    )
    other_grad = exchange(other_grad, "ffn", ffn_size, 1)
    memory_grad = place_pairs(me, memory_grad, other_grad).reshape(memory.shape)
    products = [(normed_two, query_grads, 0, 1), (self_mixed, self_low, 0, 0)]
    outer = middle = memory_sum
    if direct:
        middle = grad_blocks(sizes, me, products)
        outer = reduce_core(sizes, after(memory_sum, query_grads), middle)
        mix_grad = after(mix_grad, (middle, outer))
    wide_grad, table_grad = self_backward(
        target_lengths, mix_grad, self_wide, self_stats, small_rows, lanes_of, buckets
    )
    if direct:
        outer = reduce_corner(sizes, outer, wide_grad)
        middle = reduce_core(sizes, middle, wide_grad)
        wide_grad = after(wide_grad, (outer, middle))
    targets_grad, gain_self_grad = input_grads(wide_grad, full_first, gains, targets, hidden_one_grad)

    branch_sum = lax.psum_scatter(
        after(branch_part, query_grads),
        "ffn",
        scatter_dimension=0,
        tiled=True,
        axis_index_groups=same_core,
    )
    table_grad = jnp.pad(
        table_grad[:, :BUCKETS].reshape(devices, table_share), ((0, 0), (0, share - table_share))
    )
    small_grads = jnp.concatenate(
        [gain_self_grad, gain_cross_grad, gain_ffn_grad, table_grad.reshape(1, D), jnp.zeros((4, D), f32)]
    )
    last_product = (normed_one, wide_grad, 0, 0)
    if direct:
        first = grad_blocks(sizes, me, [last_product], small_grads)
        outer = reduce_sides(sizes, outer, first)
        middle = reduce_corner(sizes, middle, first)
        first = reduce_core(sizes, first, memory_grad)
        outer_sum = reduce_line(sizes, outer, first)
        middle = reduce_sides(sizes, middle, first)
        first = reduce_corner(sizes, first, middle)
        first = reduce_sides(sizes, first)
        middle_sum = reduce_line(sizes, middle, (first, branch_sum))
        first_sum = reduce_line(sizes, first)
        branch_sum = after(branch_sum, first)
    else:
        order = [(block // ffn_size, block % ffn_size // 2, block % 2) for block in range(devices)]
        memory_rows = jnp.concatenate(
            [
                jnp.stack(memory_sum)[core ^ me[2], (tok ^ me[0]) * lines + (line ^ me[1])]
                for tok, line, core in order
            ]
        )
        outer_sum, middle_sum, first_sum = [
            reduce_rows(jnp.concatenate(parts, axis=1), tok_size, ffn_size)
            for parts in (
                [memory_rows],
                [contract(*one) for one in products],
                [contract(*last_product), jnp.pad(small_grads.T, ((0, 0), (0, SMALL - 8)))],
            )
        ]
    ffn_branch = branch_sum.astype(f32)
    hidden_three = hidden_two + ffn_branch
    layer_out = hidden_three.astype(jnp.bfloat16)
    valid = position[None, :] < target_lengths[:, None]
    counted = target_lengths.astype(jnp.float32) * D
    squares = [
        jnp.sum(hidden_three * hidden_three, axis=1),
        self_squares[:, 0],
        cross_squares[:, 0],
        jnp.sum(ffn_branch * ffn_branch, axis=1),
    ]
    squares = jnp.stack([part.reshape(pair_count, TGT) for part in squares], axis=1)
    squares = jnp.sum(jnp.where(valid[:, None, :], squares, 0.0), axis=2)
    rms_values = jnp.sqrt(squares / counted[:, None])

    small_sum = first_sum[:, D + 2 * KEYS :]
    return (
        layer_out,
        targets_grad,
        memory_grad,
        rms_values,
        small_sum[:table_share, 3],
        small_sum[:, 0],
        small_sum[:, 1],
        small_sum[:, 2],
        first_sum[:, :D],
        first_sum[:, D : D + KEYS],
        first_sum[:, D + KEYS : D + 2 * KEYS],
        middle_sum[:, D : 2 * D],
        middle_sum[:, :D],
        outer_sum[:, :KEYS],
        outer_sum[:, KEYS : 2 * KEYS],
        outer_sum[:, 2 * KEYS :],
        gate_weight_grad,
        up_weight_grad,
        down_weight_grad,
    )


def solution(mesh):
    rows = P(("tok", "ffn"), None)
    flat = P(("tok", "ffn"))
    memory = P("tok", "ffn", None)
    columns, inner = P(None, "ffn"), P("ffn", None)
    in_specs = (
        (rows, memory, rows, flat, flat, P()) + (flat,) * 4 + (rows,) * 8 + (columns, columns, inner)
    )
    out_specs = (
        (rows, rows, memory, rows) + (flat,) * 4 + (rows,) * 8 + (columns, columns, inner)
    )
    return jax.shard_map(
        functools.partial(on_device, mesh.shape["tok"], mesh.shape["ffn"]),
        mesh=mesh,
        in_specs=in_specs,
        out_specs=out_specs,
        check_vma=False,
    )
```

```python
import functools

import jax
import jax.numpy as jnp
from jax import lax
from jax.experimental import pallas as pl
from jax.experimental.pallas import tpu as pltpu
from jax.sharding import PartitionSpec as P

D = 1024
HEADS = 16
HEAD = 64
GROUPS = 8
BUCKETS = 32
TGT = 128
KEYS = GROUPS * HEAD
SMALL = 128
VMEM = 56 * 1024 * 1024

norm_epsilon = 1e-06
masked_value = -1e30
bf16 = jnp.bfloat16
f32 = jnp.float32


def matmul(left, right):
    return jnp.dot(left, right, preferred_element_type=jnp.float32)


def contract(left, right, left_dim, right_dim):
    return lax.dot_general(
        left, right, (((left_dim,), (right_dim,)), ((), ())), preferred_element_type=jnp.float32
    )


def vmem_call(body, outs, operands, scalars=(), scratch=(), name=None, flops=1000000000):
    specs = [
        one[1] if isinstance(one, tuple) else pl.BlockSpec(memory_space=pltpu.VMEM) for one in operands
    ]
    operands = [one[0] if isinstance(one, tuple) else one for one in operands]
    return pl.pallas_call(
        body,
        in_specs=[pl.BlockSpec(memory_space=pltpu.SMEM)] * len(scalars) + specs,
        out_specs=[pl.BlockSpec(memory_space=pltpu.VMEM)] * len(outs),
        out_shape=[jax.ShapeDtypeStruct(shape, dtype) for shape, dtype in outs],
        scratch_shapes=list(scratch),
        compiler_params=pltpu.CompilerParams(vmem_limit_bytes=VMEM),
        cost_estimate=pl.CostEstimate(flops=flops, bytes_accessed=8000000, transcendentals=0),
        name=name,
    )(*scalars, *operands)


def inverse_root(hidden):
    return lax.rsqrt(jnp.mean(hidden * hidden, axis=-1, keepdims=True) + norm_epsilon)


def norm_pull(hidden, gain, cotangent):
    scale = inverse_root(hidden)
    weighted = cotangent * gain
    inner = jnp.mean(hidden * weighted, axis=-1, keepdims=True)
    hidden_grad = scale * weighted - hidden * (scale * scale * scale * inner)
    return hidden_grad, jnp.sum(cotangent * hidden * scale, axis=0, keepdims=True)


def self_pieces(pair, group, wide_ref):
    rows = slice(pair * TGT, (pair + 1) * TGT)
    start = group * 2 * HEAD
    queries = jnp.concatenate(
        [wide_ref[rows, start : start + HEAD], wide_ref[rows, start + HEAD : start + 2 * HEAD]],
        axis=0,
    )
    start = D + group * HEAD
    return (
        queries,
        wide_ref[rows, start : start + HEAD],
        wide_ref[rows, start + KEYS : start + KEYS + HEAD],
    )


def self_scores(queries, keys, bias, length):
    raw = contract(keys, queries, 1, 1) * HEAD ** (-0.5) + bias
    key = lax.broadcasted_iota(jnp.int32, (TGT, 2 * TGT), 0)
    query = lax.broadcasted_iota(jnp.int32, (TGT, 2 * TGT), 1) % TGT
    return jnp.where((key <= query) & (key < length), raw, masked_value)


def self_bias(small_ref, lane_ref, group):
    lanes = lane_ref[...]
    source = jnp.broadcast_to(small_ref[3:4, group * TGT : (group + 1) * TGT], (TGT, TGT))
    return jnp.concatenate(
        [jnp.take_along_axis(source, lanes + head * HEAD, axis=1) for head in range(2)], axis=1
    )


def self_forward_kernel(sizes, share, me_ref, length_ref, row_ref, lane_ref, *refs):
    pieces, refs = refs[:-7], refs[-7:]
    norm_ref, wide_ref, mix_ref, stat_ref, small_ref, weight_ref, sems = refs
    inputs = row_ref[...].astype(f32)
    place_pieces(sizes, share, me_ref, pieces, 0, weight_ref, sems)
    small = weight_ref[:, D + 2 * KEYS :].astype(f32).T
    small_ref[...] = small[:8]
    normed = (inputs * inverse_root(inputs) * small[0:1, :]).astype(bf16)
    norm_ref[...] = normed
    wide_ref[...] = matmul(normed, weight_ref[:, : D + 2 * KEYS]).astype(bf16)
    for group in range(GROUPS):
        bias = self_bias(small_ref, lane_ref, group)
        for pair in range(row_ref.shape[0] // TGT):
            queries, keys, values = self_pieces(pair, group, wide_ref)
            scores = self_scores(queries, keys, bias, length_ref[pair])
            highest = jnp.max(scores, axis=0, keepdims=True)
            weights = jnp.exp(scores - highest)
            totals = jnp.sum(weights, axis=0, keepdims=True)
            probs = (weights * (1.0 / totals)).astype(bf16)
            mixed = contract(probs, values, 0, 0).astype(bf16)
            start = group * 2 * HEAD
            mix_ref[pair * TGT : (pair + 1) * TGT, start : start + 2 * HEAD] = jnp.concatenate(
                [mixed[:TGT], mixed[TGT:]], axis=1
            )
            logsum = highest + jnp.log(totals)
            at = pair * HEADS + 2 * group
            stat_ref[at : at + 1, :] = logsum[:, :TGT]
            stat_ref[at + 1 : at + 2, :] = logsum[:, TGT:]


ANYWHERE = pl.BlockSpec(memory_space=pl.ANY)


def self_forward(sizes, share, me, lengths, rows, lanes, pieces):
    count = rows.shape[0]
    return vmem_call(
        functools.partial(self_forward_kernel, sizes, share),
        [
            ((count, D), bf16),
            ((count, D + 2 * KEYS), bf16),
            ((count, D), bf16),
            ((count // TGT * HEADS, TGT), f32),
            ((8, D), f32),
        ],
        [rows, lanes] + [(piece, ANYWHERE) for piece in pieces],
        [me, lengths],
        [pltpu.VMEM((D, D + 2 * KEYS + SMALL), bf16), pltpu.SemaphoreType.DMA((sizes[0] * sizes[1],))],
        name="self_forward",
    )


def self_output_kernel(sizes, share, me_ref, row_ref, mix_ref, small_ref, *refs):
    pieces, refs = refs[:-6], refs[-6:]
    hidden_ref, norm_ref, query_ref, square_ref, weight_ref, sems = refs
    place_pieces(sizes, share, me_ref, pieces, D + 2 * KEYS + SMALL, weight_ref, sems)
    branch = matmul(mix_ref[...], weight_ref[:, :D])
    square_ref[...] = jnp.sum(branch * branch, axis=1, keepdims=True)
    hidden = row_ref[...].astype(f32) + branch
    hidden_ref[...] = hidden
    normed = (hidden * inverse_root(hidden) * small_ref[1:2, :]).astype(bf16)
    norm_ref[...] = normed
    queries = matmul(normed, weight_ref[:, D:]).astype(bf16) * bf16(HEAD ** (-0.5))
    query_ref[...] = queries.T


def self_output_part(sizes, share, me, rows, mixed, small, pieces):
    count = rows.shape[0]
    return vmem_call(
        functools.partial(self_output_kernel, sizes, share),
        [((count, D), f32), ((count, D), bf16), ((D, count), bf16), ((count, 1), f32)],
        [rows, mixed, small] + [(piece, ANYWHERE) for piece in pieces],
        [me],
        [pltpu.VMEM((D, 2 * D), bf16), pltpu.SemaphoreType.DMA((sizes[0] * sizes[1],))],
        name="self_output",
    )


def cross_join_kernel(
    hidden_ref, gain_ref, weight_ref, *refs
):
    parts, (mix_ref, stat_ref, out_ref, norm_ref, square_ref) = refs[:-5], refs[-5:]
    logs = [join_terms(part[D : D + 3 * HEADS, :]) for part in parts]
    highest = functools.reduce(jnp.maximum, logs)
    weights = [jnp.exp(log - highest) for log in logs]
    totals = functools.reduce(jnp.add, weights)
    stat_ref[...] = highest + jnp.log(totals)
    weights = [weight * (1.0 / totals) for weight in weights]
    for head in range(HEADS):
        at = slice(head * HEAD, (head + 1) * HEAD)
        mix_ref[at, :] = functools.reduce(
            jnp.add,
            [
                part[at, :].astype(f32) * weight[head : head + 1, :]
                for part, weight in zip(parts, weights, strict=True)
            ],
        )
    branch = contract(mix_ref[...].astype(bf16), weight_ref[...], 0, 0)
    square_ref[...] = jnp.sum(branch * branch, axis=1, keepdims=True)
    hidden = hidden_ref[...] + branch
    out_ref[...] = hidden
    norm_ref[...] = (hidden * inverse_root(hidden) * gain_ref[2:3, :]).astype(bf16)


def cross_join(hidden, gains, weights, parts):
    count = hidden.shape[0]
    return vmem_call(
        cross_join_kernel,
        [
            ((D, count), f32),
            ((HEADS, count), f32),
            ((count, D), f32),
            ((count, D), bf16),
            ((count, 1), f32),
        ],
        [hidden, gains, weights, *parts],
        name="cross_join",
    )


def ffn_join_kernel(cotangent_ref, hidden_ref, gain_ref, weight_ref, mix_ref, stat_ref, *refs):
    parts, (grad_ref, low_ref, pack_ref, gain_grad_ref) = refs[:-4], refs[-4:]
    norm_grad = functools.reduce(jnp.add, [part[...].astype(f32) for part in parts])
    back, gain_grad_ref[...] = norm_pull(hidden_ref[...], gain_ref[2:3, :], norm_grad)
    grad = cotangent_ref[...].astype(f32) + back
    grad_ref[...] = grad
    low = grad.astype(bf16)
    low_ref[...] = low
    mixed_grad = contract(weight_ref[...], low, 1, 1).astype(bf16)
    pack_ref[:D, :] = mixed_grad
    product = mixed_grad.astype(f32) * mix_ref[...]
    inner = jnp.concatenate(
        [
            jnp.sum(product[head * HEAD : (head + 1) * HEAD], axis=0, keepdims=True)
            for head in range(HEADS)
        ],
        axis=0,
    )
    for place, term in enumerate(split_terms(stat_ref[...]) + split_terms(inner)):
        pack_ref[D + place * HEADS : D + (place + 1) * HEADS, :] = term


def ffn_join(cotangent, hidden, gains, weights, mixed, stats, parts):
    count = hidden.shape[0]
    return vmem_call(
        ffn_join_kernel,
        [((count, D), f32), ((count, D), bf16), ((D + 6 * HEADS, count), bf16), ((1, D), f32)],
        [cotangent, hidden, gains, weights, mixed, stats, *parts],
        name="ffn_join",
    )


def query_join_kernel(grad_ref, hidden_ref, gain_ref, weight_ref, *refs):
    parts, (sum_ref, out_ref, low_ref, mix_grad_ref, gain_grad_ref) = refs[:-5], refs[-5:]
    queries = functools.reduce(jnp.add, [part[...].astype(f32) for part in parts]).astype(bf16)
    sum_ref[...] = queries
    norm_grad = contract(queries, weight_ref[:, D:], 0, 1)
    back, gain_grad_ref[...] = norm_pull(hidden_ref[...], gain_ref[1:2, :], norm_grad)
    grad = grad_ref[...] + back
    out_ref[...] = grad
    low = grad.astype(bf16)
    low_ref[...] = low
    mix_grad_ref[...] = contract(low, weight_ref[:, :D], 1, 1).astype(bf16)


def query_join(grad, hidden, gains, weights, parts):
    count = hidden.shape[0]
    return vmem_call(
        query_join_kernel,
        [
            ((D, count), bf16),
            ((count, D), f32),
            ((count, D), bf16),
            ((count, D), bf16),
            ((1, D), f32),
        ],
        [grad, hidden, gains, weights, *parts],
        name="query_join",
    )


def self_backward_kernel(
    length_ref,
    mix_grad_ref,
    wide_ref,
    stat_ref,
    small_ref,
    lane_ref,
    bucket_ref,
    wide_grad_ref,
    table_grad_ref,
    score_ref,
):
    pairs = mix_grad_ref.shape[0] // TGT
    for group in range(GROUPS):
        bias = self_bias(small_ref, lane_ref, group)
        score_total = None
        for pair in range(pairs):
            queries, keys, values = self_pieces(pair, group, wide_ref)
            rows = slice(pair * TGT, (pair + 1) * TGT)
            start = group * 2 * HEAD
            mixed_grad = jnp.concatenate(
                [
                    mix_grad_ref[rows, start : start + HEAD],
                    mix_grad_ref[rows, start + HEAD : start + 2 * HEAD],
                ],
                axis=0,
            )
            at = pair * HEADS + 2 * group
            logsum = jnp.concatenate([stat_ref[at : at + 1, :], stat_ref[at + 1 : at + 2, :]], axis=1)
            scores = self_scores(queries, keys, bias, length_ref[pair])
            probs = jnp.exp(scores - logsum)
            prob_grad = contract(values, mixed_grad, 1, 1)
            inner = jnp.sum(probs * prob_grad, axis=0, keepdims=True)
            score_grad = (probs * (prob_grad - inner)).astype(bf16)
            value_grad = matmul(probs.astype(bf16), mixed_grad).astype(bf16)
            key_grad = (matmul(score_grad, queries) * HEAD ** (-0.5)).astype(bf16)
            query_grad = (contract(score_grad, keys, 0, 0) * HEAD ** (-0.5)).astype(bf16)
            wide_grad_ref[rows, start : start + 2 * HEAD] = jnp.concatenate(
                [query_grad[:TGT], query_grad[TGT:]], axis=1
            )
            start = D + group * HEAD
            wide_grad_ref[rows, start : start + HEAD] = key_grad
            wide_grad_ref[rows, start + KEYS : start + KEYS + HEAD] = value_grad
            wide = score_grad.astype(f32)
            score_total = wide if score_total is None else score_total + wide
        score_ref[2 * group] = score_total[:, :TGT]
        score_ref[2 * group + 1] = score_total[:, TGT:]
    buckets = bucket_ref[...]
    lane = lax.broadcasted_iota(jnp.int32, (HEADS, TGT), 1)

    def one_bucket(bucket, table_grad):
        inside = buckets == bucket
        sums = jnp.concatenate(
            [
                jnp.sum(jnp.where(inside, score_ref[head], 0.0), axis=0, keepdims=True)
                for head in range(HEADS)
            ],
            axis=0,
        )
        return jnp.where(lane == bucket, jnp.sum(sums, axis=1, keepdims=True), table_grad)

    table_grad_ref[...] = lax.fori_loop(0, BUCKETS, one_bucket, jnp.zeros((HEADS, TGT), f32))


def self_backward(lengths, mix_grad, wide, stats, small, lanes, buckets):
    return vmem_call(
        self_backward_kernel,
        [(wide.shape, bf16), ((HEADS, TGT), f32)],
        [mix_grad, wide, stats, small, lanes, buckets],
        [lengths],
        [pltpu.VMEM((HEADS, TGT, TGT), f32)],
        name="self_backward",
        flops=8000000000,
    )


def input_grads_kernel(wide_grad_ref, weight_ref, gain_ref, row_ref, grad_ref, out_ref, gain_grad_ref):
    norm_grad = contract(wide_grad_ref[...], weight_ref[...], 1, 1)
    back, gain_grad_ref[...] = norm_pull(row_ref[...].astype(f32), gain_ref[0:1, :], norm_grad)
    out_ref[...] = (grad_ref[...] + back).astype(bf16)


def input_grads(wide_grad, weights, gains, rows, grad):
    return vmem_call(
        input_grads_kernel,
        [(rows.shape, bf16), ((1, D), f32)],
        [wide_grad, weights, gains, rows, grad],
        name="input_grads",
    )


def split_terms(value):
    high = value.astype(bf16)
    rest = value - high.astype(f32)
    middle = rest.astype(bf16)
    low = (rest - middle.astype(f32)).astype(bf16)
    return [high, middle, low]


def join_terms(block):
    return (
        block[:HEADS].astype(f32)
        + block[HEADS : 2 * HEADS].astype(f32)
        + block[2 * HEADS : 3 * HEADS].astype(f32)
    )


def both_heads(ref, group):
    start = group * 2 * HEAD
    return jnp.concatenate(
        [ref[start : start + HEAD, :], ref[start + HEAD : start + 2 * HEAD, :]], axis=1
    )


def both_rows(stat, group):
    return jnp.concatenate([stat[2 * group : 2 * group + 1], stat[2 * group + 1 : 2 * group + 2]], axis=1)


def valid_positions(info_ref, chunk, pair, positions):
    held = positions // 2
    length = info_ref[chunk, 3 + pair]
    place = lax.broadcasted_iota(jnp.int32, (positions, 2 * TGT), 0)
    limit = jnp.where(
        place < held, length - info_ref[chunk, 1], held + length - info_ref[chunk, 2]
    )
    return place < limit


def cross_forward_kernel(chunk, info_ref, query_ref, memory_ref, mix_ref, stat_ref):
    pair = pl.program_id(0)
    mask = valid_positions(info_ref, chunk, pair, memory_ref.shape[1])
    for group in range(GROUPS):
        keys = memory_ref[0, :, group * HEAD : (group + 1) * HEAD]
        values = memory_ref[0, :, KEYS + group * HEAD : KEYS + (group + 1) * HEAD]
        scores = jnp.where(mask, matmul(keys, both_heads(query_ref, group)), masked_value)
        highest = jnp.max(scores, axis=0, keepdims=True)
        weights = jnp.exp(scores - highest)
        totals = jnp.sum(weights, axis=0, keepdims=True)
        mixed = contract(weights.astype(bf16), values, 0, 0).T * (1.0 / totals)
        mixed = mixed.astype(bf16)
        start = group * 2 * HEAD
        mix_ref[start : start + HEAD, :] = mixed[:, :TGT]
        mix_ref[start + HEAD : start + 2 * HEAD, :] = mixed[:, TGT:]
        logsum = highest + jnp.log(totals)
        stat_ref[2 * group : 2 * group + 1, :] = logsum[:, :TGT]
        stat_ref[2 * group + 1 : 2 * group + 2, :] = logsum[:, TGT:]
    for place, term in enumerate(split_terms(stat_ref[...])):
        mix_ref[D + place * HEADS : D + (place + 1) * HEADS, :] = term


def cross_forward(chunk, info, queries, memory_parts):
    positions, wide = memory_parts.shape[1], memory_parts.shape[2]
    rows = queries.shape[1]
    return pl.pallas_call(
        functools.partial(cross_forward_kernel, chunk),
        grid_spec=pltpu.PrefetchScalarGridSpec(
            num_scalar_prefetch=1,
            grid=(rows // TGT,),
            in_specs=[
                pl.BlockSpec((D, TGT), lambda pair, info: (0, pair)),
                pl.BlockSpec((1, positions, wide), lambda pair, info: (info[chunk, 0] + pair, 0, 0)),
            ],
            out_specs=pl.BlockSpec((D + 3 * HEADS, TGT), lambda pair, info: (0, pair)),
            scratch_shapes=[pltpu.VMEM((HEADS, TGT), f32)],
        ),
        out_shape=jax.ShapeDtypeStruct((D + 3 * HEADS, rows), bf16),
        compiler_params=pltpu.CompilerParams(vmem_limit_bytes=VMEM),
        cost_estimate=pl.CostEstimate(flops=6000000000, bytes_accessed=4000000, transcendentals=0),
        name="cross_forward",
    )(info, queries, memory_parts)


def cross_backward_kernel(chunk, info_ref, query_ref, grad_ref, memory_ref, *rest):
    query_grad_ref, memory_grad_ref = rest[-2:]
    pair = pl.program_id(0)
    mask = valid_positions(info_ref, chunk, pair, memory_ref.shape[1])
    logsum = join_terms(grad_ref[D : D + 3 * HEADS, :])
    inner = join_terms(grad_ref[D + 3 * HEADS : D + 6 * HEADS, :])
    for tile in range(GROUPS // 2):
        key_parts, value_parts = [], []
        for group in (2 * tile, 2 * tile + 1):
            keys = memory_ref[0, :, group * HEAD : (group + 1) * HEAD]
            values = memory_ref[0, :, KEYS + group * HEAD : KEYS + (group + 1) * HEAD]
            queries = both_heads(query_ref, group)
            mixed_grad = both_heads(grad_ref, group)
            scores = matmul(keys, queries) - both_rows(logsum, group)
            probs = jnp.exp(jnp.where(mask, scores, masked_value))
            prob_grad = matmul(values, mixed_grad) - both_rows(inner, group)
            score_grad = (probs * prob_grad).astype(bf16)
            value_parts.append(contract(probs.astype(bf16), mixed_grad, 1, 1).astype(bf16))
            key_parts.append(contract(score_grad, queries, 1, 1).astype(bf16))
            query_grad = (contract(keys, score_grad, 0, 0) * HEAD ** (-0.5)).astype(bf16)
            start = group * 2 * HEAD
            query_grad_ref[start : start + HEAD, :] = query_grad[:, :TGT]
            query_grad_ref[start + HEAD : start + 2 * HEAD, :] = query_grad[:, TGT:]
        columns = 2 * HEAD * tile
        memory_grad_ref[0, :, columns : columns + 2 * HEAD] = jnp.concatenate(key_parts, axis=1)
        memory_grad_ref[0, :, KEYS + columns : KEYS + columns + 2 * HEAD] = jnp.concatenate(
            value_parts, axis=1
        )


def cross_backward(chunk, info, queries, grads, memory_parts, *earlier):
    positions, wide = memory_parts.shape[1], memory_parts.shape[2]
    rows = queries.shape[1]
    place = pl.BlockSpec((1, positions, wide), lambda pair, info: (info[chunk, 0] + pair, 0, 0))
    return pl.pallas_call(
        functools.partial(cross_backward_kernel, chunk),
        grid_spec=pltpu.PrefetchScalarGridSpec(
            num_scalar_prefetch=1,
            grid=(rows // TGT,),
            in_specs=[
                pl.BlockSpec((D, TGT), lambda pair, info: (0, pair)),
                pl.BlockSpec((D + 6 * HEADS, TGT), lambda pair, info: (0, pair)),
                place,
            ]
            + [pl.BlockSpec(memory_space=pl.ANY)] * len(earlier),
            out_specs=[pl.BlockSpec((D, TGT), lambda pair, info: (0, pair)), place],
        ),
        out_shape=[
            jax.ShapeDtypeStruct((D, rows), bf16),
            jax.ShapeDtypeStruct(memory_parts.shape, bf16),
        ],
        input_output_aliases={4: 1} if earlier else {},
        compiler_params=pltpu.CompilerParams(vmem_limit_bytes=VMEM),
        cost_estimate=pl.CostEstimate(flops=10000000000, bytes_accessed=8000000, transcendentals=0),
        name="cross_backward",
    )(info, queries, grads, memory_parts, *earlier)


def ffn_kernel(me_ref, row_ref, cotangent_ref, gate_ref, up_ref, down_ref, *rest):
    row_grad_ref, branch_ref, rows_ref, kept_cotangent_ref, hidden_ref, gate_grad_ref, up_grad_ref = rest[
        -7:
    ]
    rows = row_ref[...]
    rows_ref[0] = rows
    gate = matmul(rows, gate_ref[...])
    up = matmul(rows, up_ref[...])
    cotangent = cotangent_ref[0]
    kept_cotangent_ref[0] = cotangent
    hidden_grad = contract(cotangent, down_ref[...], 1, 1)
    square = gate * gate
    slope = 0.7978845608028654
    bend = jnp.tanh(slope * gate * (1.0 + 0.044715 * square))
    half = 0.5 * (1.0 + bend)
    value = gate * half
    derivative = half + 0.5 * gate * (1.0 - bend * bend) * slope * (1.0 + 3 * 0.044715 * square)
    hidden = (value * up).astype(bf16)
    gate_grad = (hidden_grad * up * derivative).astype(bf16)
    up_grad = (hidden_grad * value).astype(bf16)
    row_grad = contract(gate_grad, gate_ref[...], 1, 1) + contract(up_grad, up_ref[...], 1, 1)
    row_grad_ref[...] = row_grad.astype(bf16)
    branch_ref[0] = matmul(hidden, down_ref[...]).astype(bf16)
    hidden_ref[0] = hidden
    gate_grad_ref[0] = gate_grad
    up_grad_ref[0] = up_grad


def ffn_chunk(chunk, chunks, me, rows, cotangent, gate, up, down, *earlier):
    count, width = rows.shape
    wide = gate.shape[1]
    kept = [width, width, width, wide, wide, wide]
    by_line = pl.BlockSpec((1, count, width), lambda step, me: (me[1] ^ chunk, 0, 0))

    def whole(array):
        return pl.BlockSpec(array.shape, lambda step, me: (0, 0))

    return pl.pallas_call(
        ffn_kernel,
        grid_spec=pltpu.PrefetchScalarGridSpec(
            num_scalar_prefetch=1,
            grid=(1,),
            in_specs=[whole(rows), by_line]
            + [whole(array) for array in (gate, up, down)]
            + [ANYWHERE] * len(earlier),
            out_specs=[whole(rows), by_line]
            + [pl.BlockSpec((1, count, size), lambda step, me: (chunk, 0, 0)) for size in kept[1:]],
        ),
        out_shape=[jax.ShapeDtypeStruct((count, width), bf16)]
        + [jax.ShapeDtypeStruct((chunks, count, size), bf16) for size in kept],
        input_output_aliases={6 + place: 1 + place for place in range(len(earlier))},
        compiler_params=pltpu.CompilerParams(vmem_limit_bytes=VMEM),
        cost_estimate=pl.CostEstimate(flops=3000000000, bytes_accessed=8000000, transcendentals=0),
        name="ffn_chunk",
    )(me, rows, cotangent, gate, up, down, *earlier)


def exchange(value, axis, size, mask):
    return lax.ppermute(value, axis, [(place, place ^ mask) for place in range(size)])


def visit_chunks(value, size, work, settle=False):
    lines = size // 2

    def by_lines(array, pairs):
        pairs = [(2 * old + core, 2 * new + core) for old, new in pairs for core in range(2)]
        return lax.ppermute(array, "ffn", pairs)

    if lines != 4:
        chunks = [value] + [exchange(value, "ffn", size, 2 * step) for step in range(1, lines)]
        return [work(chunk, one) for chunk, one in enumerate(chunks)]
    across = exchange(value, "ffn", size, 4)
    beside = exchange(value, "ffn", size, 2)
    results = [work(0, value)]
    across = after(across, results[0])
    middle = by_lines(after(value, across), [(1, 2), (2, 1)])
    onward = by_lines(across, [(2, 3), (1, 0)])
    results.append(work(1, after(beside, across)))
    line = lax.axis_index("ffn") // 2
    last = [middle, onward]
    if settle:
        last = after(last, results[1])
        across = after(across, last)
    results.append(work(2, across))
    results.append(work(3, jnp.where((line == 0) | (line == 3), last[1], last[0])))
    return results


def return_chunks(parts, size):
    return [parts[0]] + [
        exchange(parts[step], "ffn", size, 2 * step) for step in range(1, size // 2)
    ]


def reduce_rows(grads, tok_size, ffn_size):
    columns = grads.shape[1]
    me_ffn, me_tok = lax.axis_index("ffn"), lax.axis_index("tok")

    def halves(value, dim, bit):
        first = lax.index_in_dim(value, 0, dim, keepdims=False)
        second = lax.index_in_dim(value, 1, dim, keepdims=False)
        return jnp.where(bit == 0, first, second), jnp.where(bit == 0, second, first)

    rows = grads.shape[0] // (tok_size * ffn_size)
    value = grads.reshape(tok_size, ffn_size // 2, 2, rows, columns)
    kept, sent = halves(value, 2, me_ffn & 1)
    value = kept.astype(f32) + exchange(sent.astype(bf16), "ffn", ffn_size, 1).astype(f32)

    bits = tok_size.bit_length() - 1
    value = value.reshape((2,) * bits + (ffn_size // 2, rows, columns))
    half = columns // 2 // 128 * 128
    sides = []
    for part, order in (
        (value[..., :half], list(range(bits))),
        (value[..., half:], list(range(bits))[::-1]),
    ):
        left = list(range(bits))
        for bit in order:
            dim = left.index(bit)
            left.remove(bit)
            weight = 1 << (bits - 1 - bit)
            kept, sent = halves(part, dim, (me_tok // weight) & 1)
            part = kept.astype(f32) + exchange(sent.astype(bf16), "tok", tok_size, weight).astype(f32)
        sides.append(part)
    value = jnp.concatenate(sides, axis=-1)
    line = me_ffn // 2
    total = lax.dynamic_index_in_dim(value, line, 0, keepdims=False)
    low = value.astype(bf16)
    for step in range(1, ffn_size // 2):
        part = lax.dynamic_index_in_dim(low, line ^ step, 0, keepdims=False)
        total = total + exchange(part, "ffn", ffn_size, 2 * step).astype(f32)
    return total


def memory_forward_kernel(me_ref, own_ref, other_ref, weight_ref, out_ref):
    pairs, held, width = other_ref.shape[2:]
    for place, rows in enumerate((own_ref[0, 0], other_ref[0, 0])):
        part = matmul(rows.reshape(pairs * held, width), weight_ref[...]).astype(bf16)
        out_ref[:, place] = part.reshape(pairs, held, part.shape[1])


def own_pairs(memory):
    unused, also, step, held, width = memory.shape
    return pl.BlockSpec((1, 1, step, held, width), lambda line, me: (line, me[2], 0, 0, 0))


def memory_forward(me, memory, other, weights):
    lines, unused, step, held, width = memory.shape
    return pl.pallas_call(
        memory_forward_kernel,
        grid_spec=pltpu.PrefetchScalarGridSpec(
            num_scalar_prefetch=1,
            grid=(lines,),
            in_specs=[
                own_pairs(memory),
                own_pairs(memory),
                pl.BlockSpec((width, 2 * KEYS), lambda line, me: (0, 0)),
            ],
            out_specs=pl.BlockSpec((step, 2, held, 2 * KEYS), lambda line, me: (line, 0, 0, 0)),
        ),
        out_shape=jax.ShapeDtypeStruct((lines * step, 2, held, 2 * KEYS), bf16),
        compiler_params=pltpu.CompilerParams(vmem_limit_bytes=VMEM),
        cost_estimate=pl.CostEstimate(flops=8600000000, bytes_accessed=18000000, transcendentals=0),
        name="memory_forward",
    )(me, memory, other, weights)


def memory_backward_kernel(
    sizes, me_ref, own_ref, other_ref, grad_ref, weight_ref, mix_ref, low_ref, *rest
):
    own_grad_ref, other_grad_ref, kept_ref, sent_ref, total = rest
    step = pl.program_id(0)
    pairs, held, width = other_ref.shape[2:]
    for place, (rows, out_ref) in enumerate(
        ((own_ref[0, 0], own_grad_ref), (other_ref[0, 0], other_grad_ref))
    ):
        grads = grad_ref[:, place].reshape(pairs * held, grad_ref.shape[3])
        out = contract(grads, weight_ref[...], 1, 1).astype(bf16)
        out_ref[...] = out.reshape(out_ref.shape)
        part = contract(rows.reshape(pairs * held, width), grads, 0, 0)
        if place == 0:
            total[...] = jnp.where(step == 0, part, total[...] + part)
        else:
            total[...] += part

    @pl.when(step == 0)
    def first():
        low = low_ref[...]
        for start in range(0, low.shape[1], 512):
            part = matmul(mix_ref[...].astype(bf16), low[:, start : start + 512])
            store_blocks(sizes, me_ref, kept_ref, sent_ref, 2 * KEYS + start, part)

    @pl.when(step == pl.num_programs(0) - 1)
    def last():
        store_blocks(sizes, me_ref, kept_ref, sent_ref, 0, total[...])


def memory_backward(sizes, me, memory, other, grads, weights, mixed, low):
    lines, unused, step, held, width = memory.shape
    block = pl.BlockSpec((step, held, width), lambda line, me: (line, 0, 0))
    shape = blocks_shape(sizes, 2 * KEYS + low.shape[1])
    return pl.pallas_call(
        functools.partial(memory_backward_kernel, sizes),
        grid_spec=pltpu.PrefetchScalarGridSpec(
            num_scalar_prefetch=1,
            grid=(lines,),
            in_specs=[
                own_pairs(memory),
                own_pairs(memory),
                pl.BlockSpec((step, 2, held, 2 * KEYS), lambda line, me: (line, 0, 0, 0)),
                pl.BlockSpec((width, 2 * KEYS), lambda line, me: (0, 0)),
                pl.BlockSpec(mixed.shape, lambda line, me: (0, 0)),
                pl.BlockSpec(low.shape, lambda line, me: (0, 0)),
            ],
            out_specs=[
                own_pairs(memory),
                block,
            ]
            + [pl.BlockSpec(shape, lambda line, me: (0,) * len(shape))] * 2,
            scratch_shapes=[pltpu.VMEM((width, 2 * KEYS), f32)],
        ),
        out_shape=[
            jax.ShapeDtypeStruct(memory.shape, bf16),
            jax.ShapeDtypeStruct((lines * step, held, width), bf16),
            jax.ShapeDtypeStruct(shape, bf16),
            jax.ShapeDtypeStruct(shape, bf16),
        ],
        compiler_params=pltpu.CompilerParams(vmem_limit_bytes=VMEM),
        cost_estimate=pl.CostEstimate(flops=17200000000, bytes_accessed=28000000, transcendentals=0),
        name="memory_backward",
    )(me, memory, other, grads, weights, mixed, low)


def place_pairs_kernel(me_ref, pair_ref, unused_ref, out_ref):
    out_ref[0, 0] = pair_ref[...]


def place_pairs(me, whole, pairs):
    lines, unused, step, held, width = whole.shape
    return pl.pallas_call(
        place_pairs_kernel,
        grid_spec=pltpu.PrefetchScalarGridSpec(
            num_scalar_prefetch=1,
            grid=(lines,),
            in_specs=[
                pl.BlockSpec((step, held, width), lambda line, me: (line, 0, 0)),
                pl.BlockSpec(memory_space=pl.ANY),
            ],
            out_specs=pl.BlockSpec(
                (1, 1, step, held, width), lambda line, me: (line, 1 - me[2], 0, 0, 0)
            ),
        ),
        out_shape=jax.ShapeDtypeStruct(whole.shape, bf16),
        input_output_aliases={2: 0},
        compiler_params=pltpu.CompilerParams(vmem_limit_bytes=VMEM),
        name="place_pairs",
    )(me, pairs, whole)


def blocks_shape(sizes, columns):
    tok_size, ffn_size = sizes
    return (tok_size * ffn_size // 2, D // (tok_size * ffn_size), columns)


def store_blocks(sizes, me_ref, kept_ref, sent_ref, column, value):
    tok_size, ffn_size = sizes
    rows = D // (tok_size * ffn_size)
    low = value.astype(bf16)
    columns = slice(column, column + value.shape[1])
    for block in range(0, tok_size * ffn_size, 2):
        tok, line = block // ffn_size, block % ffn_size // 2
        place = (tok ^ me_ref[0]) * (ffn_size // 2) + (line ^ me_ref[1])
        first = low[block * rows : (block + 1) * rows]
        second = low[(block + 1) * rows : (block + 2) * rows]
        kept_ref[place, :, columns] = jnp.where(me_ref[2] == 0, first, second)
        sent_ref[place, :, columns] = jnp.where(me_ref[2] == 0, second, first)


def grad_blocks_kernel(sizes, dims, me_ref, *refs):
    kept_ref, sent_ref = refs[-2:]
    column = 0
    for place, (left_dim, right_dim) in enumerate(dims):
        left, right = refs[2 * place], refs[2 * place + 1]
        for start in range(0, right.shape[1 - right_dim], 512):
            if right_dim == 0:
                part = right[:, start : start + 512]
            else:
                part = right[start : start + 512, :]
            product = contract(left[...], part, left_dim, right_dim)
            store_blocks(sizes, me_ref, kept_ref, sent_ref, column, product)
            column += 512
    extra = refs[2 * len(dims) : -2]
    if len(extra) == 2:
        kept_ref[:, :, column:] = extra[0][...]
        sent_ref[:, :, column:] = extra[1][...]
    elif extra:
        rows = extra[0][...]
        filled = jnp.concatenate([rows, jnp.zeros((SMALL - rows.shape[0], D), f32)], axis=0)
        store_blocks(sizes, me_ref, kept_ref, sent_ref, column, filled.T)


def grad_blocks(sizes, me, products, *extra):
    operands = [array for left, right, unused, also in products for array in (left, right)]
    columns = sum(right.shape[1 - dim] for unused, right, also, dim in products)
    operands += extra
    if extra:
        columns += extra[0].shape[2] if extra[0].ndim == 3 else SMALL
    return pl.pallas_call(
        functools.partial(grad_blocks_kernel, sizes, [(one[2], one[3]) for one in products]),
        in_specs=[pl.BlockSpec(memory_space=pltpu.SMEM)]
        + [pl.BlockSpec(memory_space=pltpu.VMEM)] * len(operands),
        out_specs=[pl.BlockSpec(memory_space=pltpu.VMEM)] * 2,
        out_shape=[jax.ShapeDtypeStruct(blocks_shape(sizes, columns), bf16)] * 2,
        compiler_params=pltpu.CompilerParams(vmem_limit_bytes=VMEM),
        name="grad_blocks",
    )(me, *operands)


def plus(*parts):
    return functools.reduce(jnp.add, [part.astype(f32) for part in parts]).astype(bf16)


def reduce_core(sizes, blocks, earlier=()):
    lines = sizes[1] // 2
    kept, sent = blocks
    other = after(exchange(sent, "ffn", sizes[1], 1), earlier)
    return [
        plus(kept[tok * lines : (tok + 1) * lines], other[tok * lines : (tok + 1) * lines])
        for tok in range(4)
    ]


def reduce_corner(sizes, parts, earlier=()):
    own, by_x, by_y, across = parts
    half = sizes[1] // 4
    top = exchange(across[:half], "tok", sizes[0], 1)
    bottom = exchange(across[half:], "tok", sizes[0], 2)
    top, bottom = after([top, bottom], earlier)
    by_x = jnp.concatenate([by_x[:half], plus(by_x[half:], bottom)], axis=0)
    by_y = jnp.concatenate([plus(by_y[:half], top), by_y[half:]], axis=0)
    return [own, by_x, by_y]


def reduce_sides(sizes, parts, earlier=()):
    own, by_x, by_y = parts
    arrived = [exchange(by_x, "tok", sizes[0], 1), exchange(by_y, "tok", sizes[0], 2)]
    return plus(own, *after(arrived, earlier))


def reduce_line(sizes, total, earlier=()):
    parts = [total[0]] + [
        exchange(total[step], "ffn", sizes[1], 2 * step) for step in range(1, sizes[1] // 2)
    ]
    parts = after(parts, earlier)
    return functools.reduce(jnp.add, [part.astype(f32) for part in parts])


def place_pieces(sizes, share, me_ref, pieces, column, target_ref, sems):
    columns = pl.ds(column, target_ref.shape[1])
    copies = []
    if len(pieces) == 1:
        copies.append(pltpu.make_async_copy(pieces[0].at[:, columns], target_ref, sems.at[0]))
    else:
        lines = sizes[1] // 2
        half = lines // 2
        for core in range(2):
            line_ref, x_ref, y_ref, top_ref, bottom_ref = pieces[5 * core : 5 * core + 5]
            for tok in range(4):
                for line in range(lines):
                    if tok < 3:
                        source = (line_ref, x_ref, y_ref)[tok].at[line]
                    else:
                        source = top_ref.at[line] if line < half else bottom_ref.at[line - half]
                    block = ((tok ^ me_ref[0]) * lines + (line ^ me_ref[1])) * 2 + (core ^ me_ref[2])
                    target = target_ref.at[pl.ds(pl.multiple_of(block * share, share), share), :]
                    copies.append(
                        pltpu.make_async_copy(source.at[:, columns], target, sems.at[len(copies)])
                    )
    for copy in copies:
        copy.start()
    for copy in copies:
        copy.wait()


def place_rows_kernel(sizes, share, starts, me_ref, *refs):
    pieces, outs, sems = refs[: -len(starts) - 1], refs[-len(starts) - 1 : -1], refs[-1]
    for column, out_ref in zip(starts, outs, strict=True):
        place_pieces(sizes, share, me_ref, pieces, column, out_ref, sems)


def place_rows(sizes, share, me, pieces, starts, columns):
    return vmem_call(
        functools.partial(place_rows_kernel, sizes, share, starts),
        [((sizes[0] * sizes[1] * share, columns), bf16) for unused in starts],
        [(piece, ANYWHERE) for piece in pieces],
        [me],
        [pltpu.SemaphoreType.DMA((sizes[0] * sizes[1],))],
        name="place_rows",
    )


def after(values, earlier):
    return lax.optimization_barrier((values, earlier))[0]


def gather_pieces(sizes, pack):
    tok_size, ffn_size = sizes
    lines = ffn_size // 2
    half = lines // 2
    line = [pack] + [exchange(pack, "ffn", ffn_size, 2 * step) for step in range(1, lines)]
    begun = line
    line = jnp.stack(line)
    by_x = exchange(line, "tok", tok_size, 1)
    by_y = exchange(line, "tok", tok_size, 2)
    top = exchange(by_y[:half], "tok", tok_size, 1)
    bottom = exchange(by_x[half:], "tok", tok_size, 2)
    held = [line, by_x, by_y, top, bottom]
    return held + [exchange(one, "ffn", ffn_size, 1) for one in held], begun


def on_device(
    tok_size,
    ffn_size,
    targets,
    memory,
    out_grad,
    target_lengths,
    memory_lengths,
    buckets,
    rel_table,
    gain_self,
    gain_cross,
    gain_ffn,
    self_query,
    self_key,
    self_value,
    self_output,
    cross_query,
    cross_key,
    cross_value,
    cross_output,
    ffn_gate,
    ffn_up,
    ffn_down,
):
    pair_count = target_lengths.shape[0]
    row_count = targets.shape[0]
    held = memory.shape[1]
    devices = tok_size * ffn_size
    me_tok, me_ffn = lax.axis_index("tok"), lax.axis_index("ffn")
    share = self_query.shape[0]
    table_share = rel_table.shape[0]

    sizes = (tok_size, ffn_size)
    direct = tok_size == 4 and share % 16 == 0
    me = jnp.stack([me_tok, me_ffn // 2, me_ffn % 2]).astype(jnp.int32)
    per_row = [
        jnp.pad(part.astype(bf16), (0, share - part.shape[0]))
        for part in (gain_self, gain_cross, gain_ffn, rel_table, memory_lengths // 64, memory_lengths % 64)
    ]
    small = jnp.pad(jnp.stack(per_row, axis=1), ((0, 0), (0, SMALL - len(per_row))))

    core = me_ffn % 2
    lines = ffn_size // 2
    both = ("tok", "ffn")
    pack = jnp.concatenate(
        [self_query, self_key, self_value, small, self_output, cross_query, cross_key, cross_value],
        axis=1,
    )
    same_core = [[2 * line + one for line in range(lines)] for one in range(2)]
    memory_lines = memory.reshape(lines, 2, pair_count, held, D)

    memory_other = exchange(memory_lines, "ffn", ffn_size, 1)

    if direct:
        pieces, begun = gather_pieces(sizes, pack)
    else:
        pieces = [lax.all_gather(pack, both, axis=0, tiled=True)]
        begun = pieces
    cotangents = lax.all_gather(
        after(out_grad, begun),
        "ffn",
        axis=0,
        tiled=False,
        axis_index_groups=same_core,
    )

    per_table = BUCKETS * HEADS // devices
    buckets = buckets.T
    lanes_of = buckets // per_table * (2 * per_table) + buckets % per_table
    normed_one, self_wide, self_mixed, self_stats, small_rows = self_forward(
        sizes, share, me, target_lengths, targets, lanes_of, pieces
    )
    hidden_one, normed_two, cross_queries, self_squares = self_output_part(
        sizes, share, me, targets, self_mixed, small_rows, pieces
    )
    gains = small_rows[:3]
    lengths = (small_rows[4] * 64 + small_rows[5]).astype(jnp.int32)
    lengths = lengths.reshape(devices, share)[:, :pair_count]
    (memory_weights,) = place_rows(
        sizes, share, me, after(pieces, cross_queries), (3 * D + 2 * KEYS + SMALL,), 2 * KEYS
    )
    memory_parts = memory_forward(me, memory_lines, memory_other, memory_weights)
    memory_parts = memory_parts.reshape(-1, 2 * held, 2 * KEYS)
    lengths = lax.dynamic_index_in_dim(
        lengths.reshape(tok_size, ffn_size, pair_count), me_tok, 0, keepdims=False
    )
    owner = me_ffn ^ (2 * jnp.arange(lines))
    info = jnp.concatenate(
        [
            (owner // 2 * pair_count)[:, None],
            jnp.broadcast_to(me_ffn * held, (lines, 1)),
            jnp.broadcast_to((me_ffn ^ 1) * held, (lines, 1)),
            jnp.take(lengths, owner, axis=0),
        ],
        axis=1,
    ).astype(jnp.int32)


    position = jnp.arange(TGT)

    query_chunks, mixed_parts, kept = [], [], {}
    kept["output"] = lax.all_gather(
        after(cross_output, (self_mixed, cotangents)), both, axis=0, tiled=True
    )

    def visit_forward(chunk, chunk_queries):
        query_chunks.append(chunk_queries)
        if chunk:
            chunk_queries = after(chunk_queries, mixed_parts[-1])
        mixed_parts.append(cross_forward(chunk, info, chunk_queries, memory_parts))
        return mixed_parts[-1]

    visit_chunks(cross_queries, ffn_size, visit_forward)
    output_weights = kept["output"]
    held_pieces, units = after((pieces, (ffn_gate, ffn_up, ffn_down)), mixed_parts[-1])
    placed = place_rows(sizes, share, me, held_pieces, (0, D + 2 * KEYS + SMALL), 2 * D)
    units = [
        jnp.concatenate([array, exchange(array, "ffn", ffn_size, 1)], axis=dim)
        for array, dim in zip(units, (1, 1, 0), strict=True)
    ]
    full_first, full_second = placed
    both_gate, both_up, both_down = units
    mixed_parts = return_chunks(mixed_parts, ffn_size)
    mixed_parts = mixed_parts[:1] + after(mixed_parts[1:], (placed, units))
    cross_mixed, cross_stats, hidden_two, normed_three, cross_squares = cross_join(
        hidden_one, gains, output_weights, mixed_parts
    )

    earlier, row_parts = [], []

    def visit_ffn(chunk, rows):
        row_part, *earlier[:] = ffn_chunk(
            chunk, lines, me, rows, cotangents, both_gate, both_up, both_down, *earlier
        )
        row_parts.append(row_part)
        return row_part

    visit_chunks(normed_three, ffn_size, visit_ffn)
    row_parts = return_chunks(row_parts, ffn_size)
    branch_part, all_rows, all_cotangent, hidden, gate_grad, up_grad = [
        array.reshape(lines * row_count, array.shape[2]) for array in after(earlier, row_parts[1])
    ]
    units = ffn_gate.shape[1]
    weight_grads = []
    for part, dim in (
        (contract(all_rows, gate_grad, 0, 0), 1),
        (contract(all_rows, up_grad, 0, 0), 1),
        (contract(hidden, all_cotangent, 0, 0), 0),
    ):
        kept = lax.slice_in_dim(part, 0, units, axis=dim)
        sent = lax.slice_in_dim(part, units, 2 * units, axis=dim).astype(bf16)
        weight_grads.append((kept + exchange(sent, "ffn", ffn_size, 1).astype(f32)).astype(bf16))
    weight_sums = [lax.psum(part, "tok") for part in weight_grads]
    gate_weight_grad, up_weight_grad, down_weight_grad = [part.astype(f32) for part in weight_sums]

    row_parts = row_parts[:2] + after(row_parts[2:], weight_grads)
    hidden_two_grad, cross_low, grad_pack, gain_ffn_grad = ffn_join(
        out_grad, hidden_two, gains, output_weights, cross_mixed, cross_stats, row_parts
    )
    earlier, query_parts = [], []

    def visit_backward(chunk, grads):
        part, *earlier[:] = cross_backward(
            chunk, info, query_chunks[chunk], grads, memory_parts, *earlier
        )
        query_parts.append(part)
        return part

    visit_chunks(grad_pack, ffn_size, visit_backward, settle=True)
    memory_grads = earlier[0]
    query_parts = return_chunks(query_parts, ffn_size)
    memory_grad, other_grad, *memory_sum = memory_backward(
        sizes,
        me,
        memory_lines,
        memory_other,
        after(memory_grads, query_parts[1]).reshape(-1, 2, held, 2 * KEYS),
        memory_weights,
        cross_mixed,
        cross_low,
    )
    query_parts = query_parts[:2] + after(query_parts[2:], (memory_sum, weight_sums))
    query_grads, hidden_one_grad, self_low, mix_grad, gain_cross_grad = query_join(
        hidden_two_grad, hidden_one, gains, full_second, query_parts
    )
    other_grad = exchange(other_grad, "ffn", ffn_size, 1)
    memory_grad = place_pairs(me, memory_grad, other_grad).reshape(memory.shape)
    products = [(normed_two, query_grads, 0, 1), (self_mixed, self_low, 0, 0)]
    outer = middle = memory_sum
    if direct:
        middle = grad_blocks(sizes, me, products)
        outer = reduce_core(sizes, after(memory_sum, query_grads), middle)
        mix_grad = after(mix_grad, (middle, outer))
    wide_grad, table_grad = self_backward(
        target_lengths, mix_grad, self_wide, self_stats, small_rows, lanes_of, buckets
    )
    if direct:
        outer = reduce_corner(sizes, outer, wide_grad)
        middle = reduce_core(sizes, middle, wide_grad)
        wide_grad = after(wide_grad, (outer, middle))
    targets_grad, gain_self_grad = input_grads(wide_grad, full_first, gains, targets, hidden_one_grad)

    branch_sum = lax.psum_scatter(
        after(branch_part, query_grads),
        "ffn",
        scatter_dimension=0,
        tiled=True,
        axis_index_groups=same_core,
    )
    table_grad = jnp.pad(
        table_grad[:, :BUCKETS].reshape(devices, table_share), ((0, 0), (0, share - table_share))
    )
    small_grads = jnp.concatenate(
        [gain_self_grad, gain_cross_grad, gain_ffn_grad, table_grad.reshape(1, D), jnp.zeros((4, D), f32)]
    )
    last_product = (normed_one, wide_grad, 0, 0)
    if direct:
        first = grad_blocks(sizes, me, [last_product], small_grads)
        outer = reduce_sides(sizes, outer, first)
        middle = reduce_corner(sizes, middle, first)
        first = reduce_core(sizes, first, memory_grad)
        outer_sum = reduce_line(sizes, outer, first)
        middle = reduce_sides(sizes, middle, first)
        first = reduce_corner(sizes, first, middle)
        first = reduce_sides(sizes, first)
        middle_sum = reduce_line(sizes, middle, (first, branch_sum))
        first_sum = reduce_line(sizes, first)
        branch_sum = after(branch_sum, first)
    else:
        order = [(block // ffn_size, block % ffn_size // 2, block % 2) for block in range(devices)]
        memory_rows = jnp.concatenate(
            [
                jnp.stack(memory_sum)[core ^ me[2], (tok ^ me[0]) * lines + (line ^ me[1])]
                for tok, line, core in order
            ]
        )
        outer_sum, middle_sum, first_sum = [
            reduce_rows(jnp.concatenate(parts, axis=1), tok_size, ffn_size)
            for parts in (
                [memory_rows],
                [contract(*one) for one in products],
                [contract(*last_product), jnp.pad(small_grads.T, ((0, 0), (0, SMALL - 8)))],
            )
        ]
    ffn_branch = branch_sum.astype(f32)
    hidden_three = hidden_two + ffn_branch
    layer_out = hidden_three.astype(jnp.bfloat16)
    valid = position[None, :] < target_lengths[:, None]
    counted = target_lengths.astype(jnp.float32) * D
    squares = [
        jnp.sum(hidden_three * hidden_three, axis=1),
        self_squares[:, 0],
        cross_squares[:, 0],
        jnp.sum(ffn_branch * ffn_branch, axis=1),
    ]
    squares = jnp.stack([part.reshape(pair_count, TGT) for part in squares], axis=1)
    squares = jnp.sum(jnp.where(valid[:, None, :], squares, 0.0), axis=2)
    rms_values = jnp.sqrt(squares / counted[:, None])

    small_sum = first_sum[:, D + 2 * KEYS :]
    return (
        layer_out,
        targets_grad,
        memory_grad,
        rms_values,
        small_sum[:table_share, 3],
        small_sum[:, 0],
        small_sum[:, 1],
        small_sum[:, 2],
        first_sum[:, :D],
        first_sum[:, D : D + KEYS],
        first_sum[:, D + KEYS : D + 2 * KEYS],
        middle_sum[:, D : 2 * D],
        middle_sum[:, :D],
        outer_sum[:, :KEYS],
        outer_sum[:, KEYS : 2 * KEYS],
        outer_sum[:, 2 * KEYS :],
        gate_weight_grad,
        up_weight_grad,
        down_weight_grad,
    )


def solution(mesh):
    rows = P(("tok", "ffn"), None)
    flat = P(("tok", "ffn"))
    memory = P("tok", "ffn", None)
    columns, inner = P(None, "ffn"), P("ffn", None)
    in_specs = (
        (rows, memory, rows, flat, flat, P()) + (flat,) * 4 + (rows,) * 8 + (columns, columns, inner)
    )
    out_specs = (
        (rows, rows, memory, rows) + (flat,) * 4 + (rows,) * 8 + (columns, columns, inner)
    )
    return jax.shard_map(
        functools.partial(on_device, mesh.shape["tok"], mesh.shape["ffn"]),
        mesh=mesh,
        in_specs=in_specs,
        out_specs=out_specs,
        check_vma=False,
    )
```

```python
import functools

import jax
import jax.numpy as jnp
from jax import lax
from jax.experimental import pallas as pl
from jax.experimental.pallas import tpu as pltpu
from jax.sharding import PartitionSpec as P

D = 1024
HEADS = 16
HEAD = 64
GROUPS = 8
BUCKETS = 32
TGT = 128
KEYS = GROUPS * HEAD
SMALL = 128
VMEM = 56 * 1024 * 1024

norm_epsilon = 1e-06
masked_value = -1e30
bf16 = jnp.bfloat16
f32 = jnp.float32


def matmul(left, right):
    return jnp.dot(left, right, preferred_element_type=jnp.float32)


def contract(left, right, left_dim, right_dim):
    return lax.dot_general(
        left, right, (((left_dim,), (right_dim,)), ((), ())), preferred_element_type=jnp.float32
    )


def vmem_call(body, outs, operands, scalars=(), scratch=(), name=None, flops=1000000000):
    specs = [
        one[1] if isinstance(one, tuple) else pl.BlockSpec(memory_space=pltpu.VMEM) for one in operands
    ]
    operands = [one[0] if isinstance(one, tuple) else one for one in operands]
    return pl.pallas_call(
        body,
        in_specs=[pl.BlockSpec(memory_space=pltpu.SMEM)] * len(scalars) + specs,
        out_specs=[pl.BlockSpec(memory_space=pltpu.VMEM)] * len(outs),
        out_shape=[jax.ShapeDtypeStruct(shape, dtype) for shape, dtype in outs],
        scratch_shapes=list(scratch),
        compiler_params=pltpu.CompilerParams(vmem_limit_bytes=VMEM),
        cost_estimate=pl.CostEstimate(flops=flops, bytes_accessed=8000000, transcendentals=0),
        name=name,
    )(*scalars, *operands)


def inverse_root(hidden):
    return lax.rsqrt(jnp.mean(hidden * hidden, axis=-1, keepdims=True) + norm_epsilon)


def norm_pull(hidden, gain, cotangent):
    scale = inverse_root(hidden)
    weighted = cotangent * gain
    inner = jnp.mean(hidden * weighted, axis=-1, keepdims=True)
    hidden_grad = scale * weighted - hidden * (scale * scale * scale * inner)
    return hidden_grad, jnp.sum(cotangent * hidden * scale, axis=0, keepdims=True)


def self_pieces(pair, group, wide_ref):
    rows = slice(pair * TGT, (pair + 1) * TGT)
    start = group * 2 * HEAD
    queries = jnp.concatenate(
        [wide_ref[rows, start : start + HEAD], wide_ref[rows, start + HEAD : start + 2 * HEAD]],
        axis=0,
    )
    start = D + group * HEAD
    return (
        queries,
        wide_ref[rows, start : start + HEAD],
        wide_ref[rows, start + KEYS : start + KEYS + HEAD],
    )


def self_scores(queries, keys, bias, length):
    raw = contract(keys, queries, 1, 1) * HEAD ** (-0.5) + bias
    key = lax.broadcasted_iota(jnp.int32, (TGT, 2 * TGT), 0)
    query = lax.broadcasted_iota(jnp.int32, (TGT, 2 * TGT), 1) % TGT
    return jnp.where((key <= query) & (key < length), raw, masked_value)


def self_bias(small_ref, lane_ref, group):
    lanes = lane_ref[...]
    source = jnp.broadcast_to(small_ref[3:4, group * TGT : (group + 1) * TGT], (TGT, TGT))
    return jnp.concatenate(
        [jnp.take_along_axis(source, lanes + head * HEAD, axis=1) for head in range(2)], axis=1
    )


def self_forward_kernel(sizes, share, me_ref, length_ref, row_ref, lane_ref, *refs):
    pieces, refs = refs[:-7], refs[-7:]
    norm_ref, wide_ref, mix_ref, stat_ref, small_ref, weight_ref, sems = refs
    inputs = row_ref[...].astype(f32)
    place_pieces(sizes, share, me_ref, pieces, 0, weight_ref, sems)
    small = weight_ref[:, D + 2 * KEYS :].astype(f32).T
    small_ref[...] = small[:8]
    normed = (inputs * inverse_root(inputs) * small[0:1, :]).astype(bf16)
    norm_ref[...] = normed
    wide_ref[...] = matmul(normed, weight_ref[:, : D + 2 * KEYS]).astype(bf16)
    for group in range(GROUPS):
        bias = self_bias(small_ref, lane_ref, group)
        for pair in range(row_ref.shape[0] // TGT):
            queries, keys, values = self_pieces(pair, group, wide_ref)
            scores = self_scores(queries, keys, bias, length_ref[pair])
            highest = jnp.max(scores, axis=0, keepdims=True)
            weights = jnp.exp(scores - highest)
            totals = jnp.sum(weights, axis=0, keepdims=True)
            probs = (weights * (1.0 / totals)).astype(bf16)
            mixed = contract(probs, values, 0, 0).astype(bf16)
            start = group * 2 * HEAD
            mix_ref[pair * TGT : (pair + 1) * TGT, start : start + 2 * HEAD] = jnp.concatenate(
                [mixed[:TGT], mixed[TGT:]], axis=1
            )
            logsum = highest + jnp.log(totals)
            at = pair * HEADS + 2 * group
            stat_ref[at : at + 1, :] = logsum[:, :TGT]
            stat_ref[at + 1 : at + 2, :] = logsum[:, TGT:]


ANYWHERE = pl.BlockSpec(memory_space=pl.ANY)


def self_forward(sizes, share, me, lengths, rows, lanes, pieces):
    count = rows.shape[0]
    return vmem_call(
        functools.partial(self_forward_kernel, sizes, share),
        [
            ((count, D), bf16),
            ((count, D + 2 * KEYS), bf16),
            ((count, D), bf16),
            ((count // TGT * HEADS, TGT), f32),
            ((8, D), f32),
        ],
        [rows, lanes] + [(piece, ANYWHERE) for piece in pieces],
        [me, lengths],
        [pltpu.VMEM((D, D + 2 * KEYS + SMALL), bf16), pltpu.SemaphoreType.DMA((sizes[0] * sizes[1],))],
        name="self_forward",
    )


def self_output_kernel(sizes, share, me_ref, row_ref, mix_ref, small_ref, *refs):
    pieces, refs = refs[:-6], refs[-6:]
    hidden_ref, norm_ref, query_ref, square_ref, weight_ref, sems = refs
    place_pieces(sizes, share, me_ref, pieces, D + 2 * KEYS + SMALL, weight_ref, sems)
    branch = matmul(mix_ref[...], weight_ref[:, :D])
    square_ref[...] = jnp.sum(branch * branch, axis=1, keepdims=True)
    hidden = row_ref[...].astype(f32) + branch
    hidden_ref[...] = hidden
    normed = (hidden * inverse_root(hidden) * small_ref[1:2, :]).astype(bf16)
    norm_ref[...] = normed
    queries = matmul(normed, weight_ref[:, D:]).astype(bf16) * bf16(HEAD ** (-0.5))
    query_ref[...] = queries.T


def self_output_part(sizes, share, me, rows, mixed, small, pieces):
    count = rows.shape[0]
    return vmem_call(
        functools.partial(self_output_kernel, sizes, share),
        [((count, D), f32), ((count, D), bf16), ((D, count), bf16), ((count, 1), f32)],
        [rows, mixed, small] + [(piece, ANYWHERE) for piece in pieces],
        [me],
        [pltpu.VMEM((D, 2 * D), bf16), pltpu.SemaphoreType.DMA((sizes[0] * sizes[1],))],
        name="self_output",
    )


def cross_join_kernel(
    hidden_ref, gain_ref, weight_ref, *refs
):
    parts, (mix_ref, stat_ref, out_ref, norm_ref, square_ref) = refs[:-5], refs[-5:]
    logs = [join_terms(part[D : D + 3 * HEADS, :]) for part in parts]
    highest = functools.reduce(jnp.maximum, logs)
    weights = [jnp.exp(log - highest) for log in logs]
    totals = functools.reduce(jnp.add, weights)
    stat_ref[...] = highest + jnp.log(totals)
    weights = [weight * (1.0 / totals) for weight in weights]
    for head in range(HEADS):
        at = slice(head * HEAD, (head + 1) * HEAD)
        mix_ref[at, :] = functools.reduce(
            jnp.add,
            [
                part[at, :].astype(f32) * weight[head : head + 1, :]
                for part, weight in zip(parts, weights, strict=True)
            ],
        )
    branch = contract(mix_ref[...].astype(bf16), weight_ref[...], 0, 0)
    square_ref[...] = jnp.sum(branch * branch, axis=1, keepdims=True)
    hidden = hidden_ref[...] + branch
    out_ref[...] = hidden
    norm_ref[...] = (hidden * inverse_root(hidden) * gain_ref[2:3, :]).astype(bf16)


def cross_join(hidden, gains, weights, parts):
    count = hidden.shape[0]
    return vmem_call(
        cross_join_kernel,
        [
            ((D, count), f32),
            ((HEADS, count), f32),
            ((count, D), f32),
            ((count, D), bf16),
            ((count, 1), f32),
        ],
        [hidden, gains, weights, *parts],
        name="cross_join",
    )


def ffn_join_kernel(cotangent_ref, hidden_ref, gain_ref, weight_ref, mix_ref, stat_ref, *refs):
    parts, (grad_ref, low_ref, pack_ref, gain_grad_ref) = refs[:-4], refs[-4:]
    norm_grad = functools.reduce(jnp.add, [part[...].astype(f32) for part in parts])
    back, gain_grad_ref[...] = norm_pull(hidden_ref[...], gain_ref[2:3, :], norm_grad)
    grad = cotangent_ref[...].astype(f32) + back
    grad_ref[...] = grad
    low = grad.astype(bf16)
    low_ref[...] = low
    mixed_grad = contract(weight_ref[...], low, 1, 1).astype(bf16)
    pack_ref[:D, :] = mixed_grad
    product = mixed_grad.astype(f32) * mix_ref[...]
    inner = jnp.concatenate(
        [
            jnp.sum(product[head * HEAD : (head + 1) * HEAD], axis=0, keepdims=True)
            for head in range(HEADS)
        ],
        axis=0,
    )
    for place, term in enumerate(split_terms(stat_ref[...]) + split_terms(inner)):
        pack_ref[D + place * HEADS : D + (place + 1) * HEADS, :] = term


def ffn_join(cotangent, hidden, gains, weights, mixed, stats, parts):
    count = hidden.shape[0]
    return vmem_call(
        ffn_join_kernel,
        [((count, D), f32), ((count, D), bf16), ((D + 6 * HEADS, count), bf16), ((1, D), f32)],
        [cotangent, hidden, gains, weights, mixed, stats, *parts],
        name="ffn_join",
    )


def query_join_kernel(grad_ref, hidden_ref, gain_ref, weight_ref, *refs):
    parts, (sum_ref, out_ref, low_ref, mix_grad_ref, gain_grad_ref) = refs[:-5], refs[-5:]
    queries = functools.reduce(jnp.add, [part[...].astype(f32) for part in parts]).astype(bf16)
    sum_ref[...] = queries
    norm_grad = contract(queries, weight_ref[:, D:], 0, 1)
    back, gain_grad_ref[...] = norm_pull(hidden_ref[...], gain_ref[1:2, :], norm_grad)
    grad = grad_ref[...] + back
    out_ref[...] = grad
    low = grad.astype(bf16)
    low_ref[...] = low
    mix_grad_ref[...] = contract(low, weight_ref[:, :D], 1, 1).astype(bf16)


def query_join(grad, hidden, gains, weights, parts):
    count = hidden.shape[0]
    return vmem_call(
        query_join_kernel,
        [
            ((D, count), bf16),
            ((count, D), f32),
            ((count, D), bf16),
            ((count, D), bf16),
            ((1, D), f32),
        ],
        [grad, hidden, gains, weights, *parts],
        name="query_join",
    )


def self_backward_kernel(
    length_ref,
    mix_grad_ref,
    wide_ref,
    stat_ref,
    small_ref,
    lane_ref,
    bucket_ref,
    wide_grad_ref,
    table_grad_ref,
    score_ref,
):
    pairs = mix_grad_ref.shape[0] // TGT
    for group in range(GROUPS):
        bias = self_bias(small_ref, lane_ref, group)
        score_total = None
        for pair in range(pairs):
            queries, keys, values = self_pieces(pair, group, wide_ref)
            rows = slice(pair * TGT, (pair + 1) * TGT)
            start = group * 2 * HEAD
            mixed_grad = jnp.concatenate(
                [
                    mix_grad_ref[rows, start : start + HEAD],
                    mix_grad_ref[rows, start + HEAD : start + 2 * HEAD],
                ],
                axis=0,
            )
            at = pair * HEADS + 2 * group
            logsum = jnp.concatenate([stat_ref[at : at + 1, :], stat_ref[at + 1 : at + 2, :]], axis=1)
            scores = self_scores(queries, keys, bias, length_ref[pair])
            probs = jnp.exp(scores - logsum)
            prob_grad = contract(values, mixed_grad, 1, 1)
            inner = jnp.sum(probs * prob_grad, axis=0, keepdims=True)
            score_grad = (probs * (prob_grad - inner)).astype(bf16)
            value_grad = matmul(probs.astype(bf16), mixed_grad).astype(bf16)
            key_grad = (matmul(score_grad, queries) * HEAD ** (-0.5)).astype(bf16)
            query_grad = (contract(score_grad, keys, 0, 0) * HEAD ** (-0.5)).astype(bf16)
            wide_grad_ref[rows, start : start + 2 * HEAD] = jnp.concatenate(
                [query_grad[:TGT], query_grad[TGT:]], axis=1
            )
            start = D + group * HEAD
            wide_grad_ref[rows, start : start + HEAD] = key_grad
            wide_grad_ref[rows, start + KEYS : start + KEYS + HEAD] = value_grad
            wide = score_grad.astype(f32)
            score_total = wide if score_total is None else score_total + wide
        score_ref[2 * group] = score_total[:, :TGT]
        score_ref[2 * group + 1] = score_total[:, TGT:]
    buckets = bucket_ref[...]
    lane = lax.broadcasted_iota(jnp.int32, (HEADS, TGT), 1)

    def one_bucket(bucket, table_grad):
        inside = buckets == bucket
        sums = jnp.concatenate(
            [
                jnp.sum(jnp.where(inside, score_ref[head], 0.0), axis=0, keepdims=True)
                for head in range(HEADS)
            ],
            axis=0,
        )
        return jnp.where(lane == bucket, jnp.sum(sums, axis=1, keepdims=True), table_grad)

    table_grad_ref[...] = lax.fori_loop(0, BUCKETS, one_bucket, jnp.zeros((HEADS, TGT), f32))


def self_backward(lengths, mix_grad, wide, stats, small, lanes, buckets):
    return vmem_call(
        self_backward_kernel,
        [(wide.shape, bf16), ((HEADS, TGT), f32)],
        [mix_grad, wide, stats, small, lanes, buckets],
        [lengths],
        [pltpu.VMEM((HEADS, TGT, TGT), f32)],
        name="self_backward",
        flops=8000000000,
    )


def input_grads_kernel(wide_grad_ref, weight_ref, gain_ref, row_ref, grad_ref, out_ref, gain_grad_ref):
    norm_grad = contract(wide_grad_ref[...], weight_ref[...], 1, 1)
    back, gain_grad_ref[...] = norm_pull(row_ref[...].astype(f32), gain_ref[0:1, :], norm_grad)
    out_ref[...] = (grad_ref[...] + back).astype(bf16)


def input_grads(wide_grad, weights, gains, rows, grad):
    return vmem_call(
        input_grads_kernel,
        [(rows.shape, bf16), ((1, D), f32)],
        [wide_grad, weights, gains, rows, grad],
        name="input_grads",
    )


def split_terms(value):
    high = value.astype(bf16)
    rest = value - high.astype(f32)
    middle = rest.astype(bf16)
    low = (rest - middle.astype(f32)).astype(bf16)
    return [high, middle, low]


def join_terms(block):
    return (
        block[:HEADS].astype(f32)
        + block[HEADS : 2 * HEADS].astype(f32)
        + block[2 * HEADS : 3 * HEADS].astype(f32)
    )


def both_heads(ref, group):
    start = group * 2 * HEAD
    return jnp.concatenate(
        [ref[start : start + HEAD, :], ref[start + HEAD : start + 2 * HEAD, :]], axis=1
    )


def both_rows(stat, group):
    return jnp.concatenate([stat[2 * group : 2 * group + 1], stat[2 * group + 1 : 2 * group + 2]], axis=1)


def valid_positions(info_ref, chunk, pair, positions):
    held = positions // 2
    length = info_ref[chunk, 3 + pair]
    place = lax.broadcasted_iota(jnp.int32, (positions, 2 * TGT), 0)
    limit = jnp.where(
        place < held, length - info_ref[chunk, 1], held + length - info_ref[chunk, 2]
    )
    return place < limit


def cross_forward_kernel(chunk, info_ref, query_ref, memory_ref, mix_ref, stat_ref):
    pair = pl.program_id(0)
    mask = valid_positions(info_ref, chunk, pair, memory_ref.shape[1])
    for group in range(GROUPS):
        keys = memory_ref[0, :, group * HEAD : (group + 1) * HEAD]
        values = memory_ref[0, :, KEYS + group * HEAD : KEYS + (group + 1) * HEAD]
        scores = jnp.where(mask, matmul(keys, both_heads(query_ref, group)), masked_value)
        highest = jnp.max(scores, axis=0, keepdims=True)
        weights = jnp.exp(scores - highest)
        totals = jnp.sum(weights, axis=0, keepdims=True)
        mixed = contract(weights.astype(bf16), values, 0, 0).T * (1.0 / totals)
        mixed = mixed.astype(bf16)
        start = group * 2 * HEAD
        mix_ref[start : start + HEAD, :] = mixed[:, :TGT]
        mix_ref[start + HEAD : start + 2 * HEAD, :] = mixed[:, TGT:]
        logsum = highest + jnp.log(totals)
        stat_ref[2 * group : 2 * group + 1, :] = logsum[:, :TGT]
        stat_ref[2 * group + 1 : 2 * group + 2, :] = logsum[:, TGT:]
    for place, term in enumerate(split_terms(stat_ref[...])):
        mix_ref[D + place * HEADS : D + (place + 1) * HEADS, :] = term


def cross_forward(chunk, info, queries, memory_parts):
    positions, wide = memory_parts.shape[1], memory_parts.shape[2]
    rows = queries.shape[1]
    return pl.pallas_call(
        functools.partial(cross_forward_kernel, chunk),
        grid_spec=pltpu.PrefetchScalarGridSpec(
            num_scalar_prefetch=1,
            grid=(rows // TGT,),
            in_specs=[
                pl.BlockSpec((D, TGT), lambda pair, info: (0, pair)),
                pl.BlockSpec((1, positions, wide), lambda pair, info: (info[chunk, 0] + pair, 0, 0)),
            ],
            out_specs=pl.BlockSpec((D + 3 * HEADS, TGT), lambda pair, info: (0, pair)),
            scratch_shapes=[pltpu.VMEM((HEADS, TGT), f32)],
        ),
        out_shape=jax.ShapeDtypeStruct((D + 3 * HEADS, rows), bf16),
        compiler_params=pltpu.CompilerParams(vmem_limit_bytes=VMEM),
        cost_estimate=pl.CostEstimate(flops=6000000000, bytes_accessed=4000000, transcendentals=0),
        name="cross_forward",
    )(info, queries, memory_parts)


def cross_backward_kernel(chunk, info_ref, query_ref, grad_ref, memory_ref, *rest):
    query_grad_ref, memory_grad_ref = rest[-2:]
    pair = pl.program_id(0)
    mask = valid_positions(info_ref, chunk, pair, memory_ref.shape[1])
    logsum = join_terms(grad_ref[D : D + 3 * HEADS, :])
    inner = join_terms(grad_ref[D + 3 * HEADS : D + 6 * HEADS, :])
    for tile in range(GROUPS // 2):
        key_parts, value_parts = [], []
        for group in (2 * tile, 2 * tile + 1):
            keys = memory_ref[0, :, group * HEAD : (group + 1) * HEAD]
            values = memory_ref[0, :, KEYS + group * HEAD : KEYS + (group + 1) * HEAD]
            queries = both_heads(query_ref, group)
            mixed_grad = both_heads(grad_ref, group)
            scores = matmul(keys, queries) - both_rows(logsum, group)
            probs = jnp.exp(jnp.where(mask, scores, masked_value))
            prob_grad = matmul(values, mixed_grad) - both_rows(inner, group)
            score_grad = (probs * prob_grad).astype(bf16)
            value_parts.append(contract(probs.astype(bf16), mixed_grad, 1, 1).astype(bf16))
            key_parts.append(contract(score_grad, queries, 1, 1).astype(bf16))
            query_grad = (contract(keys, score_grad, 0, 0) * HEAD ** (-0.5)).astype(bf16)
            start = group * 2 * HEAD
            query_grad_ref[start : start + HEAD, :] = query_grad[:, :TGT]
            query_grad_ref[start + HEAD : start + 2 * HEAD, :] = query_grad[:, TGT:]
        columns = 2 * HEAD * tile
        memory_grad_ref[0, :, columns : columns + 2 * HEAD] = jnp.concatenate(key_parts, axis=1)
        memory_grad_ref[0, :, KEYS + columns : KEYS + columns + 2 * HEAD] = jnp.concatenate(
            value_parts, axis=1
        )


def cross_backward(chunk, info, queries, grads, memory_parts, *earlier):
    positions, wide = memory_parts.shape[1], memory_parts.shape[2]
    rows = queries.shape[1]
    place = pl.BlockSpec((1, positions, wide), lambda pair, info: (info[chunk, 0] + pair, 0, 0))
    return pl.pallas_call(
        functools.partial(cross_backward_kernel, chunk),
        grid_spec=pltpu.PrefetchScalarGridSpec(
            num_scalar_prefetch=1,
            grid=(rows // TGT,),
            in_specs=[
                pl.BlockSpec((D, TGT), lambda pair, info: (0, pair)),
                pl.BlockSpec((D + 6 * HEADS, TGT), lambda pair, info: (0, pair)),
                place,
            ]
            + [pl.BlockSpec(memory_space=pl.ANY)] * len(earlier),
            out_specs=[pl.BlockSpec((D, TGT), lambda pair, info: (0, pair)), place],
        ),
        out_shape=[
            jax.ShapeDtypeStruct((D, rows), bf16),
            jax.ShapeDtypeStruct(memory_parts.shape, bf16),
        ],
        input_output_aliases={4: 1} if earlier else {},
        compiler_params=pltpu.CompilerParams(vmem_limit_bytes=VMEM),
        cost_estimate=pl.CostEstimate(flops=10000000000, bytes_accessed=8000000, transcendentals=0),
        name="cross_backward",
    )(info, queries, grads, memory_parts, *earlier)


def ffn_kernel(me_ref, row_ref, cotangent_ref, gate_ref, up_ref, down_ref, *rest):
    row_grad_ref, branch_ref, rows_ref, kept_cotangent_ref, hidden_ref, gate_grad_ref, up_grad_ref = rest[
        -7:
    ]
    rows = row_ref[...]
    rows_ref[0] = rows
    gate = matmul(rows, gate_ref[...])
    up = matmul(rows, up_ref[...])
    cotangent = cotangent_ref[0]
    kept_cotangent_ref[0] = cotangent
    hidden_grad = contract(cotangent, down_ref[...], 1, 1)
    square = gate * gate
    slope = 0.7978845608028654
    bend = jnp.tanh(slope * gate * (1.0 + 0.044715 * square))
    half = 0.5 * (1.0 + bend)
    value = gate * half
    derivative = half + 0.5 * gate * (1.0 - bend * bend) * slope * (1.0 + 3 * 0.044715 * square)
    hidden = (value * up).astype(bf16)
    gate_grad = (hidden_grad * up * derivative).astype(bf16)
    up_grad = (hidden_grad * value).astype(bf16)
    row_grad = contract(gate_grad, gate_ref[...], 1, 1) + contract(up_grad, up_ref[...], 1, 1)
    row_grad_ref[...] = row_grad.astype(bf16)
    branch_ref[0] = matmul(hidden, down_ref[...]).astype(bf16)
    hidden_ref[0] = hidden
    gate_grad_ref[0] = gate_grad
    up_grad_ref[0] = up_grad


def ffn_chunk(chunk, chunks, me, rows, cotangent, gate, up, down, *earlier):
    count, width = rows.shape
    wide = gate.shape[1]
    kept = [width, width, width, wide, wide, wide]
    by_line = pl.BlockSpec((1, count, width), lambda step, me: (me[1] ^ chunk, 0, 0))

    def whole(array):
        return pl.BlockSpec(array.shape, lambda step, me: (0, 0))

    return pl.pallas_call(
        ffn_kernel,
        grid_spec=pltpu.PrefetchScalarGridSpec(
            num_scalar_prefetch=1,
            grid=(1,),
            in_specs=[whole(rows), by_line]
            + [whole(array) for array in (gate, up, down)]
            + [ANYWHERE] * len(earlier),
            out_specs=[whole(rows), by_line]
            + [pl.BlockSpec((1, count, size), lambda step, me: (chunk, 0, 0)) for size in kept[1:]],
        ),
        out_shape=[jax.ShapeDtypeStruct((count, width), bf16)]
        + [jax.ShapeDtypeStruct((chunks, count, size), bf16) for size in kept],
        input_output_aliases={6 + place: 1 + place for place in range(len(earlier))},
        compiler_params=pltpu.CompilerParams(vmem_limit_bytes=VMEM),
        cost_estimate=pl.CostEstimate(flops=3000000000, bytes_accessed=8000000, transcendentals=0),
        name="ffn_chunk",
    )(me, rows, cotangent, gate, up, down, *earlier)


def exchange(value, axis, size, mask):
    return lax.ppermute(value, axis, [(place, place ^ mask) for place in range(size)])


def visit_chunks(value, size, work, settle=False):
    lines = size // 2

    def by_lines(array, pairs):
        pairs = [(2 * old + core, 2 * new + core) for old, new in pairs for core in range(2)]
        return lax.ppermute(array, "ffn", pairs)

    if lines != 4:
        chunks = [value] + [exchange(value, "ffn", size, 2 * step) for step in range(1, lines)]
        return [work(chunk, one) for chunk, one in enumerate(chunks)]
    across = exchange(value, "ffn", size, 4)
    beside = exchange(value, "ffn", size, 2)
    results = [work(0, value)]
    across = after(across, results[0])
    middle = by_lines(after(value, across), [(1, 2), (2, 1)])
    onward = by_lines(across, [(2, 3), (1, 0)])
    results.append(work(1, after(beside, across)))
    line = lax.axis_index("ffn") // 2
    last = [middle, onward]
    if settle:
        last = after(last, results[1])
        across = after(across, last)
    results.append(work(2, across))
    results.append(work(3, jnp.where((line == 0) | (line == 3), last[1], last[0])))
    return results


def return_chunks(parts, size):
    return [parts[0]] + [
        exchange(parts[step], "ffn", size, 2 * step) for step in range(1, size // 2)
    ]


def reduce_rows(grads, tok_size, ffn_size):
    columns = grads.shape[1]
    me_ffn, me_tok = lax.axis_index("ffn"), lax.axis_index("tok")

    def halves(value, dim, bit):
        first = lax.index_in_dim(value, 0, dim, keepdims=False)
        second = lax.index_in_dim(value, 1, dim, keepdims=False)
        return jnp.where(bit == 0, first, second), jnp.where(bit == 0, second, first)

    rows = grads.shape[0] // (tok_size * ffn_size)
    value = grads.reshape(tok_size, ffn_size // 2, 2, rows, columns)
    kept, sent = halves(value, 2, me_ffn & 1)
    value = kept.astype(f32) + exchange(sent.astype(bf16), "ffn", ffn_size, 1).astype(f32)

    bits = tok_size.bit_length() - 1
    value = value.reshape((2,) * bits + (ffn_size // 2, rows, columns))
    half = columns // 2 // 128 * 128
    sides = []
    for part, order in (
        (value[..., :half], list(range(bits))),
        (value[..., half:], list(range(bits))[::-1]),
    ):
        left = list(range(bits))
        for bit in order:
            dim = left.index(bit)
            left.remove(bit)
            weight = 1 << (bits - 1 - bit)
            kept, sent = halves(part, dim, (me_tok // weight) & 1)
            part = kept.astype(f32) + exchange(sent.astype(bf16), "tok", tok_size, weight).astype(f32)
        sides.append(part)
    value = jnp.concatenate(sides, axis=-1)
    line = me_ffn // 2
    total = lax.dynamic_index_in_dim(value, line, 0, keepdims=False)
    low = value.astype(bf16)
    for step in range(1, ffn_size // 2):
        part = lax.dynamic_index_in_dim(low, line ^ step, 0, keepdims=False)
        total = total + exchange(part, "ffn", ffn_size, 2 * step).astype(f32)
    return total


def memory_forward_kernel(me_ref, own_ref, other_ref, weight_ref, out_ref):
    pairs, held, width = other_ref.shape[2:]
    for place, rows in enumerate((own_ref[0, 0], other_ref[0, 0])):
        part = matmul(rows.reshape(pairs * held, width), weight_ref[...]).astype(bf16)
        out_ref[:, place] = part.reshape(pairs, held, part.shape[1])


def own_pairs(memory):
    unused, also, step, held, width = memory.shape
    return pl.BlockSpec((1, 1, step, held, width), lambda line, me: (line, me[2], 0, 0, 0))


def memory_forward(me, memory, other, weights):
    lines, unused, step, held, width = memory.shape
    return pl.pallas_call(
        memory_forward_kernel,
        grid_spec=pltpu.PrefetchScalarGridSpec(
            num_scalar_prefetch=1,
            grid=(lines,),
            in_specs=[
                own_pairs(memory),
                own_pairs(memory),
                pl.BlockSpec((width, 2 * KEYS), lambda line, me: (0, 0)),
            ],
            out_specs=pl.BlockSpec((step, 2, held, 2 * KEYS), lambda line, me: (line, 0, 0, 0)),
        ),
        out_shape=jax.ShapeDtypeStruct((lines * step, 2, held, 2 * KEYS), bf16),
        compiler_params=pltpu.CompilerParams(vmem_limit_bytes=VMEM),
        cost_estimate=pl.CostEstimate(flops=8600000000, bytes_accessed=18000000, transcendentals=0),
        name="memory_forward",
    )(me, memory, other, weights)


def memory_backward_kernel(
    sizes, me_ref, own_ref, other_ref, grad_ref, weight_ref, mix_ref, low_ref, *rest
):
    own_grad_ref, other_grad_ref, kept_ref, sent_ref, total = rest
    step = pl.program_id(0)
    pairs, held, width = other_ref.shape[2:]
    for place, (rows, out_ref) in enumerate(
        ((own_ref[0, 0], own_grad_ref), (other_ref[0, 0], other_grad_ref))
    ):
        grads = grad_ref[:, place].reshape(pairs * held, grad_ref.shape[3])
        out = contract(grads, weight_ref[...], 1, 1).astype(bf16)
        out_ref[...] = out.reshape(out_ref.shape)
        part = contract(rows.reshape(pairs * held, width), grads, 0, 0)
        if place == 0:
            total[...] = jnp.where(step == 0, part, total[...] + part)
        else:
            total[...] += part

    @pl.when(step == 0)
    def first():
        low = low_ref[...]
        for start in range(0, low.shape[1], 512):
            part = matmul(mix_ref[...].astype(bf16), low[:, start : start + 512])
            store_blocks(sizes, me_ref, kept_ref, sent_ref, 2 * KEYS + start, part)

    @pl.when(step == pl.num_programs(0) - 1)
    def last():
        store_blocks(sizes, me_ref, kept_ref, sent_ref, 0, total[...])


def memory_backward(sizes, me, memory, other, grads, weights, mixed, low):
    lines, unused, step, held, width = memory.shape
    block = pl.BlockSpec((step, held, width), lambda line, me: (line, 0, 0))
    shape = blocks_shape(sizes, 2 * KEYS + low.shape[1])
    return pl.pallas_call(
        functools.partial(memory_backward_kernel, sizes),
        grid_spec=pltpu.PrefetchScalarGridSpec(
            num_scalar_prefetch=1,
            grid=(lines,),
            in_specs=[
                own_pairs(memory),
                own_pairs(memory),
                pl.BlockSpec((step, 2, held, 2 * KEYS), lambda line, me: (line, 0, 0, 0)),
                pl.BlockSpec((width, 2 * KEYS), lambda line, me: (0, 0)),
                pl.BlockSpec(mixed.shape, lambda line, me: (0, 0)),
                pl.BlockSpec(low.shape, lambda line, me: (0, 0)),
            ],
            out_specs=[
                own_pairs(memory),
                block,
            ]
            + [pl.BlockSpec(shape, lambda line, me: (0,) * len(shape))] * 2,
            scratch_shapes=[pltpu.VMEM((width, 2 * KEYS), f32)],
        ),
        out_shape=[
            jax.ShapeDtypeStruct(memory.shape, bf16),
            jax.ShapeDtypeStruct((lines * step, held, width), bf16),
            jax.ShapeDtypeStruct(shape, bf16),
            jax.ShapeDtypeStruct(shape, bf16),
        ],
        compiler_params=pltpu.CompilerParams(vmem_limit_bytes=VMEM),
        cost_estimate=pl.CostEstimate(flops=17200000000, bytes_accessed=28000000, transcendentals=0),
        name="memory_backward",
    )(me, memory, other, grads, weights, mixed, low)


def place_pairs_kernel(me_ref, pair_ref, unused_ref, out_ref):
    out_ref[0, 0] = pair_ref[...]


def place_pairs(me, whole, pairs):
    lines, unused, step, held, width = whole.shape
    return pl.pallas_call(
        place_pairs_kernel,
        grid_spec=pltpu.PrefetchScalarGridSpec(
            num_scalar_prefetch=1,
            grid=(lines,),
            in_specs=[
                pl.BlockSpec((step, held, width), lambda line, me: (line, 0, 0)),
                pl.BlockSpec(memory_space=pl.ANY),
            ],
            out_specs=pl.BlockSpec(
                (1, 1, step, held, width), lambda line, me: (line, 1 - me[2], 0, 0, 0)
            ),
        ),
        out_shape=jax.ShapeDtypeStruct(whole.shape, bf16),
        input_output_aliases={2: 0},
        compiler_params=pltpu.CompilerParams(vmem_limit_bytes=VMEM),
        name="place_pairs",
    )(me, pairs, whole)


def blocks_shape(sizes, columns):
    tok_size, ffn_size = sizes
    return (tok_size * ffn_size // 2, D // (tok_size * ffn_size), columns)


def store_blocks(sizes, me_ref, kept_ref, sent_ref, column, value):
    tok_size, ffn_size = sizes
    rows = D // (tok_size * ffn_size)
    low = value.astype(bf16)
    columns = slice(column, column + value.shape[1])
    for block in range(0, tok_size * ffn_size, 2):
        tok, line = block // ffn_size, block % ffn_size // 2
        place = (tok ^ me_ref[0]) * (ffn_size // 2) + (line ^ me_ref[1])
        first = low[block * rows : (block + 1) * rows]
        second = low[(block + 1) * rows : (block + 2) * rows]
        kept_ref[place, :, columns] = jnp.where(me_ref[2] == 0, first, second)
        sent_ref[place, :, columns] = jnp.where(me_ref[2] == 0, second, first)


def grad_blocks_kernel(sizes, dims, me_ref, *refs):
    kept_ref, sent_ref = refs[-2:]
    column = 0
    for place, (left_dim, right_dim) in enumerate(dims):
        left, right = refs[2 * place], refs[2 * place + 1]
        for start in range(0, right.shape[1 - right_dim], 512):
            if right_dim == 0:
                part = right[:, start : start + 512]
            else:
                part = right[start : start + 512, :]
            product = contract(left[...], part, left_dim, right_dim)
            store_blocks(sizes, me_ref, kept_ref, sent_ref, column, product)
            column += 512
    extra = refs[2 * len(dims) : -2]
    if len(extra) == 2:
        kept_ref[:, :, column:] = extra[0][...]
        sent_ref[:, :, column:] = extra[1][...]
    elif extra:
        rows = extra[0][...]
        filled = jnp.concatenate([rows, jnp.zeros((SMALL - rows.shape[0], D), f32)], axis=0)
        store_blocks(sizes, me_ref, kept_ref, sent_ref, column, filled.T)


def grad_blocks(sizes, me, products, *extra):
    operands = [array for left, right, unused, also in products for array in (left, right)]
    columns = sum(right.shape[1 - dim] for unused, right, also, dim in products)
    operands += extra
    if extra:
        columns += extra[0].shape[2] if extra[0].ndim == 3 else SMALL
    return pl.pallas_call(
        functools.partial(grad_blocks_kernel, sizes, [(one[2], one[3]) for one in products]),
        in_specs=[pl.BlockSpec(memory_space=pltpu.SMEM)]
        + [pl.BlockSpec(memory_space=pltpu.VMEM)] * len(operands),
        out_specs=[pl.BlockSpec(memory_space=pltpu.VMEM)] * 2,
        out_shape=[jax.ShapeDtypeStruct(blocks_shape(sizes, columns), bf16)] * 2,
        compiler_params=pltpu.CompilerParams(vmem_limit_bytes=VMEM),
        name="grad_blocks",
    )(me, *operands)


def plus(*parts):
    return functools.reduce(jnp.add, [part.astype(f32) for part in parts]).astype(bf16)


def reduce_core(sizes, blocks, earlier=()):
    lines = sizes[1] // 2
    kept, sent = blocks
    other = after(exchange(sent, "ffn", sizes[1], 1), earlier)
    return [
        plus(kept[tok * lines : (tok + 1) * lines], other[tok * lines : (tok + 1) * lines])
        for tok in range(4)
    ]


def reduce_corner(sizes, parts, earlier=()):
    own, by_x, by_y, across = parts
    half = sizes[1] // 4
    top = exchange(across[:half], "tok", sizes[0], 1)
    bottom = exchange(across[half:], "tok", sizes[0], 2)
    top, bottom = after([top, bottom], earlier)
    by_x = jnp.concatenate([by_x[:half], plus(by_x[half:], bottom)], axis=0)
    by_y = jnp.concatenate([plus(by_y[:half], top), by_y[half:]], axis=0)
    return [own, by_x, by_y]


def reduce_sides(sizes, parts, earlier=()):
    own, by_x, by_y = parts
    arrived = [exchange(by_x, "tok", sizes[0], 1), exchange(by_y, "tok", sizes[0], 2)]
    return plus(own, *after(arrived, earlier))


def reduce_line(sizes, total, earlier=()):
    parts = [total[0]] + [
        exchange(total[step], "ffn", sizes[1], 2 * step) for step in range(1, sizes[1] // 2)
    ]
    parts = after(parts, earlier)
    return functools.reduce(jnp.add, [part.astype(f32) for part in parts])


def place_pieces(sizes, share, me_ref, pieces, column, target_ref, sems):
    columns = pl.ds(column, target_ref.shape[1])
    copies = []
    if len(pieces) == 1:
        copies.append(pltpu.make_async_copy(pieces[0].at[:, columns], target_ref, sems.at[0]))
    else:
        lines = sizes[1] // 2
        half = lines // 2
        for core in range(2):
            line_ref, x_ref, y_ref, top_ref, bottom_ref = pieces[5 * core : 5 * core + 5]
            for tok in range(4):
                for line in range(lines):
                    if tok < 3:
                        source = (line_ref, x_ref, y_ref)[tok].at[line]
                    else:
                        source = top_ref.at[line] if line < half else bottom_ref.at[line - half]
                    block = ((tok ^ me_ref[0]) * lines + (line ^ me_ref[1])) * 2 + (core ^ me_ref[2])
                    target = target_ref.at[pl.ds(pl.multiple_of(block * share, share), share), :]
                    copies.append(
                        pltpu.make_async_copy(source.at[:, columns], target, sems.at[len(copies)])
                    )
    for copy in copies:
        copy.start()
    for copy in copies:
        copy.wait()


def place_rows_kernel(sizes, share, starts, me_ref, *refs):
    pieces, outs, sems = refs[: -len(starts) - 1], refs[-len(starts) - 1 : -1], refs[-1]
    for column, out_ref in zip(starts, outs, strict=True):
        place_pieces(sizes, share, me_ref, pieces, column, out_ref, sems)


def place_rows(sizes, share, me, pieces, starts, columns):
    return vmem_call(
        functools.partial(place_rows_kernel, sizes, share, starts),
        [((sizes[0] * sizes[1] * share, columns), bf16) for unused in starts],
        [(piece, ANYWHERE) for piece in pieces],
        [me],
        [pltpu.SemaphoreType.DMA((sizes[0] * sizes[1],))],
        name="place_rows",
    )


def after(values, earlier):
    return lax.optimization_barrier((values, earlier))[0]


def gather_pieces(sizes, pack):
    tok_size, ffn_size = sizes
    lines = ffn_size // 2
    half = lines // 2
    line = [pack] + [exchange(pack, "ffn", ffn_size, 2 * step) for step in range(1, lines)]
    begun = line
    line = jnp.stack(line)
    by_x = exchange(line, "tok", tok_size, 1)
    by_y = exchange(line, "tok", tok_size, 2)
    top = exchange(by_y[:half], "tok", tok_size, 1)
    bottom = exchange(by_x[half:], "tok", tok_size, 2)
    held = [line, by_x, by_y, top, bottom]
    return held + [exchange(one, "ffn", ffn_size, 1) for one in held], begun


def on_device(
    tok_size,
    ffn_size,
    targets,
    memory,
    out_grad,
    target_lengths,
    memory_lengths,
    buckets,
    rel_table,
    gain_self,
    gain_cross,
    gain_ffn,
    self_query,
    self_key,
    self_value,
    self_output,
    cross_query,
    cross_key,
    cross_value,
    cross_output,
    ffn_gate,
    ffn_up,
    ffn_down,
):
    pair_count = target_lengths.shape[0]
    row_count = targets.shape[0]
    held = memory.shape[1]
    devices = tok_size * ffn_size
    me_tok, me_ffn = lax.axis_index("tok"), lax.axis_index("ffn")
    share = self_query.shape[0]
    table_share = rel_table.shape[0]

    sizes = (tok_size, ffn_size)
    direct = tok_size == 4 and share % 16 == 0
    me = jnp.stack([me_tok, me_ffn // 2, me_ffn % 2]).astype(jnp.int32)
    per_row = [
        jnp.pad(part.astype(bf16), (0, share - part.shape[0]))
        for part in (gain_self, gain_cross, gain_ffn, rel_table, memory_lengths // 64, memory_lengths % 64)
    ]
    small = jnp.pad(jnp.stack(per_row, axis=1), ((0, 0), (0, SMALL - len(per_row))))

    core = me_ffn % 2
    lines = ffn_size // 2
    both = ("tok", "ffn")
    pack = jnp.concatenate(
        [self_query, self_key, self_value, small, self_output, cross_query, cross_key, cross_value],
        axis=1,
    )
    same_core = [[2 * line + one for line in range(lines)] for one in range(2)]
    memory_lines = memory.reshape(lines, 2, pair_count, held, D)

    memory_other = exchange(memory_lines, "ffn", ffn_size, 1)

    if direct:
        pieces, begun = gather_pieces(sizes, pack)
    else:
        pieces = [lax.all_gather(pack, both, axis=0, tiled=True)]
        begun = pieces
    cotangents = lax.all_gather(
        after(out_grad, begun),
        "ffn",
        axis=0,
        tiled=False,
        axis_index_groups=same_core,
    )

    per_table = BUCKETS * HEADS // devices
    buckets = buckets.T
    lanes_of = buckets // per_table * (2 * per_table) + buckets % per_table
    normed_one, self_wide, self_mixed, self_stats, small_rows = self_forward(
        sizes, share, me, target_lengths, targets, lanes_of, pieces
    )
    hidden_one, normed_two, cross_queries, self_squares = self_output_part(
        sizes, share, me, targets, self_mixed, small_rows, pieces
    )
    gains = small_rows[:3]
    lengths = (small_rows[4] * 64 + small_rows[5]).astype(jnp.int32)
    lengths = lengths.reshape(devices, share)[:, :pair_count]
    (memory_weights,) = place_rows(
        sizes, share, me, after(pieces, cross_queries), (3 * D + 2 * KEYS + SMALL,), 2 * KEYS
    )
    memory_parts = memory_forward(me, memory_lines, memory_other, memory_weights)
    memory_parts = memory_parts.reshape(-1, 2 * held, 2 * KEYS)
    lengths = lax.dynamic_index_in_dim(
        lengths.reshape(tok_size, ffn_size, pair_count), me_tok, 0, keepdims=False
    )
    owner = me_ffn ^ (2 * jnp.arange(lines))
    info = jnp.concatenate(
        [
            (owner // 2 * pair_count)[:, None],
            jnp.broadcast_to(me_ffn * held, (lines, 1)),
            jnp.broadcast_to((me_ffn ^ 1) * held, (lines, 1)),
            jnp.take(lengths, owner, axis=0),
        ],
        axis=1,
    ).astype(jnp.int32)


    position = jnp.arange(TGT)

    query_chunks, mixed_parts, kept = [], [], {}
    kept["output"] = lax.all_gather(
        after(cross_output, (self_mixed, cotangents)), both, axis=0, tiled=True
    )

    def visit_forward(chunk, chunk_queries):
        query_chunks.append(chunk_queries)
        if chunk:
            chunk_queries = after(chunk_queries, mixed_parts[-1])
        mixed_parts.append(cross_forward(chunk, info, chunk_queries, memory_parts))
        return mixed_parts[-1]

    visit_chunks(cross_queries, ffn_size, visit_forward)
    output_weights = kept["output"]
    held_pieces, units = after((pieces, (ffn_gate, ffn_up, ffn_down)), mixed_parts[-1])
    placed = place_rows(sizes, share, me, held_pieces, (0, D + 2 * KEYS + SMALL), 2 * D)
    units = [
        jnp.concatenate([array, exchange(array, "ffn", ffn_size, 1)], axis=dim)
        for array, dim in zip(units, (1, 1, 0), strict=True)
    ]
    full_first, full_second = placed
    both_gate, both_up, both_down = units
    mixed_parts = return_chunks(mixed_parts, ffn_size)
    mixed_parts = mixed_parts[:1] + after(mixed_parts[1:], (placed, units))
    cross_mixed, cross_stats, hidden_two, normed_three, cross_squares = cross_join(
        hidden_one, gains, output_weights, mixed_parts
    )

    earlier, row_parts = [], []

    def visit_ffn(chunk, rows):
        row_part, *earlier[:] = ffn_chunk(
            chunk, lines, me, rows, cotangents, both_gate, both_up, both_down, *earlier
        )
        row_parts.append(row_part)
        return row_part

    visit_chunks(normed_three, ffn_size, visit_ffn)
    row_parts = return_chunks(row_parts, ffn_size)
    branch_part, all_rows, all_cotangent, hidden, gate_grad, up_grad = [
        array.reshape(lines * row_count, array.shape[2]) for array in after(earlier, row_parts[1])
    ]
    units = ffn_gate.shape[1]
    weight_grads = []
    for part, dim in (
        (contract(all_rows, gate_grad, 0, 0), 1),
        (contract(all_rows, up_grad, 0, 0), 1),
        (contract(hidden, all_cotangent, 0, 0), 0),
    ):
        kept = lax.slice_in_dim(part, 0, units, axis=dim)
        sent = lax.slice_in_dim(part, units, 2 * units, axis=dim).astype(bf16)
        weight_grads.append((kept + exchange(sent, "ffn", ffn_size, 1).astype(f32)).astype(bf16))
    weight_sums = [lax.psum(part, "tok") for part in weight_grads]
    gate_weight_grad, up_weight_grad, down_weight_grad = [part.astype(f32) for part in weight_sums]

    row_parts = row_parts[:2] + after(row_parts[2:], weight_grads)
    hidden_two_grad, cross_low, grad_pack, gain_ffn_grad = ffn_join(
        out_grad, hidden_two, gains, output_weights, cross_mixed, cross_stats, row_parts
    )
    earlier, query_parts = [], []

    def visit_backward(chunk, grads):
        part, *earlier[:] = cross_backward(
            chunk, info, query_chunks[chunk], grads, memory_parts, *earlier
        )
        query_parts.append(part)
        return part

    visit_chunks(grad_pack, ffn_size, visit_backward, settle=True)
    memory_grads = earlier[0]
    query_parts = return_chunks(query_parts, ffn_size)
    memory_grad, other_grad, *memory_sum = memory_backward(
        sizes,
        me,
        memory_lines,
        memory_other,
        after(memory_grads, query_parts[1]).reshape(-1, 2, held, 2 * KEYS),
        memory_weights,
        cross_mixed,
        cross_low,
    )
    query_parts = query_parts[:2] + after(query_parts[2:], (memory_sum, weight_sums))
    query_grads, hidden_one_grad, self_low, mix_grad, gain_cross_grad = query_join(
        hidden_two_grad, hidden_one, gains, full_second, query_parts
    )
    other_grad = exchange(other_grad, "ffn", ffn_size, 1)
    memory_grad = place_pairs(me, memory_grad, other_grad).reshape(memory.shape)
    products = [(normed_two, query_grads, 0, 1), (self_mixed, self_low, 0, 0)]
    outer = middle = memory_sum
    if direct:
        middle = grad_blocks(sizes, me, products)
        outer = reduce_core(sizes, after(memory_sum, query_grads), middle)
        mix_grad = after(mix_grad, middle)
    wide_grad, table_grad = self_backward(
        target_lengths, mix_grad, self_wide, self_stats, small_rows, lanes_of, buckets
    )
    if direct:
        outer = reduce_corner(sizes, outer, wide_grad)
        middle = reduce_core(sizes, middle, wide_grad)
        wide_grad = after(wide_grad, (outer, middle))
    targets_grad, gain_self_grad = input_grads(wide_grad, full_first, gains, targets, hidden_one_grad)

    branch_sum = lax.psum_scatter(
        after(branch_part, query_grads),
        "ffn",
        scatter_dimension=0,
        tiled=True,
        axis_index_groups=same_core,
    )
    table_grad = jnp.pad(
        table_grad[:, :BUCKETS].reshape(devices, table_share), ((0, 0), (0, share - table_share))
    )
    small_grads = jnp.concatenate(
        [gain_self_grad, gain_cross_grad, gain_ffn_grad, table_grad.reshape(1, D), jnp.zeros((4, D), f32)]
    )
    last_product = (normed_one, wide_grad, 0, 0)
    if direct:
        first = grad_blocks(sizes, me, [last_product], small_grads)
        outer = reduce_sides(sizes, outer, first)
        middle = reduce_corner(sizes, middle, first)
        first = reduce_core(sizes, first, memory_grad)
        outer_sum = reduce_line(sizes, outer, first)
        middle = reduce_sides(sizes, middle, first)
        first = reduce_corner(sizes, first, middle)
        first = reduce_sides(sizes, first)
        middle_sum = reduce_line(sizes, middle, first)
        first_sum = reduce_line(sizes, first)
        branch_sum = after(branch_sum, first)
    else:
        order = [(block // ffn_size, block % ffn_size // 2, block % 2) for block in range(devices)]
        memory_rows = jnp.concatenate(
            [
                jnp.stack(memory_sum)[core ^ me[2], (tok ^ me[0]) * lines + (line ^ me[1])]
                for tok, line, core in order
            ]
        )
        outer_sum, middle_sum, first_sum = [
            reduce_rows(jnp.concatenate(parts, axis=1), tok_size, ffn_size)
            for parts in (
                [memory_rows],
                [contract(*one) for one in products],
                [contract(*last_product), jnp.pad(small_grads.T, ((0, 0), (0, SMALL - 8)))],
            )
        ]
    ffn_branch = branch_sum.astype(f32)
    hidden_three = hidden_two + ffn_branch
    layer_out = hidden_three.astype(jnp.bfloat16)
    valid = position[None, :] < target_lengths[:, None]
    counted = target_lengths.astype(jnp.float32) * D
    squares = [
        jnp.sum(hidden_three * hidden_three, axis=1),
        self_squares[:, 0],
        cross_squares[:, 0],
        jnp.sum(ffn_branch * ffn_branch, axis=1),
    ]
    squares = jnp.stack([part.reshape(pair_count, TGT) for part in squares], axis=1)
    squares = jnp.sum(jnp.where(valid[:, None, :], squares, 0.0), axis=2)
    rms_values = jnp.sqrt(squares / counted[:, None])

    small_sum = first_sum[:, D + 2 * KEYS :]
    return (
        layer_out,
        targets_grad,
        memory_grad,
        rms_values,
        small_sum[:table_share, 3],
        small_sum[:, 0],
        small_sum[:, 1],
        small_sum[:, 2],
        first_sum[:, :D],
        first_sum[:, D : D + KEYS],
        first_sum[:, D + KEYS : D + 2 * KEYS],
        middle_sum[:, D : 2 * D],
        middle_sum[:, :D],
        outer_sum[:, :KEYS],
        outer_sum[:, KEYS : 2 * KEYS],
        outer_sum[:, 2 * KEYS :],
        gate_weight_grad,
        up_weight_grad,
        down_weight_grad,
    )


def solution(mesh):
    rows = P(("tok", "ffn"), None)
    flat = P(("tok", "ffn"))
    memory = P("tok", "ffn", None)
    columns, inner = P(None, "ffn"), P("ffn", None)
    in_specs = (
        (rows, memory, rows, flat, flat, P()) + (flat,) * 4 + (rows,) * 8 + (columns, columns, inner)
    )
    out_specs = (
        (rows, rows, memory, rows) + (flat,) * 4 + (rows,) * 8 + (columns, columns, inner)
    )
    return jax.shard_map(
        functools.partial(on_device, mesh.shape["tok"], mesh.shape["ffn"]),
        mesh=mesh,
        in_specs=in_specs,
        out_specs=out_specs,
        check_vma=False,
    )
```
